512 devices in a mesh: particle: 16 (over x, z_lo, core), rows: 32 (over z_hi, y).
Axes of the slice: x: 4, y: 8, z: 8 (z_hi: 4, z_lo: 2; z = z_hi * 2 + z_lo), core: 2. Of those that a mesh axis runs over, the one named last changes fastest.
Arguments:
- latent: bfloat16 [16, 128, 24, 640], P('particle', 'rows'), may hold values from -20 to 20
- ada_scale: float32 [640], replicated, may hold values from -0.5 to 0.5
- ada_shift: float32 [640], replicated, may hold values from -3 to 3
- conv_weight: bfloat16 [5760, 640], P('rows'), may hold values from -0.078125 to 0.078125
- qkv_weight: bfloat16 [640, 1920], replicated, may hold values from -1.4230249 to 1.4230249
- out_weight: bfloat16 [640, 640], replicated, may hold values from -0.25 to 0.25
- ancestors: int32 [16], replicated, may hold values from 0 to 15
Outputs:
- resampled: bfloat16 [16, 128, 24, 640], P('particle', 'rows')
The draws below stay inside these ranges and needn't reach their ends.
All inputs are finite; a program needn't handle non-finite values.
Results may differ from the reference program's by a relative error of at most 0.0081.
Values may be sent and summed in bfloat16 or wider, within the bound.
No kernel may reach another device: no remote copies, remote signals or barrier semaphores. Data moves between devices by JAX's collectives and lax.ppermute only.
A program may use at most 64 MiB of HBM per device.

```python
import math
import jax
import jax.numpy as jnp
from jax import lax

C = 640
HEADS = 10
GROUPS = 32
W = 24
H = 128
PARTICLES = 16


def draw_latent(key, part):
    key_z, key_c = jax.random.split(key, 2)
    row_scale = 0.5 * 3.0 ** (jnp.arange(H, dtype=jnp.float32) / max(H - 1, 1))
    chan_scale = jnp.exp(jax.random.uniform(key_c, (C,), jnp.float32, math.log(0.3), math.log(3.0)))
    base = jnp.clip(jax.random.normal(key_z, (PARTICLES, H, W, C), jnp.float32), -4.0, 4.0)
    return (base * row_scale[None, :, None, None] * chan_scale).astype(jnp.bfloat16)


def draw_qkv_weight(key, part):
    base = jnp.clip(jax.random.normal(key, (C, 3 * C), jnp.float32), -6.0, 6.0) / math.sqrt(C)
    return base.astype(jnp.bfloat16)


def place_ends(result, own_key, smallest, largest):
    longest = result.shape.index(max(result.shape))
    spots = []
    for shift in (0, 1):
        where = [jax.random.randint(jax.random.fold_in(own_key, axis), (), 0, length) for axis, length in enumerate(result.shape)]
        where[longest] = (where[longest] + shift) % result.shape[longest]
        spots.append(tuple(where))
    return result.at[spots[0]].set(smallest).at[spots[1]].set(largest)


def steps_of(key, extent, cuts, low, largest):
    level, own = 1.0, jax.random.fold_in(key, 6)
    for dim, blocks in cuts:
        steps = jnp.exp(jax.random.uniform(jax.random.fold_in(own, dim), (blocks,), jnp.float32, low / len(cuts), largest / len(cuts)))
        level = level * jnp.repeat(steps, extent[dim] // blocks).reshape([-1 if axis == dim else 1 for axis in range(len(extent))])
    return level


def noise(rng, shape, deviation, limit, pieces=(), held_as=jnp.bfloat16):
    entries = jax.random.normal(rng, shape, jnp.float32) * deviation
    if len(pieces) > 0:
        entries = steps_of(rng, shape, pieces, -0.22, 0.18) * entries
    return jnp.clip(entries, min=-limit, max=limit).astype(held_as)


def setup_inputs(seed: int = 0) -> dict:
    streams_of = jax.random.split(jax.random.key(seed), 8)
    latent = draw_latent(jax.random.fold_in(streams_of[7], 71), 0)
    ada_scale = jnp.clip(jax.random.uniform(streams_of[1], (C,), jnp.float32, -0.5, 0.5), -0.5, 0.5)
    ada_shift = noise(streams_of[2], (C,), 0.5, 3.0, (), jnp.float32)
    conv_weight = noise(streams_of[3], (9 * C, C), (9 * C) ** -0.5, 0.078125, ((0, 32),))
    qkv_weight = draw_qkv_weight(jax.random.fold_in(streams_of[7], 71), 0)
    out_weight = noise(streams_of[5], (C, C), C ** -0.5, 0.25)
    ancestors = place_ends(jax.random.randint(streams_of[6], (PARTICLES,), 0, PARTICLES), jax.random.fold_in(streams_of[6], 1), 0, PARTICLES - 1).astype(jnp.int32)
    return {"latent": latent, "ada_scale": ada_scale, "ada_shift": ada_shift, "conv_weight": conv_weight, "qkv_weight": qkv_weight, "out_weight": out_weight, "ancestors": ancestors}


def group_norm(values):
    grouped = values.reshape(values.shape[0], GROUPS, -1)
    count = grouped.shape[0] * grouped.shape[2]
    mean_g = lax.optimization_barrier(jnp.sum(grouped, axis=(0, 2))) / count
    square_g = lax.optimization_barrier(jnp.sum(grouped * grouped, axis=(0, 2))) / count
    inverse = lax.rsqrt(square_g - mean_g * mean_g + 1e-05)
    per_group = C // GROUPS
    return (values - jnp.repeat(mean_g, per_group)) * jnp.repeat(inverse, per_group)

def reference(latent, ada_scale, ada_shift, conv_weight, qkv_weight, out_weight, ancestors):
    head_dim = C // HEADS

    def heads_of(block):
        return block.reshape(H * W, HEADS, head_dim).transpose(1, 0, 2)

    def one_head(triple):
        query_h, key_h, value_h = triple
        scores = jnp.dot(query_h, key_h.T, preferred_element_type=jnp.float32) * head_dim ** (-0.5)
        top = lax.optimization_barrier(jnp.max(scores, axis=1, keepdims=True))
        weights = jnp.exp(scores - top)
        total = lax.optimization_barrier(jnp.sum(weights, axis=1, keepdims=True))
        return jnp.dot(weights.astype(jnp.bfloat16), value_h, preferred_element_type=jnp.float32) / total

    def one_particle(latent_p):
        field = latent_p.astype(jnp.float32).reshape(H * W, C)
        active = jax.nn.silu(group_norm(field) * (1.0 + ada_scale) + ada_shift).astype(jnp.bfloat16)
        padded = jnp.pad(active.reshape(H, W, C), ((1, 1), (1, 1), (0, 0)))
        conv = jnp.zeros((H * W, C), jnp.float32)
        for row_off in range(3):
            for col_off in range(3):
                tap = row_off * 3 + col_off
                window = padded[row_off:row_off + H, col_off:col_off + W].reshape(H * W, C)
                conv = conv + jnp.dot(window, conv_weight[tap * C:(tap + 1) * C], preferred_element_type=jnp.float32)
        resid = lax.optimization_barrier((field + conv).astype(jnp.bfloat16))
        normed = group_norm(resid.astype(jnp.float32)).astype(jnp.bfloat16)
        project = jnp.dot(normed, qkv_weight, preferred_element_type=jnp.float32).astype(jnp.bfloat16)
        triple = (heads_of(project[:, :C]), heads_of(project[:, C:2 * C]), heads_of(project[:, 2 * C:]))
        mixed = lax.map(one_head, triple)
        attended = mixed.transpose(1, 0, 2).reshape(H * W, C).astype(jnp.bfloat16)
        output = resid.astype(jnp.float32) + jnp.dot(attended, out_weight, preferred_element_type=jnp.float32)
        return output.astype(jnp.bfloat16).reshape(H, W, C)
    blocks = lax.map(one_particle, latent)
    return jnp.take(blocks, ancestors.astype(jnp.int32), axis=0)
```

```python
import functools

import jax
import jax.numpy as jnp
from jax import lax
from jax.experimental import pallas as pl
from jax.experimental.pallas import tpu as pltpu
from jax.sharding import Mesh
from jax.sharding import PartitionSpec as P

HEADS = 10
GROUPS = 32
CHANS = 640
WIDTH = 24
ROWS_HERE = 4
TOKENS = ROWS_HERE * WIDTH
PARTICLES = 16
ROW_DEVS = 32
PER_GROUP = CHANS // GROUPS
SLICE = CHANS // PARTICLES
COUNT = ROWS_HERE * ROW_DEVS * WIDTH * PER_GROUP
LANES = 128
KERNEL_ROWS = 9 * CHANS // ROW_DEVS
QUERY_BLOCKS = 3
SLOT = TOKENS + 16

PART = ("x", "z_lo", "core")
CHIPS = ("x", "z_lo")
ROWS = ("z_hi", "y")

NT = (((1,), (1,)), ((), ()))
F32 = jnp.float32
BF16 = jnp.bfloat16
SMEM = pl.BlockSpec(memory_space=pltpu.SMEM)
VMEM = pl.BlockSpec(memory_space=pltpu.VMEM)


def call(kernel, out_shape, in_specs, flops, size, vmem=16, scratch=()):
    out_specs = jax.tree.map(lambda _: VMEM, out_shape)
    return pl.pallas_call(
        kernel,
        out_shape=out_shape,
        in_specs=in_specs,
        out_specs=out_specs,
        scratch_shapes=list(scratch),
        compiler_params=pltpu.CompilerParams(vmem_limit_bytes=vmem * 1024 * 1024),
        cost_estimate=pl.CostEstimate(flops=flops, bytes_accessed=size, transcendentals=0),
    )


def shaped(*shape, dtype=BF16):
    return jax.ShapeDtypeStruct(shape, dtype)


def iota(shape, dim):
    return lax.broadcasted_iota(jnp.int32, shape, dim)


def exact_dot(a, b):
    return jnp.dot(a, b, precision=lax.Precision.HIGHEST, preferred_element_type=F32)


def group_row(values):
    sums = jnp.sum(values, axis=0, keepdims=True)
    squares = jnp.sum(values * values, axis=0, keepdims=True)
    chan, lane = iota((CHANS, LANES), 0), iota((CHANS, LANES), 1)
    first = ((chan >= lane * PER_GROUP) & (chan < (lane + 1) * PER_GROUP)).astype(F32)
    other = lane - GROUPS
    second = ((chan >= other * PER_GROUP) & (chan < (other + 1) * PER_GROUP)).astype(F32)
    eight = lambda row: jnp.broadcast_to(row, (8, CHANS))
    return exact_dot(eight(sums), first) + exact_dot(eight(squares), second)


def mean_and_inverse(totals):
    lane, chan = iota((LANES, CHANS), 0), iota((LANES, CHANS), 1)
    first = ((chan >= lane * PER_GROUP) & (chan < (lane + 1) * PER_GROUP)).astype(F32)
    other = lane - GROUPS
    second = ((chan >= other * PER_GROUP) & (chan < (other + 1) * PER_GROUP)).astype(F32)
    mean = exact_dot(totals, first) * (1.0 / COUNT)
    square = exact_dot(totals, second) * (1.0 / COUNT)
    return mean, lax.rsqrt(square - mean * mean + 1e-05)


def sums_kernel(x_ref, out_ref):
    row = group_row(x_ref[...].astype(F32))
    out_ref[...] = jnp.broadcast_to(row[None], out_ref.shape)


def total_kernel(x_ref, out_ref):
    out_ref[...] = jnp.broadcast_to(jnp.sum(x_ref[...], axis=0)[None], out_ref.shape)


def pick_kernel(p_ref, w_ref, out_ref):
    row, col = iota((48, CHANS), 0), iota((48, CHANS), 1)
    chosen = ((col == row + p_ref[0] * SLICE) & (row < SLICE)).astype(F32).astype(BF16)
    picked = lax.dot_general(chosen, w_ref[...], NT, preferred_element_type=F32)
    out_ref[...] = jnp.zeros_like(out_ref)
    for r in range(ROW_DEVS):
        out_ref[r, :, :KERNEL_ROWS] = picked.astype(BF16)


PLACE = {1: 0, 0: 1, 2: 2}


def weights_kernel(x_ref, out_ref, flat_ref, tall_ref):
    flat_ref[...] = jnp.zeros_like(flat_ref)
    for r in range(ROW_DEVS):
        at = r * KERNEL_ROWS
        block, off = at // LANES, at % LANES
        piece = x_ref[r].astype(F32)
        wide = jnp.concatenate([piece, jnp.zeros((48, LANES), F32)], axis=1)
        if off:
            wide = pltpu.roll(wide, off, 1)
        spot = slice(block * LANES, (block + 3) * LANES)
        flat_ref[:, spot] = flat_ref[:, spot] + wide
    tall_ref[...] = jnp.zeros_like(tall_ref)
    for a in range(3):
        for b in range(3):
            tap = 3 * a + b
            top = a * LANES + PLACE[b] * SLICE
            tall_ref[top : top + SLICE, :] = flat_ref[:SLICE, tap * CHANS : (tap + 1) * CHANS]
    out_ref[...] = tall_ref[...].astype(BF16)


def conv_kernel(place_ref, own_ref, other_ref, totals_ref, scale_ref, shift_ref, w_ref,
                part_ref, up_ref, down_ref, gain_ref, bias_ref):
    mean, inverse = mean_and_inverse(totals_ref[:, 0, :])
    gain = inverse * (1.0 + scale_ref[...])
    gain_ref[...] = gain
    bias_ref[...] = shift_ref[...] - mean * gain
    p, core = place_ref[0], place_ref[1]
    row, col = iota((LANES, CHANS), 0), iota((LANES, CHANS), 1)
    chosen = ((col == row + p * SLICE) & (row < SLICE)).astype(F32).astype(BF16)
    weights = w_ref[...]
    each = 2
    for which, ref in ((0, own_ref), (1, other_ref)):
        first = core if which == 0 else 1 - core
        for step in range(PARTICLES // 2 // each):
            active, raw = [], []
            for k in range(each):
                j = step * each + k
                q = 2 * j + first
                x = ref[j]
                v = x.astype(F32) * gain_ref[pl.ds(q, 1), :] + bias_ref[pl.ds(q, 1), :]
                half = 0.5 * v
                active.append((half + half * jnp.tanh(half)).astype(BF16))
                raw.append(x)
            active = jnp.concatenate(active, axis=0)
            raw = jnp.concatenate(raw, axis=0)
            taps = lax.dot_general(active, weights, NT, preferred_element_type=F32)
            field = lax.dot_general(raw, chosen, NT, preferred_element_type=F32)
            for k in range(each):
                q = 2 * (step * each + k) + first
                rows = slice(k * TOKENS, (k + 1) * TOKENS)
                t0, t1, t2 = (taps[rows, n * LANES : (n + 1) * LANES] for n in range(3))
                base = t1 + field[rows]
                last = TOKENS - WIDTH
                part_ref[q, :WIDTH] = base[:WIDTH] + t2[WIDTH : 2 * WIDTH]
                part_ref[q, WIDTH:last] = (
                    base[WIDTH:last] + t0[: last - WIDTH] + t2[2 * WIDTH :]
                )
                part_ref[q, last:] = base[last:] + t0[last - WIDTH : last]
                up_ref[q] = t2[:WIDTH]
                down_ref[q] = t0[last:]


def finish_kernel(anc_ref, part_ref, above_ref, below_ref, out_ref):
    row, lane = iota((TOKENS, LANES), 0), iota((TOKENS, LANES), 1)
    at = lax.rem(row, WIDTH)
    lane_s = iota((32, LANES), 1)
    last = TOKENS - WIDTH
    for p in range(PARTICLES):
        q = anc_ref[p]
        full = jnp.concatenate(
            [
                part_ref[q, :WIDTH] + above_ref[q],
                part_ref[q, WIDTH:last],
                part_ref[q, last:] + below_ref[q],
            ],
            axis=0,
        )
        left = pltpu.roll(pltpu.roll(full, 1, 0), LANES - SLICE, 1)
        right = pltpu.roll(pltpu.roll(full, TOKENS - 1, 0), LANES - 2 * SLICE, 1)
        total = full + jnp.where(at == 0, 0.0, left) + jnp.where(at == WIDTH - 1, 0.0, right)
        total = jnp.where(lane < SLICE, total, 0.0)
        packed = total[:32]
        for t in (1, 2):
            packed = packed + pltpu.roll(total[32 * t : 32 * (t + 1)], SLICE * t, 1)
        out_ref[p] = packed.astype(BF16)


def gather_kernel(x_ref, resid_ref, out_ref, wide_ref):
    lane = iota((32, LANES), 1)
    for t in range(3):
        blocks = [jnp.zeros((32, LANES), F32) for _ in range(CHANS // LANES)]
        for p in range(PARTICLES):
            block, off = (p * SLICE) // LANES, (p * SLICE) % LANES
            turn = (off - t * SLICE) % LANES
            piece = x_ref[p].astype(F32)
            if turn:
                piece = pltpu.roll(piece, turn, 1)
            end = off + SLICE
            blocks[block] = jnp.where((lane >= off) & (lane < end), piece, blocks[block])
            if end > LANES:
                blocks[block + 1] = jnp.where(lane < end - LANES, piece, blocks[block + 1])
        for n, value in enumerate(blocks):
            wide_ref[32 * t : 32 * (t + 1), n * LANES : (n + 1) * LANES] = value
    wide = wide_ref[...]
    resid_ref[...] = wide.astype(BF16)
    out_ref[...] = jnp.broadcast_to(group_row(wide)[None], out_ref.shape)


def project_kernel(totals_ref, resid_ref, w_ref, out_ref, both_ref):
    mean, inverse = mean_and_inverse(jnp.sum(totals_ref[...], axis=0))
    normed = ((resid_ref[...].astype(F32) - mean[:1]) * inverse[:1]).astype(BF16)
    both_ref[...] = jnp.dot(normed, w_ref[...], preferred_element_type=F32)
    low = iota((TOKENS, LANES), 1) < 64
    low_s = iota((16, LANES), 1) < 64
    for pair in range(HEADS // 2):
        q, k, v = (
            both_ref[:, n * CHANS + pair * LANES : n * CHANS + (pair + 1) * LANES] for n in range(3)
        )
        q_turn, k_turn, v_turn = (pltpu.roll(x, 64, 1) for x in (q, k, v))
        mixed = (jnp.where(low, k, v_turn), jnp.where(low, k_turn, v))
        lows, highs = (q, q_turn), (q_turn, q)
        for side in range(2):
            keys_values = mixed[side].astype(BF16)
            for b in range(QUERY_BLOCKS):
                slot = (2 * pair + side) * QUERY_BLOCKS + b
                at = 32 * b
                two = jnp.where(low_s, lows[side][at : at + 16], highs[side][at + 16 : at + 32])
                out_ref[slot, :TOKENS] = keys_values
                out_ref[slot, TOKENS:] = two.astype(BF16)
    for slot in range(HEADS * QUERY_BLOCKS, ROW_DEVS):
        out_ref[slot] = jnp.zeros((SLOT, LANES), BF16)


def attend_kernel(x_ref, out_ref, keys_ref, ones_ref, query_ref, half_ref):
    low = iota((TOKENS, LANES), 1) < 64
    for r in range(ROW_DEVS):
        block = x_ref[r, :TOKENS]
        keys_ref[r * TOKENS : (r + 1) * TOKENS] = block
        ones_ref[r * TOKENS : (r + 1) * TOKENS] = jnp.where(low, jnp.ones_like(block), block)
        query_ref[r * 16 : (r + 1) * 16] = x_ref[r, TOKENS:].astype(F32)
    size = 256
    low_q = iota((size, LANES), 1) < 64
    factor = 0.125 * 1.4426950408889634
    for n in range(2):
        here = query_ref[n * size : (n + 1) * size]
        for side in range(2):
            turned = here if side == 0 else pltpu.roll(here, 64, 1)
            query = jnp.where(low_q, turned, 0.0).astype(BF16)
            scores = lax.dot_general(query, keys_ref[...], NT, preferred_element_type=F32)
            top = jnp.max(scores, axis=1, keepdims=True)
            weights = jnp.exp2((scores - top) * factor).astype(BF16)
            result = jnp.dot(weights, ones_ref[...], preferred_element_type=F32)
            other = pltpu.roll(result, 64, 1)
            if side == 0:
                half_ref[...] = other / result
            else:
                both = jnp.where(low_q, half_ref[...], result / other).astype(BF16)
                for r in range(size // 16):
                    out_ref[n * (size // 16) + r] = both[r * 16 : (r + 1) * 16]


def output_kernel(x_ref, resid_ref, w_ref, out_ref, wide_ref):
    low = iota((16, LANES), 1) < 64
    for pair in range(HEADS // 2):
        for b in range(QUERY_BLOCKS):
            first = x_ref[2 * pair * QUERY_BLOCKS + b].astype(F32)
            second = x_ref[(2 * pair + 1) * QUERY_BLOCKS + b].astype(F32)
            cols = slice(pair * LANES, (pair + 1) * LANES)
            at = 32 * b
            wide_ref[at : at + 16, cols] = jnp.where(low, first, pltpu.roll(second, 64, 1))
            wide_ref[at + 16 : at + 32, cols] = jnp.where(low, pltpu.roll(first, 64, 1), second)
    mixed = wide_ref[...].astype(BF16)
    product = jnp.dot(mixed, w_ref[...], preferred_element_type=F32)
    out_ref[...] = (resid_ref[...].astype(F32) + product).astype(BF16)


def exchange(values, axes):
    return lax.all_to_all(values, axes, split_axis=0, concat_axis=0, tiled=True)


def per_device(latent, ada_scale, ada_shift, conv_weight, qkv_weight, out_weight, ancestors):
    slab = latent.reshape(TOKENS, CHANS)
    particle = lax.axis_index(PART).astype(jnp.int32)
    core = lax.axis_index("core").astype(jnp.int32)
    where = jnp.stack([particle, core])

    sums = call(sums_kernel, shaped(ROW_DEVS, 8, LANES, dtype=F32), [VMEM], 10**6, 10**5)(slab)
    sums = exchange(sums, ROWS)
    totals = call(total_kernel, shaped(PARTICLES, 8, LANES, dtype=F32), [VMEM], 10**5, 10**5)(sums)
    totals = exchange(totals, PART)

    own = exchange(jnp.broadcast_to(slab[None], (PARTICLES // 2, TOKENS, CHANS)), CHIPS)
    other = lax.ppermute(own, "core", [(0, 1), (1, 0)])

    picked = call(pick_kernel, shaped(ROW_DEVS, 48, 256), [SMEM, VMEM], 10**7, 10**6)(
        where, conv_weight
    )
    picked = exchange(picked, ROWS)
    weights = call(
        weights_kernel,
        shaped(3 * LANES, CHANS),
        [VMEM],
        10**6,
        10**6,
        scratch=(
            pltpu.VMEM((48, 9 * CHANS + 2 * LANES), F32),
            pltpu.VMEM((3 * LANES, CHANS), F32),
        ),
    )(picked)

    edge = shaped(PARTICLES, WIDTH, LANES, dtype=F32)
    part, up, down = call(
        conv_kernel,
        [shaped(PARTICLES, TOKENS, LANES, dtype=F32), edge, edge],
        [SMEM] + [VMEM] * 6,
        2 * 10**9,
        4 * 10**6,
        vmem=32,
        scratch=(pltpu.VMEM((PARTICLES, CHANS), F32), pltpu.VMEM((PARTICLES, CHANS), F32)),
    )(where, own, other, totals, ada_scale[None], ada_shift[None], weights)
    above = lax.ppermute(down, ROWS, [(i, i + 1) for i in range(ROW_DEVS - 1)])
    below = lax.ppermute(up, ROWS, [(i + 1, i) for i in range(ROW_DEVS - 1)])
    pieces = call(
        finish_kernel, shaped(PARTICLES, 32, LANES), [SMEM] + [VMEM] * 3, 10**6, 10**6
    )(ancestors, part, above, below)
    pieces = exchange(pieces, PART)

    resid, sums = call(
        gather_kernel,
        [shaped(TOKENS, CHANS), shaped(ROW_DEVS, 8, LANES, dtype=F32)],
        [VMEM],
        10**6,
        10**6,
        scratch=(pltpu.VMEM((TOKENS, CHANS), F32),),
    )(pieces)
    sums = exchange(sums, ROWS)
    slots = call(
        project_kernel,
        shaped(ROW_DEVS, SLOT, LANES),
        [VMEM] * 3,
        3 * 10**8,
        4 * 10**6,
        scratch=(pltpu.VMEM((TOKENS, 3 * CHANS), F32),),
    )(sums, resid, qkv_weight)
    slots = exchange(slots, ROWS)
    rows = ROW_DEVS * TOKENS
    mixed = call(
        attend_kernel,
        shaped(ROW_DEVS, 16, LANES),
        [VMEM],
        2 * 10**9,
        2 * 10**6,
        vmem=40,
        scratch=(
            pltpu.VMEM((rows, LANES), BF16),
            pltpu.VMEM((rows, LANES), BF16),
            pltpu.VMEM((ROW_DEVS * 16, LANES), F32),
            pltpu.VMEM((256, LANES), F32),
        ),
    )(slots)
    mixed = exchange(mixed, ROWS)
    block = call(
        output_kernel,
        shaped(TOKENS, CHANS),
        [VMEM] * 3,
        10**8,
        10**6,
        scratch=(pltpu.VMEM((TOKENS, CHANS), F32),),
    )(mixed, resid, out_weight)
    return block.reshape(1, ROWS_HERE, WIDTH, CHANS)


def solution(mesh):
    split = Mesh(mesh.devices.reshape(4, 2, 2, 4, 8), PART + ROWS)
    placed = (P(PART, ROWS, None, None), P(), P(), P(ROWS, None), P(), P(), P())
    return jax.shard_map(
        per_device,
        mesh=split,
        in_specs=placed,
        out_specs=P(PART, ROWS, None, None),
        check_vma=False,
    )
```

```python
import functools

import jax
import jax.numpy as jnp
from jax import lax
from jax.experimental import pallas as pl
from jax.experimental.pallas import tpu as pltpu
from jax.sharding import Mesh
from jax.sharding import PartitionSpec as P

HEADS = 10
GROUPS = 32
CHANS = 640
WIDTH = 24
ROWS_HERE = 4
TOKENS = ROWS_HERE * WIDTH
PARTICLES = 16
ROW_DEVS = 32
PER_GROUP = CHANS // GROUPS
SLICE = CHANS // PARTICLES
COUNT = ROWS_HERE * ROW_DEVS * WIDTH * PER_GROUP
LANES = 128
KERNEL_ROWS = 9 * CHANS // ROW_DEVS
TAIL = KERNEL_ROWS - LANES
QUERY_BLOCKS = 3
SLOT = TOKENS + 16

PART = ("x", "z_lo", "core")
ROWS = ("z_hi", "y")

NT = (((1,), (1,)), ((), ()))
F32 = jnp.float32
BF16 = jnp.bfloat16
SMEM = pl.BlockSpec(memory_space=pltpu.SMEM)
VMEM = pl.BlockSpec(memory_space=pltpu.VMEM)


def call(kernel, out_shape, in_specs, flops, size, vmem=16, scratch=()):
    out_specs = jax.tree.map(lambda _: VMEM, out_shape)
    return pl.pallas_call(
        kernel,
        out_shape=out_shape,
        in_specs=in_specs,
        out_specs=out_specs,
        scratch_shapes=list(scratch),
        compiler_params=pltpu.CompilerParams(vmem_limit_bytes=vmem * 1024 * 1024),
        cost_estimate=pl.CostEstimate(flops=flops, bytes_accessed=size, transcendentals=0),
    )


def shaped(*shape, dtype=BF16):
    return jax.ShapeDtypeStruct(shape, dtype)


def iota(shape, dim):
    return lax.broadcasted_iota(jnp.int32, shape, dim)


def exact_dot(a, b):
    return jnp.dot(a, b, precision=lax.Precision.HIGHEST, preferred_element_type=F32)


def group_row(values):
    sums = jnp.sum(values, axis=0, keepdims=True)
    squares = jnp.sum(values * values, axis=0, keepdims=True)
    chan, lane = iota((CHANS, LANES), 0), iota((CHANS, LANES), 1)
    first = ((chan >= lane * PER_GROUP) & (chan < (lane + 1) * PER_GROUP)).astype(F32)
    other = lane - GROUPS
    second = ((chan >= other * PER_GROUP) & (chan < (other + 1) * PER_GROUP)).astype(F32)
    eight = lambda row: jnp.broadcast_to(row, (8, CHANS))
    return exact_dot(eight(sums), first) + exact_dot(eight(squares), second)


def mean_and_inverse(totals):
    lane, chan = iota((LANES, CHANS), 0), iota((LANES, CHANS), 1)
    first = ((chan >= lane * PER_GROUP) & (chan < (lane + 1) * PER_GROUP)).astype(F32)
    other = lane - GROUPS
    second = ((chan >= other * PER_GROUP) & (chan < (other + 1) * PER_GROUP)).astype(F32)
    mean = exact_dot(totals, first) * (1.0 / COUNT)
    square = exact_dot(totals, second) * (1.0 / COUNT)
    return mean, lax.rsqrt(square - mean * mean + 1e-05)


def thirds(value):
    parts = []
    for _ in range(3):
        top = value.astype(BF16).astype(F32)
        parts.append(top)
        value = value - top
    return parts


def pick_kernel(place_ref, x_ref, w_ref, out_ref):
    row, col = iota((48, CHANS), 0), iota((48, CHANS), 1)
    chosen = ((col == row + place_ref[0] * SLICE) & (row < SLICE)).astype(F32).astype(BF16)
    picked = lax.dot_general(chosen, w_ref[...], NT, preferred_element_type=F32)
    head = picked[:, :LANES]
    rest = jnp.concatenate([picked[:, LANES:], jnp.zeros((48, LANES - TAIL), F32)], axis=1)
    turned = pltpu.roll(pltpu.roll(rest, 48 - 20, 0), 64, 1)
    sums = thirds(group_row(x_ref[...].astype(F32)))
    row, lane = iota((24, LANES), 0), iota((24, LANES), 1)
    low = jnp.where(lane < 64, rest[:24], turned[:24])
    for n in range(3):
        low = jnp.where(row == 20 + n, sums[n][:1], low)
    low = jnp.where(row == 23, 0.0, low)
    slot = jnp.concatenate([head[:SLICE], low], axis=0).astype(BF16)
    out_ref[...] = jnp.broadcast_to(slot[None], out_ref.shape)


def total_kernel(x_ref, out_ref):
    total = jnp.zeros((16, LANES), F32)
    for r in range(ROW_DEVS):
        total = total + x_ref[r, 48:64].astype(F32)
    row = total[12:13] + total[13:14] + total[14:15]
    out_ref[...] = jnp.broadcast_to(row[None], out_ref.shape)


PLACE = {1: 0, 0: 1, 2: 2}


def weights_kernel(x_ref, out_ref, flat_ref, tall_ref):
    flat_ref[...] = jnp.zeros_like(flat_ref)
    row, lane = iota((SLICE, LANES), 0), iota((SLICE, LANES), 1)
    for r in range(ROW_DEVS):
        at = r * KERNEL_ROWS
        block, off = at // LANES, at % LANES
        slot = x_ref[r].astype(F32)
        low = jnp.concatenate([slot[SLICE:], jnp.zeros((16, LANES), F32)], axis=0)
        rest = jnp.where(row < 20, low, pltpu.roll(pltpu.roll(low, 20, 0), 64, 1))
        rest = jnp.where(lane < TAIL, rest, 0.0)
        wide = jnp.concatenate([slot[:SLICE], rest, jnp.zeros((SLICE, LANES), F32)], axis=1)
        if off:
            wide = pltpu.roll(wide, off, 1)
        spot = slice(block * LANES, (block + 3) * LANES)
        flat_ref[:, spot] = flat_ref[:, spot] + wide
    tall_ref[...] = jnp.zeros_like(tall_ref)
    for a in range(3):
        for b in range(3):
            tap = 3 * a + b
            top = a * LANES + PLACE[b] * SLICE
            tall_ref[top : top + SLICE, :] = flat_ref[:, tap * CHANS : (tap + 1) * CHANS]
    out_ref[...] = tall_ref[...].astype(BF16)


def gain_and_bias(totals_ref, scale_ref, shift_ref):
    mean, inverse = mean_and_inverse(totals_ref[:, 0, :])
    gain = inverse * (1.0 + scale_ref[...])
    return gain, shift_ref[...] - mean * gain


def silu(v):
    half = 0.5 * v
    return (half + half * jnp.tanh(half)).astype(BF16)


def across(full):
    rows = full.shape[0]
    at = lax.rem(iota((rows, LANES), 0), WIDTH)
    left = pltpu.roll(pltpu.roll(full, 1, 0), LANES - SLICE, 1)
    right = pltpu.roll(pltpu.roll(full, rows - 1, 0), LANES - 2 * SLICE, 1)
    total = full + jnp.where(at == 0, 0.0, left) + jnp.where(at == WIDTH - 1, 0.0, right)
    return jnp.where(iota((rows, LANES), 1) < SLICE, total, 0.0)


def packed(value):
    n = value.shape[0] // 3
    out = value[:n]
    for t in (1, 2):
        out = out + pltpu.roll(value[n * t : n * (t + 1)], SLICE * t, 1)
    return out


def unpacked(value):
    return jnp.concatenate(
        [value] + [pltpu.roll(value, LANES - SLICE * t, 1) for t in (1, 2)], axis=0
    )


def edge_kernel(x_ref, totals_ref, scale_ref, shift_ref, w_ref, up_ref, down_ref):
    gain, bias = gain_and_bias(totals_ref, scale_ref, shift_ref)
    for rows, tap, ref in (
        (slice(0, WIDTH), 2, up_ref),
        (slice(TOKENS - WIDTH, TOKENS), 0, down_ref),
    ):
        active = []
        for q in range(PARTICLES):
            x = x_ref[q].astype(F32)[rows]
            active.append(silu(x * gain[q : q + 1] + bias[q : q + 1]))
        active = jnp.concatenate(active, axis=0)
        weights = w_ref[tap * LANES : (tap + 1) * LANES, :]
        full = lax.dot_general(active, weights, NT, preferred_element_type=F32)
        full = across(full)
        for q in range(PARTICLES):
            ref[q] = packed(full[q * WIDTH : (q + 1) * WIDTH])


def conv_kernel(place_ref, x_ref, totals_ref, scale_ref, shift_ref, w_ref, part_ref):
    gain, bias = gain_and_bias(totals_ref, scale_ref, shift_ref)
    row, col = iota((LANES, CHANS), 0), iota((LANES, CHANS), 1)
    chosen = ((col == row + place_ref[0] * SLICE) & (row < SLICE)).astype(F32).astype(BF16)
    weights = w_ref[...]
    each = 2
    last = TOKENS - WIDTH
    for step in range(PARTICLES // each):
        active, raw = [], []
        for q in range(step * each, (step + 1) * each):
            x = x_ref[q]
            raw.append(x)
            active.append(silu(x.astype(F32) * gain[q : q + 1] + bias[q : q + 1]))
        active = jnp.concatenate(active, axis=0)
        raw = jnp.concatenate(raw, axis=0)
        taps = lax.dot_general(active, weights, NT, preferred_element_type=F32)
        field = lax.dot_general(raw, chosen, NT, preferred_element_type=F32)
        for k in range(each):
            rows = slice(k * TOKENS, (k + 1) * TOKENS)
            t0, t1, t2 = (taps[rows, n * LANES : (n + 1) * LANES] for n in range(3))
            base = t1 + field[rows]
            full = jnp.concatenate(
                [
                    base[:WIDTH] + t2[WIDTH : 2 * WIDTH],
                    base[WIDTH:last] + t0[: last - WIDTH] + t2[2 * WIDTH :],
                    base[last:] + t0[last - WIDTH : last],
                ],
                axis=0,
            )
            part_ref[step * each + k] = across(full)


def finish_kernel(anc_ref, part_ref, above_ref, below_ref, out_ref):
    last = TOKENS - WIDTH
    lane = iota((TOKENS, LANES), 1)
    for p in range(PARTICLES):
        q = anc_ref[p]
        total = jnp.concatenate(
            [
                part_ref[q, :WIDTH] + unpacked(above_ref[q]),
                part_ref[q, WIDTH:last],
                part_ref[q, last:] + unpacked(below_ref[q]),
            ],
            axis=0,
        )
        out_ref[p] = packed(jnp.where(lane < SLICE, total, 0.0)).astype(BF16)


def gather_kernel(x_ref, resid_ref, out_ref, wide_ref):
    lane = iota((32, LANES), 1)
    for t in range(3):
        blocks = [jnp.zeros((32, LANES), F32) for _ in range(CHANS // LANES)]
        for p in range(PARTICLES):
            block, off = (p * SLICE) // LANES, (p * SLICE) % LANES
            turn = (off - t * SLICE) % LANES
            piece = x_ref[p].astype(F32)
            if turn:
                piece = pltpu.roll(piece, turn, 1)
            end = off + SLICE
            blocks[block] = jnp.where((lane >= off) & (lane < end), piece, blocks[block])
            if end > LANES:
                blocks[block + 1] = jnp.where(lane < end - LANES, piece, blocks[block + 1])
        for n, value in enumerate(blocks):
            wide_ref[32 * t : 32 * (t + 1), n * LANES : (n + 1) * LANES] = value
    wide = wide_ref[...]
    resid_ref[...] = wide.astype(BF16)
    out_ref[...] = jnp.broadcast_to(group_row(wide)[None], out_ref.shape)


def project_kernel(totals_ref, resid_ref, w_ref, out_ref, both_ref):
    mean, inverse = mean_and_inverse(jnp.sum(totals_ref[...], axis=0))
    normed = ((resid_ref[...].astype(F32) - mean[:1]) * inverse[:1]).astype(BF16)
    both_ref[...] = jnp.dot(normed, w_ref[...], preferred_element_type=F32)
    low = iota((TOKENS, LANES), 1) < 64
    low_s = iota((16, LANES), 1) < 64
    for pair in range(HEADS // 2):
        q, k, v = (
            both_ref[:, n * CHANS + pair * LANES : n * CHANS + (pair + 1) * LANES] for n in range(3)
        )
        q_turn, k_turn, v_turn = (pltpu.roll(x, 64, 1) for x in (q, k, v))
        mixed = (jnp.where(low, k, v_turn), jnp.where(low, k_turn, v))
        lows, highs = (q, q_turn), (q_turn, q)
        for side in range(2):
            keys_values = mixed[side].astype(BF16)
            for b in range(QUERY_BLOCKS):
                slot = (2 * pair + side) * QUERY_BLOCKS + b
                at = 32 * b
                two = jnp.where(low_s, lows[side][at : at + 16], highs[side][at + 16 : at + 32])
                out_ref[slot, :TOKENS] = keys_values
                out_ref[slot, TOKENS:] = two.astype(BF16)
    for slot in range(HEADS * QUERY_BLOCKS, ROW_DEVS):
        out_ref[slot] = jnp.zeros((SLOT, LANES), BF16)


def attend_kernel(x_ref, out_ref, keys_ref, ones_ref, query_ref, half_ref):
    low = iota((TOKENS, LANES), 1) < 64
    for r in range(ROW_DEVS):
        block = x_ref[r, :TOKENS]
        keys_ref[r * TOKENS : (r + 1) * TOKENS] = block
        ones_ref[r * TOKENS : (r + 1) * TOKENS] = jnp.where(low, jnp.ones_like(block), block)
        query_ref[r * 16 : (r + 1) * 16] = x_ref[r, TOKENS:].astype(F32)
    size = 256
    low_q = iota((size, LANES), 1) < 64
    factor = 0.125 * 1.4426950408889634
    for n in range(2):
        here = query_ref[n * size : (n + 1) * size]
        for side in range(2):
            turned = here if side == 0 else pltpu.roll(here, 64, 1)
            query = jnp.where(low_q, turned, 0.0).astype(BF16)
            scores = lax.dot_general(query, keys_ref[...], NT, preferred_element_type=F32)
            top = jnp.max(scores, axis=1, keepdims=True)
            weights = jnp.exp2((scores - top) * factor).astype(BF16)
            result = jnp.dot(weights, ones_ref[...], preferred_element_type=F32)
            other = pltpu.roll(result, 64, 1)
            if side == 0:
                half_ref[...] = other / result
            else:
                both = jnp.where(low_q, half_ref[...], result / other).astype(BF16)
                for r in range(size // 16):
                    out_ref[n * (size // 16) + r] = both[r * 16 : (r + 1) * 16]


def output_kernel(x_ref, resid_ref, w_ref, out_ref, wide_ref):
    low = iota((16, LANES), 1) < 64
    for pair in range(HEADS // 2):
        for b in range(QUERY_BLOCKS):
            first = x_ref[2 * pair * QUERY_BLOCKS + b].astype(F32)
            second = x_ref[(2 * pair + 1) * QUERY_BLOCKS + b].astype(F32)
            cols = slice(pair * LANES, (pair + 1) * LANES)
            at = 32 * b
            wide_ref[at : at + 16, cols] = jnp.where(low, first, pltpu.roll(second, 64, 1))
            wide_ref[at + 16 : at + 32, cols] = jnp.where(low, pltpu.roll(first, 64, 1), second)
    mixed = wide_ref[...].astype(BF16)
    product = jnp.dot(mixed, w_ref[...], preferred_element_type=F32)
    out_ref[...] = (resid_ref[...].astype(F32) + product).astype(BF16)


def exchange(values, axes):
    return lax.all_to_all(values, axes, split_axis=0, concat_axis=0, tiled=True)


def per_device(latent, ada_scale, ada_shift, conv_weight, qkv_weight, out_weight, ancestors):
    slab = latent.reshape(TOKENS, CHANS)
    place = lax.axis_index(PART).astype(jnp.int32)[None]

    slabs = lax.all_gather(slab, PART)

    picked = call(pick_kernel, shaped(ROW_DEVS, 64, LANES), [SMEM, VMEM, VMEM], 10**7, 10**6)(
        place, slab, conv_weight
    )
    picked = exchange(picked, ROWS)
    totals = call(total_kernel, shaped(PARTICLES, 8, LANES, dtype=F32), [VMEM], 10**5, 10**5)(picked)
    totals = exchange(totals, PART)
    weights = call(
        weights_kernel,
        shaped(3 * LANES, CHANS),
        [VMEM],
        10**6,
        10**6,
        scratch=(
            pltpu.VMEM((SLICE, 9 * CHANS + 2 * LANES), F32),
            pltpu.VMEM((3 * LANES, CHANS), F32),
        ),
    )(picked)

    scale, shift = ada_scale[None], ada_shift[None]
    edge = shaped(PARTICLES, WIDTH // 3, LANES, dtype=F32)
    up, down = call(edge_kernel, [edge, edge], [VMEM] * 5, 10**8, 10**6)(
        slabs, totals, scale, shift, weights
    )
    above = lax.ppermute(down, ROWS, [(i, i + 1) for i in range(ROW_DEVS - 1)])
    below = lax.ppermute(up, ROWS, [(i + 1, i) for i in range(ROW_DEVS - 1)])
    part = call(
        conv_kernel,
        shaped(PARTICLES, TOKENS, LANES, dtype=F32),
        [SMEM] + [VMEM] * 5,
        2 * 10**9,
        4 * 10**6,
        vmem=32,
    )(place, slabs, totals, scale, shift, weights)
    pieces = call(
        finish_kernel, shaped(PARTICLES, 32, LANES), [SMEM] + [VMEM] * 3, 10**6, 10**6
    )(ancestors, part, above, below)
    pieces = exchange(pieces, PART)

    resid, sums = call(
        gather_kernel,
        [shaped(TOKENS, CHANS), shaped(ROW_DEVS, 8, LANES, dtype=F32)],
        [VMEM],
        10**6,
        10**6,
        scratch=(pltpu.VMEM((TOKENS, CHANS), F32),),
    )(pieces)
    sums = exchange(sums, ROWS)
    slots = call(
        project_kernel,
        shaped(ROW_DEVS, SLOT, LANES),
        [VMEM] * 3,
        3 * 10**8,
        4 * 10**6,
        scratch=(pltpu.VMEM((TOKENS, 3 * CHANS), F32),),
    )(sums, resid, qkv_weight)
    slots = exchange(slots, ROWS)
    rows = ROW_DEVS * TOKENS
    mixed = call(
        attend_kernel,
        shaped(ROW_DEVS, 16, LANES),
        [VMEM],
        2 * 10**9,
        2 * 10**6,
        vmem=40,
        scratch=(
            pltpu.VMEM((rows, LANES), BF16),
            pltpu.VMEM((rows, LANES), BF16),
            pltpu.VMEM((ROW_DEVS * 16, LANES), F32),
            pltpu.VMEM((256, LANES), F32),
        ),
    )(slots)
    mixed = exchange(mixed, ROWS)
    block = call(
        output_kernel,
        shaped(TOKENS, CHANS),
        [VMEM] * 3,
        10**8,
        10**6,
        scratch=(pltpu.VMEM((TOKENS, CHANS), F32),),
    )(mixed, resid, out_weight)
    return block.reshape(1, ROWS_HERE, WIDTH, CHANS)


def solution(mesh):
    split = Mesh(mesh.devices.reshape(4, 2, 2, 4, 8), PART + ROWS)
    placed = (P(PART, ROWS, None, None), P(), P(), P(ROWS, None), P(), P(), P())
    return jax.shard_map(
        per_device,
        mesh=split,
        in_specs=placed,
        out_specs=P(PART, ROWS, None, None),
        check_vma=False,
    )
```

```python
import functools

import jax
import jax.numpy as jnp
from jax import lax
from jax.experimental import pallas as pl
from jax.experimental.pallas import tpu as pltpu
from jax.sharding import Mesh
from jax.sharding import PartitionSpec as P

HEADS = 10
GROUPS = 32
CHANS = 640
WIDTH = 24
ROWS_HERE = 4
TOKENS = ROWS_HERE * WIDTH
PARTICLES = 16
ROW_DEVS = 32
PER_GROUP = CHANS // GROUPS
SLICE = CHANS // PARTICLES
COUNT = ROWS_HERE * ROW_DEVS * WIDTH * PER_GROUP
LANES = 128
KERNEL_ROWS = 9 * CHANS // ROW_DEVS
TAIL = KERNEL_ROWS - LANES
QUERY_BLOCKS = 3
SLOT = TOKENS + 16

PART = ("x", "z_lo", "core")
ROWS = ("z_hi", "y")

NT = (((1,), (1,)), ((), ()))
F32 = jnp.float32
BF16 = jnp.bfloat16
SMEM = pl.BlockSpec(memory_space=pltpu.SMEM)
VMEM = pl.BlockSpec(memory_space=pltpu.VMEM)


def call(kernel, out_shape, in_specs, flops, size, vmem=16, scratch=()):
    out_specs = jax.tree.map(lambda _: VMEM, out_shape)
    return pl.pallas_call(
        kernel,
        out_shape=out_shape,
        in_specs=in_specs,
        out_specs=out_specs,
        scratch_shapes=list(scratch),
        compiler_params=pltpu.CompilerParams(vmem_limit_bytes=vmem * 1024 * 1024),
        cost_estimate=pl.CostEstimate(flops=flops, bytes_accessed=size, transcendentals=0),
    )


def shaped(*shape, dtype=BF16):
    return jax.ShapeDtypeStruct(shape, dtype)


def iota(shape, dim):
    return lax.broadcasted_iota(jnp.int32, shape, dim)


def exact_dot(a, b):
    return jnp.dot(a, b, precision=lax.Precision.HIGHEST, preferred_element_type=F32)


def group_row(values):
    sums = jnp.sum(values, axis=0, keepdims=True)
    squares = jnp.sum(values * values, axis=0, keepdims=True)
    chan, lane = iota((CHANS, LANES), 0), iota((CHANS, LANES), 1)
    first = ((chan >= lane * PER_GROUP) & (chan < (lane + 1) * PER_GROUP)).astype(F32)
    other = lane - GROUPS
    second = ((chan >= other * PER_GROUP) & (chan < (other + 1) * PER_GROUP)).astype(F32)
    eight = lambda row: jnp.broadcast_to(row, (8, CHANS))
    return exact_dot(eight(sums), first) + exact_dot(eight(squares), second)


def mean_and_inverse(totals):
    lane, chan = iota((LANES, CHANS), 0), iota((LANES, CHANS), 1)
    first = ((chan >= lane * PER_GROUP) & (chan < (lane + 1) * PER_GROUP)).astype(F32)
    other = lane - GROUPS
    second = ((chan >= other * PER_GROUP) & (chan < (other + 1) * PER_GROUP)).astype(F32)
    mean = exact_dot(totals, first) * (1.0 / COUNT)
    square = exact_dot(totals, second) * (1.0 / COUNT)
    return mean, lax.rsqrt(square - mean * mean + 1e-05)


def thirds(value):
    parts = []
    for _ in range(3):
        top = value.astype(BF16).astype(F32)
        parts.append(top)
        value = value - top
    return parts


def pick_kernel(place_ref, x_ref, w_ref, out_ref):
    row, col = iota((48, CHANS), 0), iota((48, CHANS), 1)
    chosen = ((col == row + place_ref[0] * SLICE) & (row < SLICE)).astype(F32).astype(BF16)
    picked = lax.dot_general(chosen, w_ref[...], NT, preferred_element_type=F32)
    head = picked[:, :LANES]
    rest = jnp.concatenate([picked[:, LANES:], jnp.zeros((48, LANES - TAIL), F32)], axis=1)
    turned = pltpu.roll(pltpu.roll(rest, 48 - 20, 0), 64, 1)
    sums = thirds(group_row(x_ref[...].astype(F32)))
    row, lane = iota((24, LANES), 0), iota((24, LANES), 1)
    low = jnp.where(lane < 64, rest[:24], turned[:24])
    for n in range(3):
        low = jnp.where(row == 20 + n, sums[n][:1], low)
    low = jnp.where(row == 23, 0.0, low)
    slot = jnp.concatenate([head[:SLICE], low], axis=0).astype(BF16)
    out_ref[...] = jnp.broadcast_to(slot[None], out_ref.shape)


def total_kernel(x_ref, out_ref):
    total = jnp.zeros((16, LANES), F32)
    for r in range(ROW_DEVS):
        total = total + x_ref[r, 48:64].astype(F32)
    row = total[12:13] + total[13:14] + total[14:15]
    out_ref[...] = jnp.broadcast_to(row[None], out_ref.shape)


PLACE = {1: 0, 0: 1, 2: 2}


def weights_kernel(x_ref, out_ref, flat_ref, tall_ref):
    flat_ref[...] = jnp.zeros_like(flat_ref)
    row, lane = iota((SLICE, LANES), 0), iota((SLICE, LANES), 1)
    for r in range(ROW_DEVS):
        at = r * KERNEL_ROWS
        block, off = at // LANES, at % LANES
        slot = x_ref[r].astype(F32)
        low = jnp.concatenate([slot[SLICE:], jnp.zeros((16, LANES), F32)], axis=0)
        rest = jnp.where(row < 20, low, pltpu.roll(pltpu.roll(low, 20, 0), 64, 1))
        rest = jnp.where(lane < TAIL, rest, 0.0)
        wide = jnp.concatenate([slot[:SLICE], rest, jnp.zeros((SLICE, LANES), F32)], axis=1)
        if off:
            wide = pltpu.roll(wide, off, 1)
        spot = slice(block * LANES, (block + 3) * LANES)
        flat_ref[:, spot] = flat_ref[:, spot] + wide
    tall_ref[...] = jnp.zeros_like(tall_ref)
    for a in range(3):
        for b in range(3):
            tap = 3 * a + b
            top = a * LANES + PLACE[b] * SLICE
            tall_ref[top : top + SLICE, :] = flat_ref[:, tap * CHANS : (tap + 1) * CHANS]
    out_ref[...] = tall_ref[...].astype(BF16)


STEPS = (0, 1, 3, 2)


def order(place_ref):
    x, z, core = place_ref[1], place_ref[2], place_ref[3]
    return [
        lax.rem(x + dx, 4) * 4 + lax.rem(z + dz, 2) * 2 + lax.rem(core + dc, 2)
        for dc in range(2)
        for dx in STEPS
        for dz in range(2)
    ]


def spot(place_ref, q):
    dx = lax.rem(q // 4 + 4 - place_ref[1], 4)
    dz = lax.rem(lax.rem(q // 2, 2) + place_ref[2], 2)
    dc = lax.rem(lax.rem(q, 2) + place_ref[3], 2)
    step = jnp.where(dx == 2, 3, jnp.where(dx == 3, 2, dx))
    return dc * 8 + step * 2 + dz


def gain_and_bias(place_ref, totals_ref, scale_ref, shift_ref):
    totals = jnp.concatenate([totals_ref[q, :1] for q in order(place_ref)], axis=0)
    mean, inverse = mean_and_inverse(totals)
    gain = inverse * (1.0 + scale_ref[...])
    return gain, shift_ref[...] - mean * gain


def silu(v):
    half = 0.5 * v
    return (half + half * jnp.tanh(half)).astype(BF16)


def across(full):
    rows = full.shape[0]
    at = lax.rem(iota((rows, LANES), 0), WIDTH)
    left = pltpu.roll(pltpu.roll(full, 1, 0), LANES - SLICE, 1)
    right = pltpu.roll(pltpu.roll(full, rows - 1, 0), LANES - 2 * SLICE, 1)
    total = full + jnp.where(at == 0, 0.0, left) + jnp.where(at == WIDTH - 1, 0.0, right)
    return jnp.where(iota((rows, LANES), 1) < SLICE, total, 0.0)


def packed(value):
    n = value.shape[0] // 3
    out = value[:n]
    for t in (1, 2):
        out = out + pltpu.roll(value[n * t : n * (t + 1)], SLICE * t, 1)
    return out


def unpacked(value):
    return jnp.concatenate(
        [value] + [pltpu.roll(value, LANES - SLICE * t, 1) for t in (1, 2)], axis=0
    )


def edge_kernel(place_ref, totals_ref, scale_ref, shift_ref, w_ref, *refs):
    slabs, (up_ref, down_ref) = refs[:8], refs[8:]
    gain, bias = gain_and_bias(place_ref, totals_ref, scale_ref, shift_ref)
    for rows, tap, ref in (
        (slice(0, WIDTH), 2, up_ref),
        (slice(TOKENS - WIDTH, TOKENS), 0, down_ref),
    ):
        active = []
        for q in range(PARTICLES):
            x = slabs[q // 2][q % 2].astype(F32)[rows]
            active.append(silu(x * gain[q : q + 1] + bias[q : q + 1]))
        active = jnp.concatenate(active, axis=0)
        weights = w_ref[tap * LANES : (tap + 1) * LANES, :]
        full = lax.dot_general(active, weights, NT, preferred_element_type=F32)
        full = across(full)
        for q in range(PARTICLES):
            ref[q] = packed(full[q * WIDTH : (q + 1) * WIDTH])


def conv_kernel(place_ref, totals_ref, scale_ref, shift_ref, w_ref, *refs):
    slabs, part_ref = refs[:8], refs[8]
    gain, bias = gain_and_bias(place_ref, totals_ref, scale_ref, shift_ref)
    row, col = iota((LANES, CHANS), 0), iota((LANES, CHANS), 1)
    chosen = ((col == row + place_ref[0] * SLICE) & (row < SLICE)).astype(F32).astype(BF16)
    weights = w_ref[...]
    each = 2
    last = TOKENS - WIDTH
    for step in range(PARTICLES // each):
        active, raw = [], []
        for q in range(step * each, (step + 1) * each):
            x = slabs[q // 2][q % 2]
            raw.append(x)
            active.append(silu(x.astype(F32) * gain[q : q + 1] + bias[q : q + 1]))
        active = jnp.concatenate(active, axis=0)
        raw = jnp.concatenate(raw, axis=0)
        taps = lax.dot_general(active, weights, NT, preferred_element_type=F32)
        field = lax.dot_general(raw, chosen, NT, preferred_element_type=F32)
        for k in range(each):
            rows = slice(k * TOKENS, (k + 1) * TOKENS)
            t0, t1, t2 = (taps[rows, n * LANES : (n + 1) * LANES] for n in range(3))
            base = t1 + field[rows]
            full = jnp.concatenate(
                [
                    base[:WIDTH] + t2[WIDTH : 2 * WIDTH],
                    base[WIDTH:last] + t0[: last - WIDTH] + t2[2 * WIDTH :],
                    base[last:] + t0[last - WIDTH : last],
                ],
                axis=0,
            )
            part_ref[step * each + k] = across(full)


def finish_kernel(place_ref, anc_ref, part_ref, above_ref, below_ref, out_ref):
    last = TOKENS - WIDTH
    lane = iota((TOKENS, LANES), 1)
    for p in range(PARTICLES):
        q = spot(place_ref, anc_ref[p])
        total = jnp.concatenate(
            [
                part_ref[q, :WIDTH] + unpacked(above_ref[q]),
                part_ref[q, WIDTH:last],
                part_ref[q, last:] + unpacked(below_ref[q]),
            ],
            axis=0,
        )
        out_ref[p] = packed(jnp.where(lane < SLICE, total, 0.0)).astype(BF16)


def gather_kernel(x_ref, resid_ref, out_ref, wide_ref):
    lane = iota((32, LANES), 1)
    for t in range(3):
        blocks = [jnp.zeros((32, LANES), F32) for _ in range(CHANS // LANES)]
        for p in range(PARTICLES):
            block, off = (p * SLICE) // LANES, (p * SLICE) % LANES
            turn = (off - t * SLICE) % LANES
            piece = x_ref[p].astype(F32)
            if turn:
                piece = pltpu.roll(piece, turn, 1)
            end = off + SLICE
            blocks[block] = jnp.where((lane >= off) & (lane < end), piece, blocks[block])
            if end > LANES:
                blocks[block + 1] = jnp.where(lane < end - LANES, piece, blocks[block + 1])
        for n, value in enumerate(blocks):
            wide_ref[32 * t : 32 * (t + 1), n * LANES : (n + 1) * LANES] = value
    wide = wide_ref[...]
    resid_ref[...] = wide.astype(BF16)
    out_ref[...] = jnp.broadcast_to(group_row(wide)[None], out_ref.shape)


def project_kernel(totals_ref, resid_ref, w_ref, out_ref, both_ref):
    mean, inverse = mean_and_inverse(jnp.sum(totals_ref[...], axis=0))
    normed = ((resid_ref[...].astype(F32) - mean[:1]) * inverse[:1]).astype(BF16)
    both_ref[...] = jnp.dot(normed, w_ref[...], preferred_element_type=F32)
    low = iota((TOKENS, LANES), 1) < 64
    low_s = iota((16, LANES), 1) < 64
    for pair in range(HEADS // 2):
        q, k, v = (
            both_ref[:, n * CHANS + pair * LANES : n * CHANS + (pair + 1) * LANES] for n in range(3)
        )
        q_turn, k_turn, v_turn = (pltpu.roll(x, 64, 1) for x in (q, k, v))
        mixed = (jnp.where(low, k, v_turn), jnp.where(low, k_turn, v))
        lows, highs = (q, q_turn), (q_turn, q)
        for side in range(2):
            keys_values = mixed[side].astype(BF16)
            for b in range(QUERY_BLOCKS):
                slot = (2 * pair + side) * QUERY_BLOCKS + b
                at = 32 * b
                two = jnp.where(low_s, lows[side][at : at + 16], highs[side][at + 16 : at + 32])
                out_ref[slot, :TOKENS] = keys_values
                out_ref[slot, TOKENS:] = two.astype(BF16)
    for slot in range(HEADS * QUERY_BLOCKS, ROW_DEVS):
        out_ref[slot] = jnp.zeros((SLOT, LANES), BF16)


def attend_kernel(x_ref, out_ref, keys_ref, ones_ref, query_ref, half_ref):
    low = iota((TOKENS, LANES), 1) < 64
    for r in range(ROW_DEVS):
        block = x_ref[r, :TOKENS]
        keys_ref[r * TOKENS : (r + 1) * TOKENS] = block
        ones_ref[r * TOKENS : (r + 1) * TOKENS] = jnp.where(low, jnp.ones_like(block), block)
        query_ref[r * 16 : (r + 1) * 16] = x_ref[r, TOKENS:].astype(F32)
    size = 256
    low_q = iota((size, LANES), 1) < 64
    factor = 0.125 * 1.4426950408889634
    for n in range(2):
        here = query_ref[n * size : (n + 1) * size]
        for side in range(2):
            turned = here if side == 0 else pltpu.roll(here, 64, 1)
            query = jnp.where(low_q, turned, 0.0).astype(BF16)
            scores = lax.dot_general(query, keys_ref[...], NT, preferred_element_type=F32)
            top = jnp.max(scores, axis=1, keepdims=True)
            weights = jnp.exp2((scores - top) * factor).astype(BF16)
            result = jnp.dot(weights, ones_ref[...], preferred_element_type=F32)
            other = pltpu.roll(result, 64, 1)
            if side == 0:
                half_ref[...] = other / result
            else:
                both = jnp.where(low_q, half_ref[...], result / other).astype(BF16)
                for r in range(size // 16):
                    out_ref[n * (size // 16) + r] = both[r * 16 : (r + 1) * 16]


def output_kernel(x_ref, resid_ref, w_ref, out_ref, wide_ref):
    low = iota((16, LANES), 1) < 64
    for pair in range(HEADS // 2):
        for b in range(QUERY_BLOCKS):
            first = x_ref[2 * pair * QUERY_BLOCKS + b].astype(F32)
            second = x_ref[(2 * pair + 1) * QUERY_BLOCKS + b].astype(F32)
            cols = slice(pair * LANES, (pair + 1) * LANES)
            at = 32 * b
            wide_ref[at : at + 16, cols] = jnp.where(low, first, pltpu.roll(second, 64, 1))
            wide_ref[at + 16 : at + 32, cols] = jnp.where(low, pltpu.roll(first, 64, 1), second)
    mixed = wide_ref[...].astype(BF16)
    product = jnp.dot(mixed, w_ref[...], preferred_element_type=F32)
    out_ref[...] = (resid_ref[...].astype(F32) + product).astype(BF16)


def exchange(values, axes):
    return lax.all_to_all(values, axes, split_axis=0, concat_axis=0, tiled=True)


def per_device(latent, ada_scale, ada_shift, conv_weight, qkv_weight, out_weight, ancestors):
    slab = latent.reshape(TOKENS, CHANS)
    particle = lax.axis_index(PART).astype(jnp.int32)
    place = jnp.stack([particle] + [lax.axis_index(a).astype(jnp.int32) for a in PART])

    swap = [(0, 1), (1, 0)]
    pair = jnp.stack([slab, lax.ppermute(slab, "z_lo", swap)])
    near = [pair] + [
        lax.ppermute(pair, "x", [((i + d) % 4, i) for i in range(4)]) for d in (1, 3, 2)
    ]
    slabs = near + [lax.ppermute(values, "core", swap) for values in near]

    picked = call(pick_kernel, shaped(ROW_DEVS, 64, LANES), [SMEM, VMEM, VMEM], 10**7, 10**6)(
        place, slab, conv_weight
    )
    picked = exchange(picked, ROWS)
    totals = call(total_kernel, shaped(PARTICLES, 8, LANES, dtype=F32), [VMEM], 10**5, 10**5)(picked)
    totals = exchange(totals, PART)
    weights = call(
        weights_kernel,
        shaped(3 * LANES, CHANS),
        [VMEM],
        10**6,
        10**6,
        scratch=(
            pltpu.VMEM((SLICE, 9 * CHANS + 2 * LANES), F32),
            pltpu.VMEM((3 * LANES, CHANS), F32),
        ),
    )(picked)

    scale, shift = ada_scale[None], ada_shift[None]
    edge = shaped(PARTICLES, WIDTH // 3, LANES, dtype=F32)
    up, down = call(edge_kernel, [edge, edge], [SMEM] + [VMEM] * 12, 10**8, 10**6)(
        place, totals, scale, shift, weights, *slabs
    )
    above = lax.ppermute(down, ROWS, [(i, i + 1) for i in range(ROW_DEVS - 1)])
    below = lax.ppermute(up, ROWS, [(i + 1, i) for i in range(ROW_DEVS - 1)])
    part = call(
        conv_kernel,
        shaped(PARTICLES, TOKENS, LANES, dtype=F32),
        [SMEM] + [VMEM] * 12,
        2 * 10**9,
        4 * 10**6,
        vmem=32,
    )(place, totals, scale, shift, weights, *slabs)
    pieces = call(
        finish_kernel, shaped(PARTICLES, 32, LANES), [SMEM, SMEM] + [VMEM] * 3, 10**6, 10**6
    )(place, ancestors, part, above, below)
    pieces = exchange(pieces, PART)

    resid, sums = call(
        gather_kernel,
        [shaped(TOKENS, CHANS), shaped(ROW_DEVS, 8, LANES, dtype=F32)],
        [VMEM],
        10**6,
        10**6,
        scratch=(pltpu.VMEM((TOKENS, CHANS), F32),),
    )(pieces)
    sums = exchange(sums, ROWS)
    slots = call(
        project_kernel,
        shaped(ROW_DEVS, SLOT, LANES),
        [VMEM] * 3,
        3 * 10**8,
        4 * 10**6,
        scratch=(pltpu.VMEM((TOKENS, 3 * CHANS), F32),),
    )(sums, resid, qkv_weight)
    slots = exchange(slots, ROWS)
    rows = ROW_DEVS * TOKENS
    mixed = call(
        attend_kernel,
        shaped(ROW_DEVS, 16, LANES),
        [VMEM],
        2 * 10**9,
        2 * 10**6,
        vmem=40,
        scratch=(
            pltpu.VMEM((rows, LANES), BF16),
            pltpu.VMEM((rows, LANES), BF16),
            pltpu.VMEM((ROW_DEVS * 16, LANES), F32),
            pltpu.VMEM((256, LANES), F32),
        ),
    )(slots)
    mixed = exchange(mixed, ROWS)
    block = call(
        output_kernel,
        shaped(TOKENS, CHANS),
        [VMEM] * 3,
        10**8,
        10**6,
        scratch=(pltpu.VMEM((TOKENS, CHANS), F32),),
    )(mixed, resid, out_weight)
    return block.reshape(1, ROWS_HERE, WIDTH, CHANS)


def solution(mesh):
    split = Mesh(mesh.devices.reshape(4, 2, 2, 4, 8), PART + ROWS)
    placed = (P(PART, ROWS, None, None), P(), P(), P(ROWS, None), P(), P(), P())
    return jax.shard_map(
        per_device,
        mesh=split,
        in_specs=placed,
        out_specs=P(PART, ROWS, None, None),
        check_vma=False,
    )
```

```python
import functools

import jax
import jax.numpy as jnp
from jax import lax
from jax.experimental import pallas as pl
from jax.experimental.pallas import tpu as pltpu
from jax.sharding import Mesh
from jax.sharding import PartitionSpec as P

HEADS = 10
GROUPS = 32
CHANS = 640
WIDTH = 24
ROWS_HERE = 4
TOKENS = ROWS_HERE * WIDTH
PARTICLES = 16
ROW_DEVS = 32
PER_GROUP = CHANS // GROUPS
SLICE = CHANS // PARTICLES
COUNT = ROWS_HERE * ROW_DEVS * WIDTH * PER_GROUP
LANES = 128
KERNEL_ROWS = 9 * CHANS // ROW_DEVS
TAIL = KERNEL_ROWS - LANES
QUERY_BLOCKS = 3
SLOT = TOKENS + 16

PART = ("x", "z_lo", "core")
ROWS = ("z_hi", "y")

NT = (((1,), (1,)), ((), ()))
F32 = jnp.float32
BF16 = jnp.bfloat16
SMEM = pl.BlockSpec(memory_space=pltpu.SMEM)
VMEM = pl.BlockSpec(memory_space=pltpu.VMEM)


def call(kernel, out_shape, in_specs, flops, size, vmem=16, scratch=()):
    out_specs = jax.tree.map(lambda _: VMEM, out_shape)
    return pl.pallas_call(
        kernel,
        out_shape=out_shape,
        in_specs=in_specs,
        out_specs=out_specs,
        scratch_shapes=list(scratch),
        compiler_params=pltpu.CompilerParams(vmem_limit_bytes=vmem * 1024 * 1024),
        cost_estimate=pl.CostEstimate(flops=flops, bytes_accessed=size, transcendentals=0),
    )


def shaped(*shape, dtype=BF16):
    return jax.ShapeDtypeStruct(shape, dtype)


def iota(shape, dim):
    return lax.broadcasted_iota(jnp.int32, shape, dim)


def exact_dot(a, b):
    return jnp.dot(a, b, precision=lax.Precision.HIGHEST, preferred_element_type=F32)


def group_row(values):
    sums = jnp.sum(values, axis=0, keepdims=True)
    squares = jnp.sum(values * values, axis=0, keepdims=True)
    chan, lane = iota((CHANS, LANES), 0), iota((CHANS, LANES), 1)
    first = ((chan >= lane * PER_GROUP) & (chan < (lane + 1) * PER_GROUP)).astype(F32)
    other = lane - GROUPS
    second = ((chan >= other * PER_GROUP) & (chan < (other + 1) * PER_GROUP)).astype(F32)
    eight = lambda row: jnp.broadcast_to(row, (8, CHANS))
    return exact_dot(eight(sums), first) + exact_dot(eight(squares), second)


def mean_and_inverse(totals):
    lane, chan = iota((LANES, CHANS), 0), iota((LANES, CHANS), 1)
    first = ((chan >= lane * PER_GROUP) & (chan < (lane + 1) * PER_GROUP)).astype(F32)
    other = lane - GROUPS
    second = ((chan >= other * PER_GROUP) & (chan < (other + 1) * PER_GROUP)).astype(F32)
    mean = exact_dot(totals, first) * (1.0 / COUNT)
    square = exact_dot(totals, second) * (1.0 / COUNT)
    return mean, lax.rsqrt(square - mean * mean + 1e-05)


def thirds(value):
    parts = []
    for _ in range(3):
        top = value.astype(BF16).astype(F32)
        parts.append(top)
        value = value - top
    return parts


def pick_kernel(place_ref, x_ref, w_ref, out_ref):
    row, col = iota((48, CHANS), 0), iota((48, CHANS), 1)
    chosen = ((col == row + place_ref[0] * SLICE) & (row < SLICE)).astype(F32).astype(BF16)
    picked = lax.dot_general(chosen, w_ref[...], NT, preferred_element_type=F32)
    head = picked[:, :LANES]
    rest = jnp.concatenate([picked[:, LANES:], jnp.zeros((48, LANES - TAIL), F32)], axis=1)
    turned = pltpu.roll(pltpu.roll(rest, 48 - 20, 0), 64, 1)
    sums = thirds(group_row(x_ref[...].astype(F32)))
    row, lane = iota((24, LANES), 0), iota((24, LANES), 1)
    low = jnp.where(lane < 64, rest[:24], turned[:24])
    for n in range(3):
        low = jnp.where(row == 20 + n, sums[n][:1], low)
    low = jnp.where(row == 23, 0.0, low)
    slot = jnp.concatenate([head[:SLICE], low], axis=0).astype(BF16)
    out_ref[...] = jnp.broadcast_to(slot[None], out_ref.shape)


def total_kernel(x_ref, out_ref):
    total = jnp.zeros((16, LANES), F32)
    for r in range(ROW_DEVS):
        total = total + x_ref[r, 48:64].astype(F32)
    row = total[12:13] + total[13:14] + total[14:15]
    out_ref[...] = jnp.broadcast_to(row[None], out_ref.shape)


PLACE = {1: 0, 0: 1, 2: 2}


def weights_kernel(x_ref, out_ref, flat_ref, tall_ref):
    flat_ref[...] = jnp.zeros_like(flat_ref)
    row, lane = iota((SLICE, LANES), 0), iota((SLICE, LANES), 1)
    for r in range(ROW_DEVS):
        at = r * KERNEL_ROWS
        block, off = at // LANES, at % LANES
        slot = x_ref[r].astype(F32)
        low = jnp.concatenate([slot[SLICE:], jnp.zeros((16, LANES), F32)], axis=0)
        rest = jnp.where(row < 20, low, pltpu.roll(pltpu.roll(low, 20, 0), 64, 1))
        rest = jnp.where(lane < TAIL, rest, 0.0)
        wide = jnp.concatenate([slot[:SLICE], rest, jnp.zeros((SLICE, LANES), F32)], axis=1)
        if off:
            wide = pltpu.roll(wide, off, 1)
        spot = slice(block * LANES, (block + 3) * LANES)
        flat_ref[:, spot] = flat_ref[:, spot] + wide
    tall_ref[...] = jnp.zeros_like(tall_ref)
    for a in range(3):
        for b in range(3):
            tap = 3 * a + b
            top = a * LANES + PLACE[b] * SLICE
            tall_ref[top : top + SLICE, :] = flat_ref[:, tap * CHANS : (tap + 1) * CHANS]
    out_ref[...] = tall_ref[...].astype(BF16)


STEPS = (0, 1, 3, 2)


def order(place_ref):
    x, z, core = place_ref[1], place_ref[2], place_ref[3]
    return [
        lax.rem(x + dx, 4) * 4 + lax.rem(z + dz, 2) * 2 + lax.rem(core + dc, 2)
        for dc in range(2)
        for dz in range(2)
        for dx in STEPS
    ]


def spot(place_ref, q):
    dx = lax.rem(q // 4 + 4 - place_ref[1], 4)
    dz = lax.rem(lax.rem(q // 2, 2) + place_ref[2], 2)
    dc = lax.rem(lax.rem(q, 2) + place_ref[3], 2)
    step = jnp.where(dx == 2, 3, jnp.where(dx == 3, 2, dx))
    return dc * 8 + dz * 4 + step


def gain_and_bias(place_ref, totals_ref, scale_ref, shift_ref):
    totals = jnp.concatenate([totals_ref[q, :1] for q in order(place_ref)], axis=0)
    mean, inverse = mean_and_inverse(totals)
    gain = inverse * (1.0 + scale_ref[...])
    return gain, shift_ref[...] - mean * gain


def silu(v):
    half = 0.5 * v
    return (half + half * jnp.tanh(half)).astype(BF16)


def across(full):
    rows = full.shape[0]
    at = lax.rem(iota((rows, LANES), 0), WIDTH)
    left = pltpu.roll(pltpu.roll(full, 1, 0), LANES - SLICE, 1)
    right = pltpu.roll(pltpu.roll(full, rows - 1, 0), LANES - 2 * SLICE, 1)
    total = full + jnp.where(at == 0, 0.0, left) + jnp.where(at == WIDTH - 1, 0.0, right)
    return jnp.where(iota((rows, LANES), 1) < SLICE, total, 0.0)


def packed(value):
    n = value.shape[0] // 3
    out = value[:n]
    for t in (1, 2):
        out = out + pltpu.roll(value[n * t : n * (t + 1)], SLICE * t, 1)
    return out


def unpacked(value):
    return jnp.concatenate(
        [value] + [pltpu.roll(value, LANES - SLICE * t, 1) for t in (1, 2)], axis=0
    )


def edge_kernel(place_ref, totals_ref, scale_ref, shift_ref, w_ref, *refs):
    slabs, (up_ref, down_ref) = refs[:4], refs[4:]
    gain, bias = gain_and_bias(place_ref, totals_ref, scale_ref, shift_ref)
    for rows, tap, ref in (
        (slice(0, WIDTH), 2, up_ref),
        (slice(TOKENS - WIDTH, TOKENS), 0, down_ref),
    ):
        active = []
        for q in range(PARTICLES):
            x = slabs[q // 4][q % 4].astype(F32)[rows]
            active.append(silu(x * gain[q : q + 1] + bias[q : q + 1]))
        active = jnp.concatenate(active, axis=0)
        weights = w_ref[tap * LANES : (tap + 1) * LANES, :]
        full = lax.dot_general(active, weights, NT, preferred_element_type=F32)
        full = across(full)
        for q in range(PARTICLES):
            ref[q] = packed(full[q * WIDTH : (q + 1) * WIDTH])


def conv_kernel(place_ref, totals_ref, scale_ref, shift_ref, w_ref, *refs):
    slabs, part_ref = refs[:4], refs[4]
    gain, bias = gain_and_bias(place_ref, totals_ref, scale_ref, shift_ref)
    row, col = iota((LANES, CHANS), 0), iota((LANES, CHANS), 1)
    chosen = ((col == row + place_ref[0] * SLICE) & (row < SLICE)).astype(F32).astype(BF16)
    weights = w_ref[...]
    each = 2
    last = TOKENS - WIDTH
    for step in range(PARTICLES // each):
        active, raw = [], []
        for q in range(step * each, (step + 1) * each):
            x = slabs[q // 4][q % 4]
            raw.append(x)
            active.append(silu(x.astype(F32) * gain[q : q + 1] + bias[q : q + 1]))
        active = jnp.concatenate(active, axis=0)
        raw = jnp.concatenate(raw, axis=0)
        taps = lax.dot_general(active, weights, NT, preferred_element_type=F32)
        field = lax.dot_general(raw, chosen, NT, preferred_element_type=F32)
        for k in range(each):
            rows = slice(k * TOKENS, (k + 1) * TOKENS)
            t0, t1, t2 = (taps[rows, n * LANES : (n + 1) * LANES] for n in range(3))
            base = t1 + field[rows]
            full = jnp.concatenate(
                [
                    base[:WIDTH] + t2[WIDTH : 2 * WIDTH],
                    base[WIDTH:last] + t0[: last - WIDTH] + t2[2 * WIDTH :],
                    base[last:] + t0[last - WIDTH : last],
                ],
                axis=0,
            )
            part_ref[step * each + k] = across(full)


def finish_kernel(place_ref, anc_ref, part_ref, above_ref, below_ref, out_ref):
    last = TOKENS - WIDTH
    lane = iota((TOKENS, LANES), 1)
    for p in range(PARTICLES):
        q = spot(place_ref, anc_ref[p])
        total = jnp.concatenate(
            [
                part_ref[q, :WIDTH] + unpacked(above_ref[q]),
                part_ref[q, WIDTH:last],
                part_ref[q, last:] + unpacked(below_ref[q]),
            ],
            axis=0,
        )
        out_ref[p] = packed(jnp.where(lane < SLICE, total, 0.0)).astype(BF16)


def gather_kernel(x_ref, resid_ref, out_ref, wide_ref):
    lane = iota((32, LANES), 1)
    for t in range(3):
        blocks = [jnp.zeros((32, LANES), F32) for _ in range(CHANS // LANES)]
        for p in range(PARTICLES):
            block, off = (p * SLICE) // LANES, (p * SLICE) % LANES
            turn = (off - t * SLICE) % LANES
            piece = x_ref[p].astype(F32)
            if turn:
                piece = pltpu.roll(piece, turn, 1)
            end = off + SLICE
            blocks[block] = jnp.where((lane >= off) & (lane < end), piece, blocks[block])
            if end > LANES:
                blocks[block + 1] = jnp.where(lane < end - LANES, piece, blocks[block + 1])
        for n, value in enumerate(blocks):
            wide_ref[32 * t : 32 * (t + 1), n * LANES : (n + 1) * LANES] = value
    wide = wide_ref[...]
    resid_ref[...] = wide.astype(BF16)
    out_ref[...] = jnp.broadcast_to(group_row(wide)[None], out_ref.shape)


def project_kernel(totals_ref, resid_ref, w_ref, out_ref, both_ref):
    mean, inverse = mean_and_inverse(jnp.sum(totals_ref[...], axis=0))
    normed = ((resid_ref[...].astype(F32) - mean[:1]) * inverse[:1]).astype(BF16)
    both_ref[...] = jnp.dot(normed, w_ref[...], preferred_element_type=F32)
    low = iota((TOKENS, LANES), 1) < 64
    low_s = iota((16, LANES), 1) < 64
    for pair in range(HEADS // 2):
        q, k, v = (
            both_ref[:, n * CHANS + pair * LANES : n * CHANS + (pair + 1) * LANES] for n in range(3)
        )
        q_turn, k_turn, v_turn = (pltpu.roll(x, 64, 1) for x in (q, k, v))
        mixed = (jnp.where(low, k, v_turn), jnp.where(low, k_turn, v))
        lows, highs = (q, q_turn), (q_turn, q)
        for side in range(2):
            keys_values = mixed[side].astype(BF16)
            for b in range(QUERY_BLOCKS):
                slot = (2 * pair + side) * QUERY_BLOCKS + b
                at = 32 * b
                two = jnp.where(low_s, lows[side][at : at + 16], highs[side][at + 16 : at + 32])
                out_ref[slot, :TOKENS] = keys_values
                out_ref[slot, TOKENS:] = two.astype(BF16)
    for slot in range(HEADS * QUERY_BLOCKS, ROW_DEVS):
        out_ref[slot] = jnp.zeros((SLOT, LANES), BF16)


def attend_kernel(x_ref, out_ref, keys_ref, ones_ref, query_ref, half_ref):
    low = iota((TOKENS, LANES), 1) < 64
    for r in range(ROW_DEVS):
        block = x_ref[r, :TOKENS]
        keys_ref[r * TOKENS : (r + 1) * TOKENS] = block
        ones_ref[r * TOKENS : (r + 1) * TOKENS] = jnp.where(low, jnp.ones_like(block), block)
        query_ref[r * 16 : (r + 1) * 16] = x_ref[r, TOKENS:].astype(F32)
    size = 256
    low_q = iota((size, LANES), 1) < 64
    factor = 0.125 * 1.4426950408889634
    for n in range(2):
        here = query_ref[n * size : (n + 1) * size]
        for side in range(2):
            turned = here if side == 0 else pltpu.roll(here, 64, 1)
            query = jnp.where(low_q, turned, 0.0).astype(BF16)
            scores = lax.dot_general(query, keys_ref[...], NT, preferred_element_type=F32)
            top = jnp.max(scores, axis=1, keepdims=True)
            weights = jnp.exp2((scores - top) * factor).astype(BF16)
            result = jnp.dot(weights, ones_ref[...], preferred_element_type=F32)
            other = pltpu.roll(result, 64, 1)
            if side == 0:
                half_ref[...] = other / result
            else:
                both = jnp.where(low_q, half_ref[...], result / other).astype(BF16)
                for r in range(size // 16):
                    out_ref[n * (size // 16) + r] = both[r * 16 : (r + 1) * 16]


def output_kernel(x_ref, resid_ref, w_ref, out_ref, wide_ref):
    low = iota((16, LANES), 1) < 64
    for pair in range(HEADS // 2):
        for b in range(QUERY_BLOCKS):
            first = x_ref[2 * pair * QUERY_BLOCKS + b].astype(F32)
            second = x_ref[(2 * pair + 1) * QUERY_BLOCKS + b].astype(F32)
            cols = slice(pair * LANES, (pair + 1) * LANES)
            at = 32 * b
            wide_ref[at : at + 16, cols] = jnp.where(low, first, pltpu.roll(second, 64, 1))
            wide_ref[at + 16 : at + 32, cols] = jnp.where(low, pltpu.roll(first, 64, 1), second)
    mixed = wide_ref[...].astype(BF16)
    product = jnp.dot(mixed, w_ref[...], preferred_element_type=F32)
    out_ref[...] = (resid_ref[...].astype(F32) + product).astype(BF16)


def exchange(values, axes):
    return lax.all_to_all(values, axes, split_axis=0, concat_axis=0, tiled=True)


def per_device(latent, ada_scale, ada_shift, conv_weight, qkv_weight, out_weight, ancestors):
    slab = latent.reshape(TOKENS, CHANS)
    particle = lax.axis_index(PART).astype(jnp.int32)
    place = jnp.stack([particle] + [lax.axis_index(a).astype(jnp.int32) for a in PART])

    swap = [(0, 1), (1, 0)]
    along = [slab] + [
        lax.ppermute(slab, "x", [((i + d) % 4, i) for i in range(4)]) for d in STEPS[1:]
    ]
    four = jnp.stack(along)
    eight = [four, lax.ppermute(four, "z_lo", swap)]
    slabs = eight + [lax.ppermute(values, "core", swap) for values in eight]

    picked = call(pick_kernel, shaped(ROW_DEVS, 64, LANES), [SMEM, VMEM, VMEM], 10**7, 10**6)(
        place, slab, conv_weight
    )
    picked = exchange(picked, ROWS)
    totals = call(total_kernel, shaped(PARTICLES, 8, LANES, dtype=F32), [VMEM], 10**5, 10**5)(picked)
    totals = exchange(totals, PART)
    weights = call(
        weights_kernel,
        shaped(3 * LANES, CHANS),
        [VMEM],
        10**6,
        10**6,
        scratch=(
            pltpu.VMEM((SLICE, 9 * CHANS + 2 * LANES), F32),
            pltpu.VMEM((3 * LANES, CHANS), F32),
        ),
    )(picked)

    scale, shift = ada_scale[None], ada_shift[None]
    edge = shaped(PARTICLES, WIDTH // 3, LANES, dtype=F32)
    up, down = call(edge_kernel, [edge, edge], [SMEM] + [VMEM] * 8, 10**8, 10**6)(
        place, totals, scale, shift, weights, *slabs
    )
    above = lax.ppermute(down, ROWS, [(i, i + 1) for i in range(ROW_DEVS - 1)])
    below = lax.ppermute(up, ROWS, [(i + 1, i) for i in range(ROW_DEVS - 1)])
    part = call(
        conv_kernel,
        shaped(PARTICLES, TOKENS, LANES, dtype=F32),
        [SMEM] + [VMEM] * 8,
        2 * 10**9,
        4 * 10**6,
        vmem=32,
    )(place, totals, scale, shift, weights, *slabs)
    pieces = call(
        finish_kernel, shaped(PARTICLES, 32, LANES), [SMEM, SMEM] + [VMEM] * 3, 10**6, 10**6
    )(place, ancestors, part, above, below)
    pieces = exchange(pieces, PART)

    resid, sums = call(
        gather_kernel,
        [shaped(TOKENS, CHANS), shaped(ROW_DEVS, 8, LANES, dtype=F32)],
        [VMEM],
        10**6,
        10**6,
        scratch=(pltpu.VMEM((TOKENS, CHANS), F32),),
    )(pieces)
    sums = exchange(sums, ROWS)
    slots = call(
        project_kernel,
        shaped(ROW_DEVS, SLOT, LANES),
        [VMEM] * 3,
        3 * 10**8,
        4 * 10**6,
        scratch=(pltpu.VMEM((TOKENS, 3 * CHANS), F32),),
    )(sums, resid, qkv_weight)
    slots = exchange(slots, ROWS)
    rows = ROW_DEVS * TOKENS
    mixed = call(
        attend_kernel,
        shaped(ROW_DEVS, 16, LANES),
        [VMEM],
        2 * 10**9,
        2 * 10**6,
        vmem=40,
        scratch=(
            pltpu.VMEM((rows, LANES), BF16),
            pltpu.VMEM((rows, LANES), BF16),
            pltpu.VMEM((ROW_DEVS * 16, LANES), F32),
            pltpu.VMEM((256, LANES), F32),
        ),
    )(slots)
    mixed = exchange(mixed, ROWS)
    block = call(
        output_kernel,
        shaped(TOKENS, CHANS),
        [VMEM] * 3,
        10**8,
        10**6,
        scratch=(pltpu.VMEM((TOKENS, CHANS), F32),),
    )(mixed, resid, out_weight)
    return block.reshape(1, ROWS_HERE, WIDTH, CHANS)


def solution(mesh):
    split = Mesh(mesh.devices.reshape(4, 2, 2, 4, 8), PART + ROWS)
    placed = (P(PART, ROWS, None, None), P(), P(), P(ROWS, None), P(), P(), P())
    return jax.shard_map(
        per_device,
        mesh=split,
        in_specs=placed,
        out_specs=P(PART, ROWS, None, None),
        check_vma=False,
    )
```

```python
import functools

import jax
import jax.numpy as jnp
from jax import lax
from jax.experimental import pallas as pl
from jax.experimental.pallas import tpu as pltpu
from jax.sharding import Mesh
from jax.sharding import PartitionSpec as P

HEADS = 10
GROUPS = 32
CHANS = 640
WIDTH = 24
ROWS_HERE = 4
TOKENS = ROWS_HERE * WIDTH
PARTICLES = 16
ROW_DEVS = 32
PER_GROUP = CHANS // GROUPS
SLICE = CHANS // PARTICLES
COUNT = ROWS_HERE * ROW_DEVS * WIDTH * PER_GROUP
LANES = 128
KERNEL_ROWS = 9 * CHANS // ROW_DEVS
TAIL = KERNEL_ROWS - LANES
QUERY_BLOCKS = 3
SLOT = TOKENS + 16

PART = ("x", "z_lo", "core")
ROWS = ("z_hi", "y")

NT = (((1,), (1,)), ((), ()))
F32 = jnp.float32
BF16 = jnp.bfloat16
SMEM = pl.BlockSpec(memory_space=pltpu.SMEM)
VMEM = pl.BlockSpec(memory_space=pltpu.VMEM)
ANY = pl.BlockSpec(memory_space=pl.ANY)


def call(kernel, out_shape, in_specs, flops, size, vmem=16, scratch=()):
    out_specs = jax.tree.map(lambda _: VMEM, out_shape)
    return pl.pallas_call(
        kernel,
        out_shape=out_shape,
        in_specs=in_specs,
        out_specs=out_specs,
        scratch_shapes=list(scratch),
        compiler_params=pltpu.CompilerParams(vmem_limit_bytes=vmem * 1024 * 1024),
        cost_estimate=pl.CostEstimate(flops=flops, bytes_accessed=size, transcendentals=0),
    )


def shaped(*shape, dtype=BF16):
    return jax.ShapeDtypeStruct(shape, dtype)


def iota(shape, dim):
    return lax.broadcasted_iota(jnp.int32, shape, dim)


def exact_dot(a, b):
    return jnp.dot(a, b, precision=lax.Precision.HIGHEST, preferred_element_type=F32)


def group_row(values):
    sums = jnp.sum(values, axis=0, keepdims=True)
    squares = jnp.sum(values * values, axis=0, keepdims=True)
    chan, lane = iota((CHANS, LANES), 0), iota((CHANS, LANES), 1)
    first = ((chan >= lane * PER_GROUP) & (chan < (lane + 1) * PER_GROUP)).astype(F32)
    other = lane - GROUPS
    second = ((chan >= other * PER_GROUP) & (chan < (other + 1) * PER_GROUP)).astype(F32)
    eight = lambda row: jnp.broadcast_to(row, (8, CHANS))
    return exact_dot(eight(sums), first) + exact_dot(eight(squares), second)


def mean_and_inverse(totals):
    lane, chan = iota((LANES, CHANS), 0), iota((LANES, CHANS), 1)
    first = ((chan >= lane * PER_GROUP) & (chan < (lane + 1) * PER_GROUP)).astype(F32)
    other = lane - GROUPS
    second = ((chan >= other * PER_GROUP) & (chan < (other + 1) * PER_GROUP)).astype(F32)
    mean = exact_dot(totals, first) * (1.0 / COUNT)
    square = exact_dot(totals, second) * (1.0 / COUNT)
    return mean, lax.rsqrt(square - mean * mean + 1e-05)


def thirds(value):
    parts = []
    for _ in range(3):
        top = value.astype(BF16).astype(F32)
        parts.append(top)
        value = value - top
    return parts


def pick_kernel(place_ref, x_ref, w_ref, _, out_ref):
    row, col = iota((48, CHANS), 0), iota((48, CHANS), 1)
    chosen = ((col == row + place_ref[0] * SLICE) & (row < SLICE)).astype(F32).astype(BF16)
    picked = lax.dot_general(chosen, w_ref[...], NT, preferred_element_type=F32)
    head = picked[:, :LANES]
    rest = jnp.concatenate([picked[:, LANES:], jnp.zeros((48, LANES - TAIL), F32)], axis=1)
    turned = pltpu.roll(pltpu.roll(rest, 48 - 20, 0), 64, 1)
    sums = thirds(group_row(x_ref[...].astype(F32)))
    row, lane = iota((24, LANES), 0), iota((24, LANES), 1)
    low = jnp.where(lane < 64, rest[:24], turned[:24])
    for n in range(3):
        low = jnp.where(row == 20 + n, sums[n][:1], low)
    low = jnp.where(row == 23, 0.0, low)
    slot = jnp.concatenate([head[:SLICE], low], axis=0).astype(BF16)
    out_ref[...] = jnp.broadcast_to(slot[None], out_ref.shape)


def total_kernel(x_ref, out_ref):
    total = jnp.zeros((16, LANES), F32)
    for r in range(ROW_DEVS):
        total = total + x_ref[r, 48:64].astype(F32)
    row = total[12:13] + total[13:14] + total[14:15]
    out_ref[...] = jnp.broadcast_to(row[None], out_ref.shape)


PLACE = {1: 0, 0: 1, 2: 2}


def weights_kernel(x_ref, out_ref, flat_ref, tall_ref):
    flat_ref[...] = jnp.zeros_like(flat_ref)
    row, lane = iota((SLICE, LANES), 0), iota((SLICE, LANES), 1)
    for r in range(ROW_DEVS):
        at = r * KERNEL_ROWS
        block, off = at // LANES, at % LANES
        slot = x_ref[r].astype(F32)
        low = jnp.concatenate([slot[SLICE:], jnp.zeros((16, LANES), F32)], axis=0)
        rest = jnp.where(row < 20, low, pltpu.roll(pltpu.roll(low, 20, 0), 64, 1))
        rest = jnp.where(lane < TAIL, rest, 0.0)
        wide = jnp.concatenate([slot[:SLICE], rest, jnp.zeros((SLICE, LANES), F32)], axis=1)
        if off:
            wide = pltpu.roll(wide, off, 1)
        spot = slice(block * LANES, (block + 3) * LANES)
        flat_ref[:, spot] = flat_ref[:, spot] + wide
    tall_ref[...] = jnp.zeros_like(tall_ref)
    for a in range(3):
        for b in range(3):
            tap = 3 * a + b
            top = a * LANES + PLACE[b] * SLICE
            tall_ref[top : top + SLICE, :] = flat_ref[:, tap * CHANS : (tap + 1) * CHANS]
    out_ref[...] = tall_ref[...].astype(BF16)


STEPS = (0, 1, 3, 2)


def order(place_ref):
    x, z, core = place_ref[1], place_ref[2], place_ref[3]
    return [
        lax.rem(x + dx, 4) * 4 + lax.rem(z + dz, 2) * 2 + lax.rem(core + dc, 2)
        for dc in range(2)
        for dz in range(2)
        for dx in STEPS
    ]


def spot(place_ref, q):
    dx = lax.rem(q // 4 + 4 - place_ref[1], 4)
    dz = lax.rem(lax.rem(q // 2, 2) + place_ref[2], 2)
    dc = lax.rem(lax.rem(q, 2) + place_ref[3], 2)
    step = jnp.where(dx == 2, 3, jnp.where(dx == 3, 2, dx))
    return dc * 8 + dz * 4 + step


def gain_and_bias(place_ref, totals_ref, scale_ref, shift_ref):
    totals = jnp.concatenate([totals_ref[q, :1] for q in order(place_ref)], axis=0)
    mean, inverse = mean_and_inverse(totals)
    gain = inverse * (1.0 + scale_ref[...])
    return gain, shift_ref[...] - mean * gain


def silu(v):
    half = 0.5 * v
    return (half + half * jnp.tanh(half)).astype(BF16)


def across(full):
    rows = full.shape[0]
    at = lax.rem(iota((rows, LANES), 0), WIDTH)
    left = pltpu.roll(pltpu.roll(full, 1, 0), LANES - SLICE, 1)
    right = pltpu.roll(pltpu.roll(full, rows - 1, 0), LANES - 2 * SLICE, 1)
    total = full + jnp.where(at == 0, 0.0, left) + jnp.where(at == WIDTH - 1, 0.0, right)
    return jnp.where(iota((rows, LANES), 1) < SLICE, total, 0.0)


def packed(value):
    n = value.shape[0] // 3
    out = value[:n]
    for t in (1, 2):
        out = out + pltpu.roll(value[n * t : n * (t + 1)], SLICE * t, 1)
    return out


def unpacked(value):
    return jnp.concatenate(
        [value] + [pltpu.roll(value, LANES - SLICE * t, 1) for t in (1, 2)], axis=0
    )


def edge_kernel(place_ref, totals_ref, scale_ref, shift_ref, w_ref, *refs):
    slabs, (up_ref, down_ref) = refs[:4], refs[4:]
    gain, bias = gain_and_bias(place_ref, totals_ref, scale_ref, shift_ref)
    for rows, tap, ref in (
        (slice(0, WIDTH), 2, up_ref),
        (slice(TOKENS - WIDTH, TOKENS), 0, down_ref),
    ):
        active = []
        for q in range(PARTICLES):
            x = slabs[q // 4][q % 4].astype(F32)[rows]
            active.append(silu(x * gain[q : q + 1] + bias[q : q + 1]))
        active = jnp.concatenate(active, axis=0)
        weights = w_ref[tap * LANES : (tap + 1) * LANES, :]
        full = lax.dot_general(active, weights, NT, preferred_element_type=F32)
        full = across(full)
        for q in range(PARTICLES):
            ref[q] = packed(full[q * WIDTH : (q + 1) * WIDTH])


def conv_kernel(place_ref, totals_ref, scale_ref, shift_ref, w_ref, *refs):
    slabs, part_ref = refs[:4], refs[4]
    gain, bias = gain_and_bias(place_ref, totals_ref, scale_ref, shift_ref)
    row, col = iota((LANES, CHANS), 0), iota((LANES, CHANS), 1)
    chosen = ((col == row + place_ref[0] * SLICE) & (row < SLICE)).astype(F32).astype(BF16)
    weights = w_ref[...]
    each = 2
    last = TOKENS - WIDTH
    for step in range(PARTICLES // each):
        active, raw = [], []
        for q in range(step * each, (step + 1) * each):
            x = slabs[q // 4][q % 4]
            raw.append(x)
            active.append(silu(x.astype(F32) * gain[q : q + 1] + bias[q : q + 1]))
        active = jnp.concatenate(active, axis=0)
        raw = jnp.concatenate(raw, axis=0)
        taps = lax.dot_general(active, weights, NT, preferred_element_type=F32)
        field = lax.dot_general(raw, chosen, NT, preferred_element_type=F32)
        for k in range(each):
            rows = slice(k * TOKENS, (k + 1) * TOKENS)
            t0, t1, t2 = (taps[rows, n * LANES : (n + 1) * LANES] for n in range(3))
            base = t1 + field[rows]
            full = jnp.concatenate(
                [
                    base[:WIDTH] + t2[WIDTH : 2 * WIDTH],
                    base[WIDTH:last] + t0[: last - WIDTH] + t2[2 * WIDTH :],
                    base[last:] + t0[last - WIDTH : last],
                ],
                axis=0,
            )
            part_ref[step * each + k] = across(full)


def finish_kernel(place_ref, anc_ref, part_ref, above_ref, below_ref, out_ref):
    last = TOKENS - WIDTH
    lane = iota((TOKENS, LANES), 1)
    for p in range(PARTICLES):
        q = spot(place_ref, anc_ref[p])
        total = jnp.concatenate(
            [
                part_ref[q, :WIDTH] + unpacked(above_ref[q]),
                part_ref[q, WIDTH:last],
                part_ref[q, last:] + unpacked(below_ref[q]),
            ],
            axis=0,
        )
        out_ref[p] = packed(jnp.where(lane < SLICE, total, 0.0)).astype(BF16)


def gather_kernel(x_ref, resid_ref, out_ref, wide_ref):
    lane = iota((32, LANES), 1)
    for t in range(3):
        blocks = [jnp.zeros((32, LANES), F32) for _ in range(CHANS // LANES)]
        for p in range(PARTICLES):
            block, off = (p * SLICE) // LANES, (p * SLICE) % LANES
            turn = (off - t * SLICE) % LANES
            piece = x_ref[p].astype(F32)
            if turn:
                piece = pltpu.roll(piece, turn, 1)
            end = off + SLICE
            blocks[block] = jnp.where((lane >= off) & (lane < end), piece, blocks[block])
            if end > LANES:
                blocks[block + 1] = jnp.where(lane < end - LANES, piece, blocks[block + 1])
        for n, value in enumerate(blocks):
            wide_ref[32 * t : 32 * (t + 1), n * LANES : (n + 1) * LANES] = value
    wide = wide_ref[...]
    resid_ref[...] = wide.astype(BF16)
    out_ref[...] = jnp.broadcast_to(group_row(wide)[None], out_ref.shape)


def project_kernel(totals_ref, resid_ref, w_ref, out_ref, both_ref):
    mean, inverse = mean_and_inverse(jnp.sum(totals_ref[...], axis=0))
    normed = ((resid_ref[...].astype(F32) - mean[:1]) * inverse[:1]).astype(BF16)
    both_ref[...] = jnp.dot(normed, w_ref[...], preferred_element_type=F32)
    low = iota((TOKENS, LANES), 1) < 64
    low_s = iota((16, LANES), 1) < 64
    for pair in range(HEADS // 2):
        q, k, v = (
            both_ref[:, n * CHANS + pair * LANES : n * CHANS + (pair + 1) * LANES] for n in range(3)
        )
        q_turn, k_turn, v_turn = (pltpu.roll(x, 64, 1) for x in (q, k, v))
        mixed = (jnp.where(low, k, v_turn), jnp.where(low, k_turn, v))
        lows, highs = (q, q_turn), (q_turn, q)
        for side in range(2):
            keys_values = mixed[side].astype(BF16)
            for b in range(QUERY_BLOCKS):
                slot = (2 * pair + side) * QUERY_BLOCKS + b
                at = 32 * b
                two = jnp.where(low_s, lows[side][at : at + 16], highs[side][at + 16 : at + 32])
                out_ref[slot, :TOKENS] = keys_values
                out_ref[slot, TOKENS:] = two.astype(BF16)
    for slot in range(HEADS * QUERY_BLOCKS, ROW_DEVS):
        out_ref[slot] = jnp.zeros((SLOT, LANES), BF16)


def attend_kernel(x_ref, out_ref, keys_ref, ones_ref, query_ref, half_ref):
    low = iota((TOKENS, LANES), 1) < 64
    for r in range(ROW_DEVS):
        block = x_ref[r, :TOKENS]
        keys_ref[r * TOKENS : (r + 1) * TOKENS] = block
        ones_ref[r * TOKENS : (r + 1) * TOKENS] = jnp.where(low, jnp.ones_like(block), block)
        query_ref[r * 16 : (r + 1) * 16] = x_ref[r, TOKENS:].astype(F32)
    size = 256
    low_q = iota((size, LANES), 1) < 64
    factor = 0.125 * 1.4426950408889634
    for n in range(2):
        here = query_ref[n * size : (n + 1) * size]
        for side in range(2):
            turned = here if side == 0 else pltpu.roll(here, 64, 1)
            query = jnp.where(low_q, turned, 0.0).astype(BF16)
            scores = lax.dot_general(query, keys_ref[...], NT, preferred_element_type=F32)
            top = jnp.max(scores, axis=1, keepdims=True)
            weights = jnp.exp2((scores - top) * factor).astype(BF16)
            result = jnp.dot(weights, ones_ref[...], preferred_element_type=F32)
            other = pltpu.roll(result, 64, 1)
            if side == 0:
                half_ref[...] = other / result
            else:
                both = jnp.where(low_q, half_ref[...], result / other).astype(BF16)
                for r in range(size // 16):
                    out_ref[n * (size // 16) + r] = both[r * 16 : (r + 1) * 16]


def output_kernel(x_ref, resid_ref, w_ref, out_ref, wide_ref):
    low = iota((16, LANES), 1) < 64
    for pair in range(HEADS // 2):
        for b in range(QUERY_BLOCKS):
            first = x_ref[2 * pair * QUERY_BLOCKS + b].astype(F32)
            second = x_ref[(2 * pair + 1) * QUERY_BLOCKS + b].astype(F32)
            cols = slice(pair * LANES, (pair + 1) * LANES)
            at = 32 * b
            wide_ref[at : at + 16, cols] = jnp.where(low, first, pltpu.roll(second, 64, 1))
            wide_ref[at + 16 : at + 32, cols] = jnp.where(low, pltpu.roll(first, 64, 1), second)
    mixed = wide_ref[...].astype(BF16)
    product = jnp.dot(mixed, w_ref[...], preferred_element_type=F32)
    out_ref[...] = (resid_ref[...].astype(F32) + product).astype(BF16)


def exchange(values, axes):
    return lax.all_to_all(values, axes, split_axis=0, concat_axis=0, tiled=True)


def per_device(latent, ada_scale, ada_shift, conv_weight, qkv_weight, out_weight, ancestors):
    slab = latent.reshape(TOKENS, CHANS)
    particle = lax.axis_index(PART).astype(jnp.int32)
    place = jnp.stack([particle] + [lax.axis_index(a).astype(jnp.int32) for a in PART])

    swap = [(0, 1), (1, 0)]
    opposite = lax.ppermute(slab, "z_lo", swap)

    def along(values):
        turns = [[((i + d) % 4, i) for i in range(4)] for d in STEPS[1:]]
        return jnp.stack([values] + [lax.ppermute(values, "x", turn) for turn in turns])

    eight = [along(slab), along(opposite)]
    slabs = eight + [lax.ppermute(values, "core", swap) for values in eight]

    picked = call(pick_kernel, shaped(ROW_DEVS, 64, LANES), [SMEM, VMEM, VMEM, ANY], 10**7, 10**6)(
        place, slab, conv_weight, opposite
    )
    picked = exchange(picked, ROWS)
    totals = call(total_kernel, shaped(PARTICLES, 8, LANES, dtype=F32), [VMEM], 10**5, 10**5)(picked)
    totals = exchange(totals, PART)
    weights = call(
        weights_kernel,
        shaped(3 * LANES, CHANS),
        [VMEM],
        10**6,
        10**6,
        scratch=(
            pltpu.VMEM((SLICE, 9 * CHANS + 2 * LANES), F32),
            pltpu.VMEM((3 * LANES, CHANS), F32),
        ),
    )(picked)

    scale, shift = ada_scale[None], ada_shift[None]
    edge = shaped(PARTICLES, WIDTH // 3, LANES, dtype=F32)
    up, down = call(edge_kernel, [edge, edge], [SMEM] + [VMEM] * 8, 10**8, 10**6)(
        place, totals, scale, shift, weights, *slabs
    )
    above = lax.ppermute(down, ROWS, [(i, i + 1) for i in range(ROW_DEVS - 1)])
    below = lax.ppermute(up, ROWS, [(i + 1, i) for i in range(ROW_DEVS - 1)])
    part = call(
        conv_kernel,
        shaped(PARTICLES, TOKENS, LANES, dtype=F32),
        [SMEM] + [VMEM] * 8,
        2 * 10**9,
        4 * 10**6,
        vmem=32,
    )(place, totals, scale, shift, weights, *slabs)
    pieces = call(
        finish_kernel, shaped(PARTICLES, 32, LANES), [SMEM, SMEM] + [VMEM] * 3, 10**6, 10**6
    )(place, ancestors, part, above, below)
    pieces = exchange(pieces, PART)

    resid, sums = call(
        gather_kernel,
        [shaped(TOKENS, CHANS), shaped(ROW_DEVS, 8, LANES, dtype=F32)],
        [VMEM],
        10**6,
        10**6,
        scratch=(pltpu.VMEM((TOKENS, CHANS), F32),),
    )(pieces)
    sums = exchange(sums, ROWS)
    slots = call(
        project_kernel,
        shaped(ROW_DEVS, SLOT, LANES),
        [VMEM] * 3,
        3 * 10**8,
        4 * 10**6,
        scratch=(pltpu.VMEM((TOKENS, 3 * CHANS), F32),),
    )(sums, resid, qkv_weight)
    slots = exchange(slots, ROWS)
    rows = ROW_DEVS * TOKENS
    mixed = call(
        attend_kernel,
        shaped(ROW_DEVS, 16, LANES),
        [VMEM],
        2 * 10**9,
        2 * 10**6,
        vmem=40,
        scratch=(
            pltpu.VMEM((rows, LANES), BF16),
            pltpu.VMEM((rows, LANES), BF16),
            pltpu.VMEM((ROW_DEVS * 16, LANES), F32),
            pltpu.VMEM((256, LANES), F32),
        ),
    )(slots)
    mixed = exchange(mixed, ROWS)
    block = call(
        output_kernel,
        shaped(TOKENS, CHANS),
        [VMEM] * 3,
        10**8,
        10**6,
        scratch=(pltpu.VMEM((TOKENS, CHANS), F32),),
    )(mixed, resid, out_weight)
    return block.reshape(1, ROWS_HERE, WIDTH, CHANS)


def solution(mesh):
    split = Mesh(mesh.devices.reshape(4, 2, 2, 4, 8), PART + ROWS)
    placed = (P(PART, ROWS, None, None), P(), P(), P(ROWS, None), P(), P(), P())
    return jax.shard_map(
        per_device,
        mesh=split,
        in_specs=placed,
        out_specs=P(PART, ROWS, None, None),
        check_vma=False,
    )
```

```python
import jax
import jax.numpy as jnp
from jax import lax
from jax.experimental import pallas as pl
from jax.experimental.pallas import tpu as pltpu
from jax.sharding import Mesh
from jax.sharding import PartitionSpec as P

HEADS = 10
GROUPS = 32
CHANS = 640
WIDTH = 24
ROWS_HERE = 4
TOKENS = ROWS_HERE * WIDTH
LAST = TOKENS - WIDTH
PARTICLES = 16
HALF = PARTICLES // 2
ROW_DEVS = 32
PER_GROUP = CHANS // GROUPS
SLICE = CHANS // PARTICLES
COUNT = ROWS_HERE * ROW_DEVS * WIDTH * PER_GROUP
LANES = 128
KERNEL_ROWS = 9 * CHANS // ROW_DEVS
TAIL = KERNEL_ROWS - LANES
QUERY_BLOCKS = 3
SLOT = TOKENS + 16

PART = ("x", "z_lo", "core")
CHIPS = ("x", "z_lo")
ROWS = ("z_hi", "y")

NT = (((1,), (1,)), ((), ()))
F32 = jnp.float32
BF16 = jnp.bfloat16
SMEM = pl.BlockSpec(memory_space=pltpu.SMEM)
VMEM = pl.BlockSpec(memory_space=pltpu.VMEM)


def call(kernel, out_shape, in_specs, flops, size, vmem=16, scratch=()):
    out_specs = jax.tree.map(lambda _: VMEM, out_shape)
    return pl.pallas_call(
        kernel,
        out_shape=out_shape,
        in_specs=in_specs,
        out_specs=out_specs,
        scratch_shapes=list(scratch),
        compiler_params=pltpu.CompilerParams(vmem_limit_bytes=vmem * 1024 * 1024),
        cost_estimate=pl.CostEstimate(flops=flops, bytes_accessed=size, transcendentals=0),
    )


def shaped(*shape, dtype=BF16):
    return jax.ShapeDtypeStruct(shape, dtype)


def iota(shape, dim):
    return lax.broadcasted_iota(jnp.int32, shape, dim)


def exact_dot(a, b):
    return jnp.dot(a, b, precision=lax.Precision.HIGHEST, preferred_element_type=F32)


def group_rows(values):
    fill = [jnp.zeros((1, CHANS), F32)] * (8 - len(values))
    sums = jnp.concatenate([jnp.sum(v, axis=0, keepdims=True) for v in values] + fill, axis=0)
    squares = [jnp.sum(v * v, axis=0, keepdims=True) for v in values] + fill
    squares = jnp.concatenate(squares, axis=0)
    chan, lane = iota((CHANS, LANES), 0), iota((CHANS, LANES), 1)
    first = ((chan >= lane * PER_GROUP) & (chan < (lane + 1) * PER_GROUP)).astype(F32)
    other = lane - GROUPS
    second = ((chan >= other * PER_GROUP) & (chan < (other + 1) * PER_GROUP)).astype(F32)
    return exact_dot(sums, first) + exact_dot(squares, second)


def mean_and_inverse(totals):
    lane, chan = iota((LANES, CHANS), 0), iota((LANES, CHANS), 1)
    first = ((chan >= lane * PER_GROUP) & (chan < (lane + 1) * PER_GROUP)).astype(F32)
    other = lane - GROUPS
    second = ((chan >= other * PER_GROUP) & (chan < (other + 1) * PER_GROUP)).astype(F32)
    mean = exact_dot(totals, first) * (1.0 / COUNT)
    square = exact_dot(totals, second) * (1.0 / COUNT)
    return mean, lax.rsqrt(square - mean * mean + 1e-05)


def thirds(value):
    parts = []
    for _ in range(3):
        top = value.astype(BF16).astype(F32)
        parts.append(top)
        value = value - top
    return parts


def pick_kernel(place_ref, x_ref, w_ref, out_ref):
    row, col = iota((48, CHANS), 0), iota((48, CHANS), 1)
    chosen = ((col == row + place_ref[0] * SLICE) & (row < SLICE)).astype(F32).astype(BF16)
    picked = lax.dot_general(chosen, w_ref[...], NT, preferred_element_type=F32)
    head = picked[:, :LANES]
    rest = jnp.concatenate([picked[:, LANES:], jnp.zeros((48, LANES - TAIL), F32)], axis=1)
    turned = pltpu.roll(pltpu.roll(rest, 48 - 20, 0), 64, 1)
    low = jnp.where(iota((24, LANES), 1) < 64, rest[:24], turned[:24])
    values = [x_ref[j].astype(F32) for j in range(HALF)]
    first, second, third = thirds(group_rows(values))
    sums = jnp.concatenate([first + pltpu.roll(second, 64, 1), third], axis=0)
    slot = jnp.concatenate([head[:SLICE], low, sums], axis=0).astype(BF16)
    out_ref[...] = jnp.broadcast_to(slot[None], out_ref.shape)


def total_kernel(x_ref, out_ref):
    total = jnp.zeros((16, LANES), F32)
    for r in range(ROW_DEVS):
        total = total + x_ref[r, 64:80].astype(F32)
    total = total[:8] + pltpu.roll(total[:8], 64, 1) + total[8:]
    out_ref[...] = jnp.where(iota((HALF, LANES), 1) < 64, total, 0.0)


PLACE = {1: 0, 0: 1, 2: 2}


def weights_kernel(x_ref, out_ref, flat_ref, tall_ref):
    flat_ref[...] = jnp.zeros_like(flat_ref)
    row, lane = iota((SLICE, LANES), 0), iota((SLICE, LANES), 1)
    for r in range(ROW_DEVS):
        at = r * KERNEL_ROWS
        block, off = at // LANES, at % LANES
        slot = x_ref[r].astype(F32)
        low = jnp.concatenate([slot[SLICE:64], jnp.zeros((16, LANES), F32)], axis=0)
        rest = jnp.where(row < 20, low, pltpu.roll(pltpu.roll(low, 20, 0), 64, 1))
        rest = jnp.where(lane < TAIL, rest, 0.0)
        wide = jnp.concatenate([slot[:SLICE], rest, jnp.zeros((SLICE, LANES), F32)], axis=1)
        if off:
            wide = pltpu.roll(wide, off, 1)
        spot = slice(block * LANES, (block + 3) * LANES)
        flat_ref[:, spot] = flat_ref[:, spot] + wide
    tall_ref[...] = jnp.zeros_like(tall_ref)
    for a in range(3):
        for b in range(3):
            tap = 3 * a + b
            top = a * LANES + PLACE[b] * SLICE
            tall_ref[top : top + SLICE, :] = flat_ref[:, tap * CHANS : (tap + 1) * CHANS]
    out_ref[...] = tall_ref[...].astype(BF16)


def spot(place_ref, q):
    return lax.rem(lax.rem(q, 2) + place_ref[1], 2) * HALF + q // 2


def silu(v):
    half = 0.5 * v
    return half + half * jnp.tanh(half)


def across(full):
    rows = full.shape[0]
    at = lax.rem(iota((rows, LANES), 0), WIDTH)
    left = pltpu.roll(pltpu.roll(full, 1, 0), LANES - SLICE, 1)
    right = pltpu.roll(pltpu.roll(full, rows - 1, 0), LANES - 2 * SLICE, 1)
    total = full + jnp.where(at == 0, 0.0, left) + jnp.where(at == WIDTH - 1, 0.0, right)
    return jnp.where(iota((rows, LANES), 1) < SLICE, total, 0.0)


def packed(value):
    n = value.shape[0] // 3
    out = value[:n]
    for t in (1, 2):
        out = out + pltpu.roll(value[n * t : n * (t + 1)], SLICE * t, 1)
    return out


def conv_kernel(place_ref, anc_ref, scale_ref, shift_ref, w_ref, *refs):
    totals, slabs, edges, (out_ref, done_ref) = refs[:2], refs[2:4], refs[4:6], refs[6:]
    mean, inverse = mean_and_inverse(jnp.concatenate([ref[...] for ref in totals], axis=0))
    gain = inverse * (1.0 + scale_ref[...])
    bias = shift_ref[...] - mean * gain
    row, col = iota((LANES, CHANS), 0), iota((LANES, CHANS), 1)
    chosen = ((col == row + place_ref[0] * SLICE) & (row < SLICE)).astype(F32).astype(BF16)
    weights = w_ref[...]
    top, bottom = place_ref[2] == 0, place_ref[2] == ROW_DEVS - 1
    each = 2
    for step in range(PARTICLES // each):
        active, raw = [], []
        for n in range(step * each, (step + 1) * each):
            which, j = n // HALF, n % HALF
            x = slabs[which][j]
            raw.append(x)
            act = lambda v: silu(v.astype(F32) * gain[n : n + 1] + bias[n : n + 1])
            above, below = act(edges[which][0, j]), act(edges[which][1, j])
            active += [jnp.where(top, 0.0, above), act(x), jnp.where(bottom, 0.0, below)]
        active = jnp.concatenate(active, axis=0).astype(BF16)
        raw = jnp.concatenate(raw, axis=0)
        taps = lax.dot_general(active, weights, NT, preferred_element_type=F32)
        field = lax.dot_general(raw, chosen, NT, preferred_element_type=F32)
        for k in range(each):
            at = k * (TOKENS + 2 * WIDTH)
            full = field[k * TOKENS : (k + 1) * TOKENS]
            for a in range(3):
                rows = slice(at + a * WIDTH, at + a * WIDTH + TOKENS)
                full = full + taps[rows, a * LANES : (a + 1) * LANES]
            done_ref[step * each + k] = packed(across(full)).astype(BF16)
    for p in range(PARTICLES):
        out_ref[p] = done_ref[spot(place_ref, anc_ref[p])]


def gather_kernel(x_ref, resid_ref, out_ref, wide_ref):
    lane = iota((32, LANES), 1)
    for t in range(3):
        blocks = [jnp.zeros((32, LANES), F32) for _ in range(CHANS // LANES)]
        for p in range(PARTICLES):
            block, off = (p * SLICE) // LANES, (p * SLICE) % LANES
            turn = (off - t * SLICE) % LANES
            piece = x_ref[p].astype(F32)
            if turn:
                piece = pltpu.roll(piece, turn, 1)
            end = off + SLICE
            blocks[block] = jnp.where((lane >= off) & (lane < end), piece, blocks[block])
            if end > LANES:
                blocks[block + 1] = jnp.where(lane < end - LANES, piece, blocks[block + 1])
        for n, value in enumerate(blocks):
            wide_ref[32 * t : 32 * (t + 1), n * LANES : (n + 1) * LANES] = value
    wide = wide_ref[...]
    resid_ref[...] = wide.astype(BF16)
    out_ref[...] = jnp.broadcast_to(group_rows([wide])[None], out_ref.shape)


def project_kernel(totals_ref, resid_ref, w_ref, out_ref, both_ref):
    mean, inverse = mean_and_inverse(jnp.sum(totals_ref[...], axis=0))
    normed = ((resid_ref[...].astype(F32) - mean[:1]) * inverse[:1]).astype(BF16)
    both_ref[...] = jnp.dot(normed, w_ref[...], preferred_element_type=F32)
    low = iota((TOKENS, LANES), 1) < 64
    low_s = iota((16, LANES), 1) < 64
    for pair in range(HEADS // 2):
        q, k, v = (
            both_ref[:, n * CHANS + pair * LANES : n * CHANS + (pair + 1) * LANES] for n in range(3)
        )
        q_turn, k_turn, v_turn = (pltpu.roll(x, 64, 1) for x in (q, k, v))
        mixed = (jnp.where(low, k, v_turn), jnp.where(low, k_turn, v))
        lows, highs = (q, q_turn), (q_turn, q)
        for side in range(2):
            keys_values = mixed[side].astype(BF16)
            for b in range(QUERY_BLOCKS):
                slot = (2 * pair + side) * QUERY_BLOCKS + b
                at = 32 * b
                two = jnp.where(low_s, lows[side][at : at + 16], highs[side][at + 16 : at + 32])
                out_ref[slot, :TOKENS] = keys_values
                out_ref[slot, TOKENS:] = two.astype(BF16)
    for slot in range(HEADS * QUERY_BLOCKS, ROW_DEVS):
        out_ref[slot] = jnp.zeros((SLOT, LANES), BF16)


def attend_kernel(x_ref, out_ref, keys_ref, ones_ref, query_ref, half_ref):
    low = iota((TOKENS, LANES), 1) < 64
    for r in range(ROW_DEVS):
        block = x_ref[r, :TOKENS]
        keys_ref[r * TOKENS : (r + 1) * TOKENS] = block
        ones_ref[r * TOKENS : (r + 1) * TOKENS] = jnp.where(low, jnp.ones_like(block), block)
        query_ref[r * 16 : (r + 1) * 16] = x_ref[r, TOKENS:].astype(F32)
    size = 256
    low_q = iota((size, LANES), 1) < 64
    factor = 0.125 * 1.4426950408889634
    for n in range(2):
        here = query_ref[n * size : (n + 1) * size]
        for side in range(2):
            turned = here if side == 0 else pltpu.roll(here, 64, 1)
            query = jnp.where(low_q, turned, 0.0).astype(BF16)
            scores = lax.dot_general(query, keys_ref[...], NT, preferred_element_type=F32)
            top = jnp.max(scores, axis=1, keepdims=True)
            weights = jnp.exp2((scores - top) * factor).astype(BF16)
            result = jnp.dot(weights, ones_ref[...], preferred_element_type=F32)
            other = pltpu.roll(result, 64, 1)
            if side == 0:
                half_ref[...] = other / result
            else:
                both = jnp.where(low_q, half_ref[...], result / other).astype(BF16)
                for r in range(size // 16):
                    out_ref[n * (size // 16) + r] = both[r * 16 : (r + 1) * 16]


def output_kernel(x_ref, resid_ref, w_ref, out_ref, wide_ref):
    low = iota((16, LANES), 1) < 64
    for pair in range(HEADS // 2):
        for b in range(QUERY_BLOCKS):
            first = x_ref[2 * pair * QUERY_BLOCKS + b].astype(F32)
            second = x_ref[(2 * pair + 1) * QUERY_BLOCKS + b].astype(F32)
            cols = slice(pair * LANES, (pair + 1) * LANES)
            at = 32 * b
            wide_ref[at : at + 16, cols] = jnp.where(low, first, pltpu.roll(second, 64, 1))
            wide_ref[at + 16 : at + 32, cols] = jnp.where(low, pltpu.roll(first, 64, 1), second)
    mixed = wide_ref[...].astype(BF16)
    product = jnp.dot(mixed, w_ref[...], preferred_element_type=F32)
    out_ref[...] = (resid_ref[...].astype(F32) + product).astype(BF16)


def exchange(values, axes):
    return lax.all_to_all(values, axes, split_axis=0, concat_axis=0, tiled=True)


def per_device(latent, ada_scale, ada_shift, conv_weight, qkv_weight, out_weight, ancestors):
    slab = latent.reshape(TOKENS, CHANS)
    particle = lax.axis_index(PART).astype(jnp.int32)
    place = jnp.stack(
        [particle] + [lax.axis_index(a).astype(jnp.int32) for a in ("core", ROWS)]
    )

    swap = [(0, 1), (1, 0)]
    here = exchange(jnp.broadcast_to(slab[None], (HALF, TOKENS, CHANS)), CHIPS)
    above = lax.ppermute(here[:, LAST:], ROWS, [(i, i + 1) for i in range(ROW_DEVS - 1)])
    below = lax.ppermute(here[:, :WIDTH], ROWS, [(i + 1, i) for i in range(ROW_DEVS - 1)])
    edges = jnp.stack([above, below])
    slabs = [here, lax.ppermute(here, "core", swap)]
    edges = [edges, lax.ppermute(edges, "core", swap)]

    picked = call(pick_kernel, shaped(ROW_DEVS, 80, LANES), [SMEM, VMEM, VMEM], 10**7, 10**6)(
        place, here, conv_weight
    )
    picked = exchange(picked, ROWS)
    totals = call(total_kernel, shaped(HALF, LANES, dtype=F32), [VMEM], 10**5, 10**5)(picked)
    totals = [totals, lax.ppermute(totals, "core", swap)]
    weights = call(
        weights_kernel,
        shaped(3 * LANES, CHANS),
        [VMEM],
        10**6,
        10**6,
        scratch=(
            pltpu.VMEM((SLICE, 9 * CHANS + 2 * LANES), F32),
            pltpu.VMEM((3 * LANES, CHANS), F32),
        ),
    )(picked)
    pieces = call(
        conv_kernel,
        shaped(PARTICLES, 32, LANES),
        [SMEM, SMEM] + [VMEM] * 9,
        2 * 10**9,
        4 * 10**6,
        vmem=32,
        scratch=(pltpu.VMEM((PARTICLES, 32, LANES), BF16),),
    )(place, ancestors, ada_scale[None], ada_shift[None], weights, *totals, *slabs, *edges)
    pieces = exchange(pieces, PART)

    resid, sums = call(
        gather_kernel,
        [shaped(TOKENS, CHANS), shaped(ROW_DEVS, 8, LANES, dtype=F32)],
        [VMEM],
        10**6,
        10**6,
        scratch=(pltpu.VMEM((TOKENS, CHANS), F32),),
    )(pieces)
    sums = exchange(sums, ROWS)
    slots = call(
        project_kernel,
        shaped(ROW_DEVS, SLOT, LANES),
        [VMEM] * 3,
        3 * 10**8,
        4 * 10**6,
        scratch=(pltpu.VMEM((TOKENS, 3 * CHANS), F32),),
    )(sums, resid, qkv_weight)
    slots = exchange(slots, ROWS)
    rows = ROW_DEVS * TOKENS
    mixed = call(
        attend_kernel,
        shaped(ROW_DEVS, 16, LANES),
        [VMEM],
        2 * 10**9,
        2 * 10**6,
        vmem=40,
        scratch=(
            pltpu.VMEM((rows, LANES), BF16),
            pltpu.VMEM((rows, LANES), BF16),
            pltpu.VMEM((ROW_DEVS * 16, LANES), F32),
            pltpu.VMEM((256, LANES), F32),
        ),
    )(slots)
    mixed = exchange(mixed, ROWS)
    block = call(
        output_kernel,
        shaped(TOKENS, CHANS),
        [VMEM] * 3,
        10**8,
        10**6,
        scratch=(pltpu.VMEM((TOKENS, CHANS), F32),),
    )(mixed, resid, out_weight)
    return block.reshape(1, ROWS_HERE, WIDTH, CHANS)


def solution(mesh):
    split = Mesh(mesh.devices.reshape(4, 2, 2, 4, 8), PART + ROWS)
    placed = (P(PART, ROWS, None, None), P(), P(), P(ROWS, None), P(), P(), P())
    return jax.shard_map(
        per_device,
        mesh=split,
        in_specs=placed,
        out_specs=P(PART, ROWS, None, None),
        check_vma=False,
    )
```

```python
import jax
import jax.numpy as jnp
from jax import lax
from jax.experimental import pallas as pl
from jax.experimental.pallas import tpu as pltpu
from jax.sharding import Mesh
from jax.sharding import PartitionSpec as P

HEADS = 10
GROUPS = 32
CHANS = 640
WIDTH = 24
ROWS_HERE = 4
TOKENS = ROWS_HERE * WIDTH
LAST = TOKENS - WIDTH
PARTICLES = 16
HALF = PARTICLES // 2
ROW_DEVS = 32
PER_GROUP = CHANS // GROUPS
SLICE = CHANS // PARTICLES
COUNT = ROWS_HERE * ROW_DEVS * WIDTH * PER_GROUP
LANES = 128
KERNEL_ROWS = 9 * CHANS // ROW_DEVS
TAIL = KERNEL_ROWS - LANES
QUERY_BLOCKS = 3
SLOT = TOKENS + 16

PART = ("x", "z_lo", "core")
CHIPS = ("x", "z_lo")
ROWS = ("z_hi", "y")

NT = (((1,), (1,)), ((), ()))
F32 = jnp.float32
BF16 = jnp.bfloat16
SMEM = pl.BlockSpec(memory_space=pltpu.SMEM)
VMEM = pl.BlockSpec(memory_space=pltpu.VMEM)


def call(kernel, out_shape, in_specs, flops, size, vmem=16, scratch=()):
    out_specs = jax.tree.map(lambda _: VMEM, out_shape)
    return pl.pallas_call(
        kernel,
        out_shape=out_shape,
        in_specs=in_specs,
        out_specs=out_specs,
        scratch_shapes=list(scratch),
        compiler_params=pltpu.CompilerParams(vmem_limit_bytes=vmem * 1024 * 1024),
        cost_estimate=pl.CostEstimate(flops=flops, bytes_accessed=size, transcendentals=0),
    )


def shaped(*shape, dtype=BF16):
    return jax.ShapeDtypeStruct(shape, dtype)


def iota(shape, dim):
    return lax.broadcasted_iota(jnp.int32, shape, dim)


def exact_dot(a, b):
    return jnp.dot(a, b, precision=lax.Precision.HIGHEST, preferred_element_type=F32)


def group_rows(values):
    fill = [jnp.zeros((1, CHANS), F32)] * (8 - len(values))
    sums = jnp.concatenate([jnp.sum(v, axis=0, keepdims=True) for v in values] + fill, axis=0)
    squares = [jnp.sum(v * v, axis=0, keepdims=True) for v in values] + fill
    squares = jnp.concatenate(squares, axis=0)
    chan, lane = iota((CHANS, LANES), 0), iota((CHANS, LANES), 1)
    first = ((chan >= lane * PER_GROUP) & (chan < (lane + 1) * PER_GROUP)).astype(F32)
    other = lane - GROUPS
    second = ((chan >= other * PER_GROUP) & (chan < (other + 1) * PER_GROUP)).astype(F32)
    return exact_dot(sums, first) + exact_dot(squares, second)


def mean_and_inverse(totals):
    lane, chan = iota((LANES, CHANS), 0), iota((LANES, CHANS), 1)
    first = ((chan >= lane * PER_GROUP) & (chan < (lane + 1) * PER_GROUP)).astype(F32)
    other = lane - GROUPS
    second = ((chan >= other * PER_GROUP) & (chan < (other + 1) * PER_GROUP)).astype(F32)
    mean = exact_dot(totals, first) * (1.0 / COUNT)
    square = exact_dot(totals, second) * (1.0 / COUNT)
    return mean, lax.rsqrt(square - mean * mean + 1e-05)


def thirds(value):
    parts = []
    for _ in range(3):
        top = value.astype(BF16).astype(F32)
        parts.append(top)
        value = value - top
    return parts


def spread_kernel(x_ref, out_ref):
    out_ref[...] = jnp.broadcast_to(x_ref[...][None], out_ref.shape)


def pick_kernel(place_ref, x_ref, w_ref, out_ref):
    row, col = iota((48, CHANS), 0), iota((48, CHANS), 1)
    chosen = ((col == row + place_ref[0] * SLICE) & (row < SLICE)).astype(F32).astype(BF16)
    picked = lax.dot_general(chosen, w_ref[...], NT, preferred_element_type=F32)
    head = picked[:, :LANES]
    rest = jnp.concatenate([picked[:, LANES:], jnp.zeros((48, LANES - TAIL), F32)], axis=1)
    turned = pltpu.roll(pltpu.roll(rest, 48 - 20, 0), 64, 1)
    low = jnp.where(iota((24, LANES), 1) < 64, rest[:24], turned[:24])
    values = [x_ref[j].astype(F32) for j in range(HALF)]
    first, second, third = thirds(group_rows(values))
    sums = jnp.concatenate([first + pltpu.roll(second, 64, 1), third], axis=0)
    slot = jnp.concatenate([head[:SLICE], low, sums], axis=0).astype(BF16)
    out_ref[...] = jnp.broadcast_to(slot[None], out_ref.shape)


def total_kernel(x_ref, out_ref):
    total = jnp.zeros((16, LANES), F32)
    for r in range(ROW_DEVS):
        total = total + x_ref[r, 64:80].astype(F32)
    total = total[:8] + pltpu.roll(total[:8], 64, 1) + total[8:]
    out_ref[...] = jnp.where(iota((HALF, LANES), 1) < 64, total, 0.0)


PLACE = {1: 0, 0: 1, 2: 2}


def weights_kernel(x_ref, out_ref, flat_ref, tall_ref):
    flat_ref[...] = jnp.zeros_like(flat_ref)
    row, lane = iota((SLICE, LANES), 0), iota((SLICE, LANES), 1)
    for r in range(ROW_DEVS):
        at = r * KERNEL_ROWS
        block, off = at // LANES, at % LANES
        slot = x_ref[r].astype(F32)
        low = jnp.concatenate([slot[SLICE:64], jnp.zeros((16, LANES), F32)], axis=0)
        rest = jnp.where(row < 20, low, pltpu.roll(pltpu.roll(low, 20, 0), 64, 1))
        rest = jnp.where(lane < TAIL, rest, 0.0)
        wide = jnp.concatenate([slot[:SLICE], rest, jnp.zeros((SLICE, LANES), F32)], axis=1)
        if off:
            wide = pltpu.roll(wide, off, 1)
        spot = slice(block * LANES, (block + 3) * LANES)
        flat_ref[:, spot] = flat_ref[:, spot] + wide
    tall_ref[...] = jnp.zeros_like(tall_ref)
    for a in range(3):
        for b in range(3):
            tap = 3 * a + b
            top = a * LANES + PLACE[b] * SLICE
            tall_ref[top : top + SLICE, :] = flat_ref[:, tap * CHANS : (tap + 1) * CHANS]
    out_ref[...] = tall_ref[...].astype(BF16)


def spot(place_ref, q):
    return lax.rem(lax.rem(q, 2) + place_ref[1], 2) * HALF + q // 2


def silu(v):
    half = 0.5 * v
    return half + half * jnp.tanh(half)


def across(full):
    rows = full.shape[0]
    at = lax.rem(iota((rows, LANES), 0), WIDTH)
    left = pltpu.roll(pltpu.roll(full, 1, 0), LANES - SLICE, 1)
    right = pltpu.roll(pltpu.roll(full, rows - 1, 0), LANES - 2 * SLICE, 1)
    total = full + jnp.where(at == 0, 0.0, left) + jnp.where(at == WIDTH - 1, 0.0, right)
    return jnp.where(iota((rows, LANES), 1) < SLICE, total, 0.0)


def packed(value):
    n = value.shape[0] // 3
    out = value[:n]
    for t in (1, 2):
        out = out + pltpu.roll(value[n * t : n * (t + 1)], SLICE * t, 1)
    return out


def unpacked(value):
    return jnp.concatenate(
        [value] + [pltpu.roll(value, LANES - SLICE * t, 1) for t in (1, 2)], axis=0
    )


def edge_kernel(scale_ref, shift_ref, w_ref, *refs):
    totals, slabs, (up_ref, down_ref, gain_ref, bias_ref) = refs[:2], refs[2:4], refs[4:]
    mean, inverse = mean_and_inverse(jnp.concatenate([ref[...] for ref in totals], axis=0))
    gain = inverse * (1.0 + scale_ref[...])
    bias = shift_ref[...] - mean * gain
    gain_ref[...] = gain
    bias_ref[...] = bias
    for rows, tap, ref in ((slice(0, WIDTH), 2, up_ref), (slice(LAST, TOKENS), 0, down_ref)):
        active = []
        for n in range(PARTICLES):
            x = slabs[n // HALF][n % HALF].astype(F32)[rows]
            active.append(silu(x * gain[n : n + 1] + bias[n : n + 1]))
        active = jnp.concatenate(active, axis=0).astype(BF16)
        weights = w_ref[tap * LANES : (tap + 1) * LANES, :]
        full = across(lax.dot_general(active, weights, NT, preferred_element_type=F32))
        for n in range(PARTICLES):
            ref[n] = packed(full[n * WIDTH : (n + 1) * WIDTH])


def conv_kernel(place_ref, gain_ref, bias_ref, w_ref, *refs):
    slabs, part_ref = refs[:2], refs[2]
    row, col = iota((LANES, CHANS), 0), iota((LANES, CHANS), 1)
    chosen = ((col == row + place_ref[0] * SLICE) & (row < SLICE)).astype(F32).astype(BF16)
    weights = w_ref[...]
    each = 2
    for step in range(PARTICLES // each):
        active, raw = [], []
        for n in range(step * each, (step + 1) * each):
            x = slabs[n // HALF][n % HALF]
            raw.append(x)
            v = x.astype(F32) * gain_ref[n : n + 1] + bias_ref[n : n + 1]
            active.append(silu(v).astype(BF16))
        active = jnp.concatenate(active, axis=0)
        raw = jnp.concatenate(raw, axis=0)
        taps = lax.dot_general(active, weights, NT, preferred_element_type=F32)
        field = lax.dot_general(raw, chosen, NT, preferred_element_type=F32)
        for k in range(each):
            rows = slice(k * TOKENS, (k + 1) * TOKENS)
            t0, t1, t2 = (taps[rows, n * LANES : (n + 1) * LANES] for n in range(3))
            base = t1 + field[rows]
            full = jnp.concatenate(
                [
                    base[:WIDTH] + t2[WIDTH : 2 * WIDTH],
                    base[WIDTH:LAST] + t0[: LAST - WIDTH] + t2[2 * WIDTH :],
                    base[LAST:] + t0[LAST - WIDTH : LAST],
                ],
                axis=0,
            )
            part_ref[step * each + k] = across(full)


def finish_kernel(place_ref, anc_ref, part_ref, above_ref, below_ref, out_ref):
    lane = iota((TOKENS, LANES), 1)
    for p in range(PARTICLES):
        q = spot(place_ref, anc_ref[p])
        total = jnp.concatenate(
            [
                part_ref[q, :WIDTH] + unpacked(above_ref[q]),
                part_ref[q, WIDTH:LAST],
                part_ref[q, LAST:] + unpacked(below_ref[q]),
            ],
            axis=0,
        )
        out_ref[p] = packed(jnp.where(lane < SLICE, total, 0.0)).astype(BF16)


def gather_kernel(x_ref, resid_ref, out_ref, wide_ref):
    lane = iota((32, LANES), 1)
    for t in range(3):
        blocks = [jnp.zeros((32, LANES), F32) for _ in range(CHANS // LANES)]
        for p in range(PARTICLES):
            block, off = (p * SLICE) // LANES, (p * SLICE) % LANES
            turn = (off - t * SLICE) % LANES
            piece = x_ref[p].astype(F32)
            if turn:
                piece = pltpu.roll(piece, turn, 1)
            end = off + SLICE
            blocks[block] = jnp.where((lane >= off) & (lane < end), piece, blocks[block])
            if end > LANES:
                blocks[block + 1] = jnp.where(lane < end - LANES, piece, blocks[block + 1])
        for n, value in enumerate(blocks):
            wide_ref[32 * t : 32 * (t + 1), n * LANES : (n + 1) * LANES] = value
    wide = wide_ref[...]
    resid_ref[...] = wide.astype(BF16)
    out_ref[...] = jnp.broadcast_to(group_rows([wide])[None], out_ref.shape)


def project_kernel(totals_ref, resid_ref, w_ref, out_ref, both_ref):
    mean, inverse = mean_and_inverse(jnp.sum(totals_ref[...], axis=0))
    normed = ((resid_ref[...].astype(F32) - mean[:1]) * inverse[:1]).astype(BF16)
    both_ref[...] = jnp.dot(normed, w_ref[...], preferred_element_type=F32)
    low = iota((TOKENS, LANES), 1) < 64
    low_s = iota((16, LANES), 1) < 64
    for pair in range(HEADS // 2):
        q, k, v = (
            both_ref[:, n * CHANS + pair * LANES : n * CHANS + (pair + 1) * LANES] for n in range(3)
        )
        q_turn, k_turn, v_turn = (pltpu.roll(x, 64, 1) for x in (q, k, v))
        mixed = (jnp.where(low, k, v_turn), jnp.where(low, k_turn, v))
        lows, highs = (q, q_turn), (q_turn, q)
        for side in range(2):
            keys_values = mixed[side].astype(BF16)
            for b in range(QUERY_BLOCKS):
                slot = (2 * pair + side) * QUERY_BLOCKS + b
                at = 32 * b
                two = jnp.where(low_s, lows[side][at : at + 16], highs[side][at + 16 : at + 32])
                out_ref[slot, :TOKENS] = keys_values
                out_ref[slot, TOKENS:] = two.astype(BF16)
    for slot in range(HEADS * QUERY_BLOCKS, ROW_DEVS):
        out_ref[slot] = jnp.zeros((SLOT, LANES), BF16)


def attend_kernel(x_ref, out_ref, keys_ref, ones_ref, query_ref, half_ref):
    low = iota((TOKENS, LANES), 1) < 64
    for r in range(ROW_DEVS):
        block = x_ref[r, :TOKENS]
        keys_ref[r * TOKENS : (r + 1) * TOKENS] = block
        ones_ref[r * TOKENS : (r + 1) * TOKENS] = jnp.where(low, jnp.ones_like(block), block)
        query_ref[r * 16 : (r + 1) * 16] = x_ref[r, TOKENS:].astype(F32)
    size = 256
    low_q = iota((size, LANES), 1) < 64
    factor = 0.125 * 1.4426950408889634
    for n in range(2):
        here = query_ref[n * size : (n + 1) * size]
        for side in range(2):
            turned = here if side == 0 else pltpu.roll(here, 64, 1)
            query = jnp.where(low_q, turned, 0.0).astype(BF16)
            scores = lax.dot_general(query, keys_ref[...], NT, preferred_element_type=F32)
            top = jnp.max(scores, axis=1, keepdims=True)
            weights = jnp.exp2((scores - top) * factor).astype(BF16)
            result = jnp.dot(weights, ones_ref[...], preferred_element_type=F32)
            other = pltpu.roll(result, 64, 1)
            if side == 0:
                half_ref[...] = other / result
            else:
                both = jnp.where(low_q, half_ref[...], result / other).astype(BF16)
                for r in range(size // 16):
                    out_ref[n * (size // 16) + r] = both[r * 16 : (r + 1) * 16]


def output_kernel(x_ref, resid_ref, w_ref, out_ref, wide_ref):
    low = iota((16, LANES), 1) < 64
    for pair in range(HEADS // 2):
        for b in range(QUERY_BLOCKS):
            first = x_ref[2 * pair * QUERY_BLOCKS + b].astype(F32)
            second = x_ref[(2 * pair + 1) * QUERY_BLOCKS + b].astype(F32)
            cols = slice(pair * LANES, (pair + 1) * LANES)
            at = 32 * b
            wide_ref[at : at + 16, cols] = jnp.where(low, first, pltpu.roll(second, 64, 1))
            wide_ref[at + 16 : at + 32, cols] = jnp.where(low, pltpu.roll(first, 64, 1), second)
    mixed = wide_ref[...].astype(BF16)
    product = jnp.dot(mixed, w_ref[...], preferred_element_type=F32)
    out_ref[...] = (resid_ref[...].astype(F32) + product).astype(BF16)


def exchange(values, axes):
    return lax.all_to_all(values, axes, split_axis=0, concat_axis=0, tiled=True)


def per_device(latent, ada_scale, ada_shift, conv_weight, qkv_weight, out_weight, ancestors):
    slab = latent.reshape(TOKENS, CHANS)
    particle = lax.axis_index(PART).astype(jnp.int32)
    place = jnp.stack([particle, lax.axis_index("core").astype(jnp.int32)])

    swap = [(0, 1), (1, 0)]
    copies = call(spread_kernel, shaped(HALF, TOKENS, CHANS), [VMEM], 10**5, 10**6)(slab)
    here = exchange(copies, CHIPS)
    slabs = [here, lax.ppermute(here, "core", swap)]

    picked = call(pick_kernel, shaped(ROW_DEVS, 80, LANES), [SMEM, VMEM, VMEM], 10**7, 10**6)(
        place, here, conv_weight
    )
    picked = exchange(picked, ROWS)
    totals = call(total_kernel, shaped(HALF, LANES, dtype=F32), [VMEM], 10**5, 10**5)(picked)
    totals = [totals, lax.ppermute(totals, "core", swap)]
    weights = call(
        weights_kernel,
        shaped(3 * LANES, CHANS),
        [VMEM],
        10**6,
        10**6,
        scratch=(
            pltpu.VMEM((SLICE, 9 * CHANS + 2 * LANES), F32),
            pltpu.VMEM((3 * LANES, CHANS), F32),
        ),
    )(picked)

    edge = shaped(PARTICLES, WIDTH // 3, LANES, dtype=F32)
    each = shaped(PARTICLES, CHANS, dtype=F32)
    up, down, gain, bias = call(edge_kernel, [edge, edge, each, each], [VMEM] * 7, 10**8, 10**6)(
        ada_scale[None], ada_shift[None], weights, *totals, *slabs
    )
    above = lax.ppermute(down, ROWS, [(i, i + 1) for i in range(ROW_DEVS - 1)])
    below = lax.ppermute(up, ROWS, [(i + 1, i) for i in range(ROW_DEVS - 1)])
    part = call(
        conv_kernel,
        shaped(PARTICLES, TOKENS, LANES, dtype=F32),
        [SMEM] + [VMEM] * 5,
        2 * 10**9,
        4 * 10**6,
        vmem=32,
    )(place, gain, bias, weights, *slabs)
    pieces = call(
        finish_kernel, shaped(PARTICLES, 32, LANES), [SMEM, SMEM] + [VMEM] * 3, 10**6, 10**6
    )(place, ancestors, part, above, below)
    pieces = exchange(pieces, PART)

    resid, sums = call(
        gather_kernel,
        [shaped(TOKENS, CHANS), shaped(ROW_DEVS, 8, LANES, dtype=F32)],
        [VMEM],
        10**6,
        10**6,
        scratch=(pltpu.VMEM((TOKENS, CHANS), F32),),
    )(pieces)
    sums = exchange(sums, ROWS)
    slots = call(
        project_kernel,
        shaped(ROW_DEVS, SLOT, LANES),
        [VMEM] * 3,
        3 * 10**8,
        4 * 10**6,
        scratch=(pltpu.VMEM((TOKENS, 3 * CHANS), F32),),
    )(sums, resid, qkv_weight)
    slots = exchange(slots, ROWS)
    rows = ROW_DEVS * TOKENS
    mixed = call(
        attend_kernel,
        shaped(ROW_DEVS, 16, LANES),
        [VMEM],
        2 * 10**9,
        2 * 10**6,
        vmem=40,
        scratch=(
            pltpu.VMEM((rows, LANES), BF16),
            pltpu.VMEM((rows, LANES), BF16),
            pltpu.VMEM((ROW_DEVS * 16, LANES), F32),
            pltpu.VMEM((256, LANES), F32),
        ),
    )(slots)
    mixed = exchange(mixed, ROWS)
    block = call(
        output_kernel,
        shaped(TOKENS, CHANS),
        [VMEM] * 3,
        10**8,
        10**6,
        scratch=(pltpu.VMEM((TOKENS, CHANS), F32),),
    )(mixed, resid, out_weight)
    return block.reshape(1, ROWS_HERE, WIDTH, CHANS)


def solution(mesh):
    split = Mesh(mesh.devices.reshape(4, 2, 2, 4, 8), PART + ROWS)
    placed = (P(PART, ROWS, None, None), P(), P(), P(ROWS, None), P(), P(), P())
    return jax.shard_map(
        per_device,
        mesh=split,
        in_specs=placed,
        out_specs=P(PART, ROWS, None, None),
        check_vma=False,
    )
```

```python
import jax
import jax.numpy as jnp
from jax import lax
from jax.experimental import pallas as pl
from jax.experimental.pallas import tpu as pltpu
from jax.sharding import Mesh
from jax.sharding import PartitionSpec as P

HEADS = 10
GROUPS = 32
CHANS = 640
WIDTH = 24
ROWS_HERE = 4
TOKENS = ROWS_HERE * WIDTH
LAST = TOKENS - WIDTH
ALL = TOKENS + 2 * WIDTH
PARTICLES = 16
HALF = PARTICLES // 2
ROW_DEVS = 32
PER_GROUP = CHANS // GROUPS
SLICE = CHANS // PARTICLES
COUNT = ROWS_HERE * ROW_DEVS * WIDTH * PER_GROUP
LANES = 128
KERNEL_ROWS = 9 * CHANS // ROW_DEVS
TAIL = KERNEL_ROWS - LANES
QUERY_BLOCKS = 3
SLOT = TOKENS + 16

PART = ("x", "z_lo", "core")
CHIPS = ("x", "z_lo")
ROWS = ("z_hi", "y")

NT = (((1,), (1,)), ((), ()))
F32 = jnp.float32
BF16 = jnp.bfloat16
SMEM = pl.BlockSpec(memory_space=pltpu.SMEM)
VMEM = pl.BlockSpec(memory_space=pltpu.VMEM)
ANY = pl.BlockSpec(memory_space=pl.ANY)


def call(kernel, out_shape, in_specs, flops, size, vmem=16, scratch=()):
    out_specs = jax.tree.map(lambda _: VMEM, out_shape)
    return pl.pallas_call(
        kernel,
        out_shape=out_shape,
        in_specs=in_specs,
        out_specs=out_specs,
        scratch_shapes=list(scratch),
        compiler_params=pltpu.CompilerParams(vmem_limit_bytes=vmem * 1024 * 1024),
        cost_estimate=pl.CostEstimate(flops=flops, bytes_accessed=size, transcendentals=0),
    )


def shaped(*shape, dtype=BF16):
    return jax.ShapeDtypeStruct(shape, dtype)


def iota(shape, dim):
    return lax.broadcasted_iota(jnp.int32, shape, dim)


def exact_dot(a, b):
    return jnp.dot(a, b, precision=lax.Precision.HIGHEST, preferred_element_type=F32)


def group_rows(values):
    fill = [jnp.zeros((1, CHANS), F32)] * (8 - len(values))
    sums = jnp.concatenate([jnp.sum(v, axis=0, keepdims=True) for v in values] + fill, axis=0)
    squares = [jnp.sum(v * v, axis=0, keepdims=True) for v in values] + fill
    squares = jnp.concatenate(squares, axis=0)
    chan, lane = iota((CHANS, LANES), 0), iota((CHANS, LANES), 1)
    first = ((chan >= lane * PER_GROUP) & (chan < (lane + 1) * PER_GROUP)).astype(F32)
    other = lane - GROUPS
    second = ((chan >= other * PER_GROUP) & (chan < (other + 1) * PER_GROUP)).astype(F32)
    return exact_dot(sums, first) + exact_dot(squares, second)


def mean_and_inverse(totals):
    lane, chan = iota((LANES, CHANS), 0), iota((LANES, CHANS), 1)
    first = ((chan >= lane * PER_GROUP) & (chan < (lane + 1) * PER_GROUP)).astype(F32)
    other = lane - GROUPS
    second = ((chan >= other * PER_GROUP) & (chan < (other + 1) * PER_GROUP)).astype(F32)
    mean = exact_dot(totals, first) * (1.0 / COUNT)
    square = exact_dot(totals, second) * (1.0 / COUNT)
    return mean, lax.rsqrt(square - mean * mean + 1e-05)


def thirds(value):
    parts = []
    for _ in range(3):
        top = value.astype(BF16).astype(F32)
        parts.append(top)
        value = value - top
    return parts


def spread_kernel(x_ref, out_ref, first_ref, last_ref):
    out_ref[...] = jnp.broadcast_to(x_ref[...][None], out_ref.shape)
    wide = x_ref[...].astype(F32)
    first_ref[...] = wide[:WIDTH].astype(BF16)
    last_ref[...] = wide[LAST:].astype(BF16)


def join_kernel(mine_ref, opposite_ref, _, out_ref):
    out_ref[0] = mine_ref[...]
    out_ref[1] = opposite_ref[...]


def pick_kernel(place_ref, x_ref, w_ref, _, out_ref):
    row, col = iota((48, CHANS), 0), iota((48, CHANS), 1)
    chosen = ((col == row + place_ref[0] * SLICE) & (row < SLICE)).astype(F32).astype(BF16)
    picked = lax.dot_general(chosen, w_ref[...], NT, preferred_element_type=F32)
    head = picked[:, :LANES]
    rest = jnp.concatenate([picked[:, LANES:], jnp.zeros((48, LANES - TAIL), F32)], axis=1)
    turned = pltpu.roll(pltpu.roll(rest, 48 - 20, 0), 64, 1)
    low = jnp.where(iota((24, LANES), 1) < 64, rest[:24], turned[:24])
    values = [x_ref[j].astype(F32) for j in range(HALF)]
    first, second, third = thirds(group_rows(values))
    sums = jnp.concatenate([first + pltpu.roll(second, 64, 1), third], axis=0)
    slot = jnp.concatenate([head[:SLICE], low, sums], axis=0).astype(BF16)
    out_ref[...] = jnp.broadcast_to(slot[None], out_ref.shape)


def total_kernel(x_ref, out_ref):
    total = jnp.zeros((16, LANES), F32)
    for r in range(ROW_DEVS):
        total = total + x_ref[r, 64:80].astype(F32)
    total = total[:8] + pltpu.roll(total[:8], 64, 1) + total[8:]
    out_ref[...] = jnp.where(iota((HALF, LANES), 1) < 64, total, 0.0)


PLACE = {1: 0, 0: 1, 2: 2}


def weights_kernel(x_ref, out_ref, flat_ref, tall_ref):
    flat_ref[...] = jnp.zeros_like(flat_ref)
    row, lane = iota((SLICE, LANES), 0), iota((SLICE, LANES), 1)
    for r in range(ROW_DEVS):
        at = r * KERNEL_ROWS
        block, off = at // LANES, at % LANES
        slot = x_ref[r].astype(F32)
        low = jnp.concatenate([slot[SLICE:64], jnp.zeros((16, LANES), F32)], axis=0)
        rest = jnp.where(row < 20, low, pltpu.roll(pltpu.roll(low, 20, 0), 64, 1))
        rest = jnp.where(lane < TAIL, rest, 0.0)
        wide = jnp.concatenate([slot[:SLICE], rest, jnp.zeros((SLICE, LANES), F32)], axis=1)
        if off:
            wide = pltpu.roll(wide, off, 1)
        spot = slice(block * LANES, (block + 3) * LANES)
        flat_ref[:, spot] = flat_ref[:, spot] + wide
    tall_ref[...] = jnp.zeros_like(tall_ref)
    for a in range(3):
        for b in range(3):
            tap = 3 * a + b
            top = a * LANES + PLACE[b] * SLICE
            tall_ref[top : top + SLICE, :] = flat_ref[:, tap * CHANS : (tap + 1) * CHANS]
    out_ref[...] = tall_ref[...].astype(BF16)


def spot(place_ref, q):
    return lax.rem(lax.rem(q, 2) + place_ref[1], 2) * HALF + q // 2


def silu(v):
    half = 0.5 * v
    return half + half * jnp.tanh(half)


def across(full):
    rows = full.shape[0]
    at = lax.rem(iota((rows, LANES), 0), WIDTH)
    left = pltpu.roll(pltpu.roll(full, 1, 0), LANES - SLICE, 1)
    right = pltpu.roll(pltpu.roll(full, rows - 1, 0), LANES - 2 * SLICE, 1)
    total = full + jnp.where(at == 0, 0.0, left) + jnp.where(at == WIDTH - 1, 0.0, right)
    return jnp.where(iota((rows, LANES), 1) < SLICE, total, 0.0)


def packed(value):
    n = value.shape[0] // 3
    out = value[:n]
    for t in (1, 2):
        out = out + pltpu.roll(value[n * t : n * (t + 1)], SLICE * t, 1)
    return out


STEPS = (0, 1, 3, 2)


def beside(place_ref, j):
    dx = lax.rem(j // 2 + 4 - place_ref[2], 4)
    dz = lax.rem(j % 2 + place_ref[3], 2)
    return 2 * jnp.where(dx == 2, 3, jnp.where(dx == 3, 2, dx)) + dz


def merge_kernel(place_ref, x_ref, edge_ref, out_ref):
    for j in range(HALF):
        at = beside(place_ref, j)
        parts = [x_ref[j], edge_ref[at, 0], edge_ref[at, 1]]
        out_ref[j] = jnp.concatenate([v.astype(F32) for v in parts], axis=0).astype(BF16)


def conv_kernel(place_ref, anc_ref, scale_ref, shift_ref, w_ref, *refs):
    totals, slabs, (out_ref, done_ref) = refs[:2], refs[2:4], refs[4:]
    mean, inverse = mean_and_inverse(jnp.concatenate([ref[...] for ref in totals], axis=0))
    gain = inverse * (1.0 + scale_ref[...])
    bias = shift_ref[...] - mean * gain
    row, col = iota((LANES, CHANS), 0), iota((LANES, CHANS), 1)
    chosen = ((col == row + place_ref[0] * SLICE) & (row < SLICE)).astype(F32).astype(BF16)
    weights = w_ref[...]
    top, bottom = place_ref[4] == 0, place_ref[4] == ROW_DEVS - 1
    each = 2
    for step in range(PARTICLES // each):
        active, raw = [], []
        for n in range(step * each, (step + 1) * each):
            x = slabs[n // HALF][n % HALF]
            raw.append(x[:TOKENS])
            active.append(silu(x.astype(F32) * gain[n : n + 1] + bias[n : n + 1]).astype(BF16))
        active = jnp.concatenate(active, axis=0)
        raw = jnp.concatenate(raw, axis=0)
        taps = lax.dot_general(active, weights, NT, preferred_element_type=F32)
        field = lax.dot_general(raw, chosen, NT, preferred_element_type=F32)
        for k in range(each):
            here = taps[k * ALL : (k + 1) * ALL]
            t0, t1, t2 = (here[:, a * LANES : (a + 1) * LANES] for a in range(3))
            above = jnp.where(top, 0.0, t0[TOKENS : TOKENS + WIDTH])
            below = jnp.where(bottom, 0.0, t2[TOKENS + WIDTH :])
            full = field[k * TOKENS : (k + 1) * TOKENS] + t1[:TOKENS]
            full = full + jnp.concatenate([above, t0[:LAST]], axis=0)
            full = full + jnp.concatenate([t2[WIDTH:TOKENS], below], axis=0)
            done_ref[step * each + k] = packed(across(full)).astype(BF16)
    for p in range(PARTICLES):
        out_ref[p] = done_ref[spot(place_ref, anc_ref[p])]


def gather_kernel(x_ref, resid_ref, out_ref, wide_ref):
    lane = iota((32, LANES), 1)
    for t in range(3):
        blocks = [jnp.zeros((32, LANES), F32) for _ in range(CHANS // LANES)]
        for p in range(PARTICLES):
            block, off = (p * SLICE) // LANES, (p * SLICE) % LANES
            turn = (off - t * SLICE) % LANES
            piece = x_ref[p].astype(F32)
            if turn:
                piece = pltpu.roll(piece, turn, 1)
            end = off + SLICE
            blocks[block] = jnp.where((lane >= off) & (lane < end), piece, blocks[block])
            if end > LANES:
                blocks[block + 1] = jnp.where(lane < end - LANES, piece, blocks[block + 1])
        for n, value in enumerate(blocks):
            wide_ref[32 * t : 32 * (t + 1), n * LANES : (n + 1) * LANES] = value
    wide = wide_ref[...]
    resid_ref[...] = wide.astype(BF16)
    out_ref[...] = jnp.broadcast_to(group_rows([wide])[None], out_ref.shape)


def project_kernel(totals_ref, resid_ref, w_ref, out_ref, both_ref):
    mean, inverse = mean_and_inverse(jnp.sum(totals_ref[...], axis=0))
    normed = ((resid_ref[...].astype(F32) - mean[:1]) * inverse[:1]).astype(BF16)
    both_ref[...] = jnp.dot(normed, w_ref[...], preferred_element_type=F32)
    low = iota((TOKENS, LANES), 1) < 64
    low_s = iota((16, LANES), 1) < 64
    for pair in range(HEADS // 2):
        q, k, v = (
            both_ref[:, n * CHANS + pair * LANES : n * CHANS + (pair + 1) * LANES] for n in range(3)
        )
        q_turn, k_turn, v_turn = (pltpu.roll(x, 64, 1) for x in (q, k, v))
        mixed = (jnp.where(low, k, v_turn), jnp.where(low, k_turn, v))
        lows, highs = (q, q_turn), (q_turn, q)
        for side in range(2):
            keys_values = mixed[side].astype(BF16)
            for b in range(QUERY_BLOCKS):
                slot = (2 * pair + side) * QUERY_BLOCKS + b
                at = 32 * b
                two = jnp.where(low_s, lows[side][at : at + 16], highs[side][at + 16 : at + 32])
                out_ref[slot, :TOKENS] = keys_values
                out_ref[slot, TOKENS:] = two.astype(BF16)
    for slot in range(HEADS * QUERY_BLOCKS, ROW_DEVS):
        out_ref[slot] = jnp.zeros((SLOT, LANES), BF16)


def attend_kernel(x_ref, out_ref, keys_ref, ones_ref, query_ref, half_ref):
    low = iota((TOKENS, LANES), 1) < 64
    for r in range(ROW_DEVS):
        block = x_ref[r, :TOKENS]
        keys_ref[r * TOKENS : (r + 1) * TOKENS] = block
        ones_ref[r * TOKENS : (r + 1) * TOKENS] = jnp.where(low, jnp.ones_like(block), block)
        query_ref[r * 16 : (r + 1) * 16] = x_ref[r, TOKENS:].astype(F32)
    size = 256
    low_q = iota((size, LANES), 1) < 64
    factor = 0.125 * 1.4426950408889634
    for n in range(2):
        here = query_ref[n * size : (n + 1) * size]
        for side in range(2):
            turned = here if side == 0 else pltpu.roll(here, 64, 1)
            query = jnp.where(low_q, turned, 0.0).astype(BF16)
            scores = lax.dot_general(query, keys_ref[...], NT, preferred_element_type=F32)
            top = jnp.max(scores, axis=1, keepdims=True)
            weights = jnp.exp2((scores - top) * factor).astype(BF16)
            result = jnp.dot(weights, ones_ref[...], preferred_element_type=F32)
            other = pltpu.roll(result, 64, 1)
            if side == 0:
                half_ref[...] = other / result
            else:
                both = jnp.where(low_q, half_ref[...], result / other).astype(BF16)
                for r in range(size // 16):
                    out_ref[n * (size // 16) + r] = both[r * 16 : (r + 1) * 16]


def output_kernel(x_ref, resid_ref, w_ref, out_ref, wide_ref):
    low = iota((16, LANES), 1) < 64
    for pair in range(HEADS // 2):
        for b in range(QUERY_BLOCKS):
            first = x_ref[2 * pair * QUERY_BLOCKS + b].astype(F32)
            second = x_ref[(2 * pair + 1) * QUERY_BLOCKS + b].astype(F32)
            cols = slice(pair * LANES, (pair + 1) * LANES)
            at = 32 * b
            wide_ref[at : at + 16, cols] = jnp.where(low, first, pltpu.roll(second, 64, 1))
            wide_ref[at + 16 : at + 32, cols] = jnp.where(low, pltpu.roll(first, 64, 1), second)
    mixed = wide_ref[...].astype(BF16)
    product = jnp.dot(mixed, w_ref[...], preferred_element_type=F32)
    out_ref[...] = (resid_ref[...].astype(F32) + product).astype(BF16)


def exchange(values, axes):
    return lax.all_to_all(values, axes, split_axis=0, concat_axis=0, tiled=True)


def per_device(latent, ada_scale, ada_shift, conv_weight, qkv_weight, out_weight, ancestors):
    slab = latent.reshape(TOKENS, CHANS)
    particle = lax.axis_index(PART).astype(jnp.int32)
    place = jnp.stack(
        [particle] + [lax.axis_index(a).astype(jnp.int32) for a in ("core", "x", "z_lo", ROWS)]
    )

    swap = [(0, 1), (1, 0)]
    row = shaped(WIDTH, CHANS)
    copies, first, last = call(
        spread_kernel, [shaped(HALF, TOKENS, CHANS), row, row], [VMEM], 10**5, 10**6
    )(slab)
    here = exchange(copies, CHIPS)
    above = lax.ppermute(last, ROWS, [(i, i + 1) for i in range(ROW_DEVS - 1)])
    below = lax.ppermute(first, ROWS, [(i + 1, i) for i in range(ROW_DEVS - 1)])
    mine = jnp.stack([above, below])
    opposite = lax.ppermute(mine, "z_lo", swap)

    picked = call(pick_kernel, shaped(ROW_DEVS, 80, LANES), [SMEM, VMEM, VMEM, ANY], 10**7, 10**6)(
        place, here, conv_weight, opposite
    )
    pair = call(join_kernel, shaped(2, 2, WIDTH, CHANS), [VMEM, VMEM, ANY], 10**5, 10**6)(
        mine, opposite, picked
    )
    turns = [[((i + d) % 4, i) for i in range(4)] for d in STEPS[1:]]
    edges = jnp.concatenate([pair] + [lax.ppermute(pair, "x", turn) for turn in turns])
    merged = call(merge_kernel, shaped(HALF, ALL, CHANS), [SMEM, VMEM, VMEM], 10**6, 10**6)(
        place, here, edges
    )
    slabs = [merged, lax.ppermute(merged, "core", swap)]
    picked = exchange(picked, ROWS)
    totals = call(total_kernel, shaped(HALF, LANES, dtype=F32), [VMEM], 10**5, 10**5)(picked)
    totals = [totals, lax.ppermute(totals, "core", swap)]
    weights = call(
        weights_kernel,
        shaped(3 * LANES, CHANS),
        [VMEM],
        10**6,
        10**6,
        scratch=(
            pltpu.VMEM((SLICE, 9 * CHANS + 2 * LANES), F32),
            pltpu.VMEM((3 * LANES, CHANS), F32),
        ),
    )(picked)
    pieces = call(
        conv_kernel,
        shaped(PARTICLES, 32, LANES),
        [SMEM, SMEM] + [VMEM] * 7,
        2 * 10**9,
        4 * 10**6,
        vmem=32,
        scratch=(pltpu.VMEM((PARTICLES, 32, LANES), BF16),),
    )(place, ancestors, ada_scale[None], ada_shift[None], weights, *totals, *slabs)
    pieces = exchange(pieces, PART)

    resid, sums = call(
        gather_kernel,
        [shaped(TOKENS, CHANS), shaped(ROW_DEVS, 8, LANES, dtype=F32)],
        [VMEM],
        10**6,
        10**6,
        scratch=(pltpu.VMEM((TOKENS, CHANS), F32),),
    )(pieces)
    sums = exchange(sums, ROWS)
    slots = call(
        project_kernel,
        shaped(ROW_DEVS, SLOT, LANES),
        [VMEM] * 3,
        3 * 10**8,
        4 * 10**6,
        scratch=(pltpu.VMEM((TOKENS, 3 * CHANS), F32),),
    )(sums, resid, qkv_weight)
    slots = exchange(slots, ROWS)
    rows = ROW_DEVS * TOKENS
    mixed = call(
        attend_kernel,
        shaped(ROW_DEVS, 16, LANES),
        [VMEM],
        2 * 10**9,
        2 * 10**6,
        vmem=40,
        scratch=(
            pltpu.VMEM((rows, LANES), BF16),
            pltpu.VMEM((rows, LANES), BF16),
            pltpu.VMEM((ROW_DEVS * 16, LANES), F32),
            pltpu.VMEM((256, LANES), F32),
        ),
    )(slots)
    mixed = exchange(mixed, ROWS)
    block = call(
        output_kernel,
        shaped(TOKENS, CHANS),
        [VMEM] * 3,
        10**8,
        10**6,
        scratch=(pltpu.VMEM((TOKENS, CHANS), F32),),
    )(mixed, resid, out_weight)
    return block.reshape(1, ROWS_HERE, WIDTH, CHANS)


def solution(mesh):
    split = Mesh(mesh.devices.reshape(4, 2, 2, 4, 8), PART + ROWS)
    placed = (P(PART, ROWS, None, None), P(), P(), P(ROWS, None), P(), P(), P())
    return jax.shard_map(
        per_device,
        mesh=split,
        in_specs=placed,
        out_specs=P(PART, ROWS, None, None),
        check_vma=False,
    )
```

```python
import jax
import jax.numpy as jnp
from jax import lax
from jax.experimental import pallas as pl
from jax.experimental.pallas import tpu as pltpu
from jax.sharding import Mesh
from jax.sharding import PartitionSpec as P

HEADS = 10
GROUPS = 32
CHANS = 640
WIDTH = 24
ROWS_HERE = 4
TOKENS = ROWS_HERE * WIDTH
LAST = TOKENS - WIDTH
PARTICLES = 16
HALF = PARTICLES // 2
ROW_DEVS = 32
PER_GROUP = CHANS // GROUPS
SLICE = CHANS // PARTICLES
COUNT = ROWS_HERE * ROW_DEVS * WIDTH * PER_GROUP
LANES = 128
KERNEL_ROWS = 9 * CHANS // ROW_DEVS
TAIL = KERNEL_ROWS - LANES
QUERY_BLOCKS = 3
SLOT = TOKENS + 16

PART = ("x", "z_lo", "core")
CHIPS = ("x", "z_lo")
ROWS = ("z_hi", "y")

NT = (((1,), (1,)), ((), ()))
F32 = jnp.float32
BF16 = jnp.bfloat16
SMEM = pl.BlockSpec(memory_space=pltpu.SMEM)
VMEM = pl.BlockSpec(memory_space=pltpu.VMEM)
ANY = pl.BlockSpec(memory_space=pl.ANY)


def call(kernel, out_shape, in_specs, flops, size, vmem=16, scratch=()):
    out_specs = jax.tree.map(lambda _: VMEM, out_shape)
    return pl.pallas_call(
        kernel,
        out_shape=out_shape,
        in_specs=in_specs,
        out_specs=out_specs,
        scratch_shapes=list(scratch),
        compiler_params=pltpu.CompilerParams(vmem_limit_bytes=vmem * 1024 * 1024),
        cost_estimate=pl.CostEstimate(flops=flops, bytes_accessed=size, transcendentals=0),
    )


def shaped(*shape, dtype=BF16):
    return jax.ShapeDtypeStruct(shape, dtype)


def iota(shape, dim):
    return lax.broadcasted_iota(jnp.int32, shape, dim)


def exact_dot(a, b):
    return jnp.dot(a, b, precision=lax.Precision.HIGHEST, preferred_element_type=F32)


def group_rows(values):
    fill = [jnp.zeros((1, CHANS), F32)] * (8 - len(values))
    sums = jnp.concatenate([jnp.sum(v, axis=0, keepdims=True) for v in values] + fill, axis=0)
    squares = [jnp.sum(v * v, axis=0, keepdims=True) for v in values] + fill
    squares = jnp.concatenate(squares, axis=0)
    chan, lane = iota((CHANS, LANES), 0), iota((CHANS, LANES), 1)
    first = ((chan >= lane * PER_GROUP) & (chan < (lane + 1) * PER_GROUP)).astype(F32)
    other = lane - GROUPS
    second = ((chan >= other * PER_GROUP) & (chan < (other + 1) * PER_GROUP)).astype(F32)
    return exact_dot(sums, first) + exact_dot(squares, second)


def mean_and_inverse(totals):
    lane, chan = iota((LANES, CHANS), 0), iota((LANES, CHANS), 1)
    first = ((chan >= lane * PER_GROUP) & (chan < (lane + 1) * PER_GROUP)).astype(F32)
    other = lane - GROUPS
    second = ((chan >= other * PER_GROUP) & (chan < (other + 1) * PER_GROUP)).astype(F32)
    mean = exact_dot(totals, first) * (1.0 / COUNT)
    square = exact_dot(totals, second) * (1.0 / COUNT)
    return mean, lax.rsqrt(square - mean * mean + 1e-05)


def thirds(value):
    parts = []
    for _ in range(3):
        top = value.astype(BF16).astype(F32)
        parts.append(top)
        value = value - top
    return parts


def spread_kernel(x_ref, out_ref, first_ref, last_ref):
    out_ref[...] = jnp.broadcast_to(x_ref[...][None], out_ref.shape)
    wide = x_ref[...].astype(F32)
    first_ref[...] = wide[:WIDTH].astype(BF16)
    last_ref[...] = wide[LAST:].astype(BF16)


def join_kernel(mine_ref, opposite_ref, _, out_ref):
    out_ref[0] = mine_ref[...]
    out_ref[1] = opposite_ref[...]


def pick_kernel(place_ref, w_ref, out_ref):
    row, col = iota((48, CHANS), 0), iota((48, CHANS), 1)
    chosen = ((col == row + place_ref[0] * SLICE) & (row < SLICE)).astype(F32).astype(BF16)
    picked = lax.dot_general(chosen, w_ref[...], NT, preferred_element_type=F32)
    rest = jnp.concatenate([picked[:, LANES:], jnp.zeros((48, LANES - TAIL), F32)], axis=1)
    turned = pltpu.roll(pltpu.roll(rest, 48 - 20, 0), 64, 1)
    row, lane = iota((32, LANES), 0), iota((32, LANES), 1)
    low = jnp.where(lane < 64, rest[:32], turned[:32])
    out_ref[:SLICE] = picked[:SLICE, :LANES]
    out_ref[SLICE:] = jnp.where(row < 20, low, 0.0)


def slots_kernel(x_ref, part_ref, _, out_ref):
    values = [x_ref[j].astype(F32) for j in range(HALF)]
    first, second, third = thirds(group_rows(values))
    row, lane = iota((8, LANES), 0), iota((8, LANES), 1)
    third = jnp.where(lane < 64, third, pltpu.roll(pltpu.roll(third, 4, 0), 64, 1))
    third = jnp.where(row < 4, third, 0.0)
    rest = jnp.zeros((24, LANES), F32)
    sums = pltpu.roll(jnp.concatenate([first + pltpu.roll(second, 64, 1), rest], axis=0), 20, 0)
    sums = sums + pltpu.roll(jnp.concatenate([third, rest], axis=0), 28, 0)
    slot = jnp.concatenate([part_ref[:SLICE], part_ref[SLICE:] + sums], axis=0).astype(BF16)
    out_ref[...] = jnp.broadcast_to(slot[None], out_ref.shape)


def total_kernel(x_ref, out_ref):
    total = jnp.zeros((32, LANES), F32)
    for r in range(ROW_DEVS):
        total = total + x_ref[r].astype(F32)[SLICE:]
    two, third = pltpu.roll(total, 12, 0)[:8], pltpu.roll(total, 4, 0)[:8]
    row, lane = iota((8, LANES), 0), iota((8, LANES), 1)
    third = jnp.where(row < 4, third, pltpu.roll(pltpu.roll(third, 4, 0), 64, 1))
    out_ref[...] = jnp.where(lane < 64, two + pltpu.roll(two, 64, 1) + third, 0.0)


PLACE = {1: 0, 0: 1, 2: 2}


def weights_kernel(x_ref, out_ref, flat_ref, tall_ref):
    flat_ref[...] = jnp.zeros_like(flat_ref)
    row, lane = iota((SLICE, LANES), 0), iota((SLICE, LANES), 1)
    for r in range(ROW_DEVS):
        at = r * KERNEL_ROWS
        block, off = at // LANES, at % LANES
        slot = x_ref[r].astype(F32)
        low = jnp.concatenate([slot[SLICE:], jnp.zeros((8, LANES), F32)], axis=0)
        rest = jnp.where(row < 20, low, pltpu.roll(pltpu.roll(low, 20, 0), 64, 1))
        rest = jnp.where(lane < TAIL, rest, 0.0)
        wide = jnp.concatenate([slot[:SLICE], rest, jnp.zeros((SLICE, LANES), F32)], axis=1)
        if off:
            wide = pltpu.roll(wide, off, 1)
        spot = slice(block * LANES, (block + 3) * LANES)
        flat_ref[:, spot] = flat_ref[:, spot] + wide
    tall_ref[...] = jnp.zeros_like(tall_ref)
    for a in range(3):
        for b in range(3):
            tap = 3 * a + b
            top = a * LANES + PLACE[b] * SLICE
            tall_ref[top : top + SLICE, :] = flat_ref[:, tap * CHANS : (tap + 1) * CHANS]
    out_ref[...] = tall_ref[...].astype(BF16)


def spot(place_ref, q):
    return lax.rem(lax.rem(q, 2) + place_ref[1], 2) * HALF + q // 2


def silu(v):
    half = 0.5 * v
    return half + half * jnp.tanh(half)


def across(full):
    rows = full.shape[0]
    at = lax.rem(iota((rows, LANES), 0), WIDTH)
    left = pltpu.roll(pltpu.roll(full, 1, 0), LANES - SLICE, 1)
    right = pltpu.roll(pltpu.roll(full, rows - 1, 0), LANES - 2 * SLICE, 1)
    total = full + jnp.where(at == 0, 0.0, left) + jnp.where(at == WIDTH - 1, 0.0, right)
    return jnp.where(iota((rows, LANES), 1) < SLICE, total, 0.0)


def packed(value):
    n = value.shape[0] // 3
    out = value[:n]
    for t in (1, 2):
        out = out + pltpu.roll(value[n * t : n * (t + 1)], SLICE * t, 1)
    return out


STEPS = (0, 1, 3, 2)


def beside(place_ref, j):
    dx = lax.rem(j // 2 + 4 - place_ref[2], 4)
    dz = lax.rem(j % 2 + place_ref[3], 2)
    return 2 * jnp.where(dx == 2, 3, jnp.where(dx == 3, 2, dx)) + dz


def conv_kernel(place_ref, anc_ref, scale_ref, shift_ref, w_ref, *refs):
    totals, slabs, edges, (out_ref, done_ref) = refs[:2], refs[2:4], refs[4:6], refs[6:]
    mean, inverse = mean_and_inverse(jnp.concatenate([ref[...] for ref in totals], axis=0))
    gain = inverse * (1.0 + scale_ref[...])
    bias = shift_ref[...] - mean * gain
    row, col = iota((LANES, CHANS), 0), iota((LANES, CHANS), 1)
    chosen = ((col == row + place_ref[0] * SLICE) & (row < SLICE)).astype(F32).astype(BF16)
    weights = w_ref[...]
    top, bottom = place_ref[4] == 0, place_ref[4] == ROW_DEVS - 1
    each = 2
    for step in range(PARTICLES // each):
        active, raw = [], []
        for n in range(step * each, (step + 1) * each):
            which, j = n // HALF, n % HALF
            x = slabs[which][j]
            raw.append(x)
            act = lambda v: silu(v.astype(F32) * gain[n : n + 1] + bias[n : n + 1])
            at = beside(place_ref, j)
            above, below = act(edges[which][at, 0]), act(edges[which][at, 1])
            active += [jnp.where(top, 0.0, above), act(x), jnp.where(bottom, 0.0, below)]
        active = jnp.concatenate(active, axis=0).astype(BF16)
        raw = jnp.concatenate(raw, axis=0)
        taps = lax.dot_general(active, weights, NT, preferred_element_type=F32)
        field = lax.dot_general(raw, chosen, NT, preferred_element_type=F32)
        for k in range(each):
            at = k * (TOKENS + 2 * WIDTH)
            full = field[k * TOKENS : (k + 1) * TOKENS]
            for a in range(3):
                rows = slice(at + a * WIDTH, at + a * WIDTH + TOKENS)
                full = full + taps[rows, a * LANES : (a + 1) * LANES]
            done_ref[step * each + k] = packed(across(full)).astype(BF16)
    for p in range(PARTICLES):
        out_ref[p] = done_ref[spot(place_ref, anc_ref[p])]


def gather_kernel(x_ref, resid_ref, out_ref, wide_ref):
    lane = iota((32, LANES), 1)
    for t in range(3):
        blocks = [jnp.zeros((32, LANES), F32) for _ in range(CHANS // LANES)]
        for p in range(PARTICLES):
            block, off = (p * SLICE) // LANES, (p * SLICE) % LANES
            turn = (off - t * SLICE) % LANES
            piece = x_ref[p].astype(F32)
            if turn:
                piece = pltpu.roll(piece, turn, 1)
            end = off + SLICE
            blocks[block] = jnp.where((lane >= off) & (lane < end), piece, blocks[block])
            if end > LANES:
                blocks[block + 1] = jnp.where(lane < end - LANES, piece, blocks[block + 1])
        for n, value in enumerate(blocks):
            wide_ref[32 * t : 32 * (t + 1), n * LANES : (n + 1) * LANES] = value
    wide = wide_ref[...]
    resid_ref[...] = wide.astype(BF16)
    out_ref[...] = jnp.broadcast_to(group_rows([wide])[None], out_ref.shape)


def project_kernel(totals_ref, resid_ref, w_ref, out_ref, both_ref):
    mean, inverse = mean_and_inverse(jnp.sum(totals_ref[...], axis=0))
    normed = ((resid_ref[...].astype(F32) - mean[:1]) * inverse[:1]).astype(BF16)
    both_ref[...] = jnp.dot(normed, w_ref[...], preferred_element_type=F32)
    low = iota((TOKENS, LANES), 1) < 64
    low_s = iota((16, LANES), 1) < 64
    for pair in range(HEADS // 2):
        q, k, v = (
            both_ref[:, n * CHANS + pair * LANES : n * CHANS + (pair + 1) * LANES] for n in range(3)
        )
        q_turn, k_turn, v_turn = (pltpu.roll(x, 64, 1) for x in (q, k, v))
        mixed = (jnp.where(low, k, v_turn), jnp.where(low, k_turn, v))
        lows, highs = (q, q_turn), (q_turn, q)
        for side in range(2):
            keys_values = mixed[side].astype(BF16)
            for b in range(QUERY_BLOCKS):
                slot = (2 * pair + side) * QUERY_BLOCKS + b
                at = 32 * b
                two = jnp.where(low_s, lows[side][at : at + 16], highs[side][at + 16 : at + 32])
                out_ref[slot, :TOKENS] = keys_values
                out_ref[slot, TOKENS:] = two.astype(BF16)
    for slot in range(HEADS * QUERY_BLOCKS, ROW_DEVS):
        out_ref[slot] = jnp.zeros((SLOT, LANES), BF16)


def attend_kernel(x_ref, out_ref, keys_ref, ones_ref, query_ref):
    low = iota((TOKENS, LANES), 1) < 64
    for r in range(ROW_DEVS):
        block = x_ref[r, :TOKENS]
        keys_ref[r * TOKENS : (r + 1) * TOKENS] = block
        ones_ref[r * TOKENS : (r + 1) * TOKENS] = jnp.where(low, jnp.ones_like(block), block)
        query_ref[r * 16 : (r + 1) * 16] = x_ref[r, TOKENS:].astype(F32)
    size, chunk = 512, 1024
    low_q = iota((size, LANES), 1) < 64
    factor = 0.125 * 1.4426950408889634
    done = []
    for side in range(2):
        here = query_ref[...]
        turned = here if side == 0 else pltpu.roll(here, 64, 1)
        query = jnp.where(low_q, turned, 0.0).astype(BF16)
        top = result = None
        for c in range(0, ROW_DEVS * TOKENS, chunk):
            span = slice(c, c + chunk)
            scores = lax.dot_general(query, keys_ref[span], NT, preferred_element_type=F32)
            higher = jnp.max(scores, axis=1, keepdims=True)
            if c:
                higher = jnp.maximum(higher, top)
            weights = jnp.exp2((scores - higher) * factor).astype(BF16)
            new = jnp.dot(weights, ones_ref[span], preferred_element_type=F32)
            result = result * jnp.exp2((top - higher) * factor) + new if c else new
            top = higher
        done.append((result, pltpu.roll(result, 64, 1)))
    (first, first_turned), (second, second_turned) = done
    both = jnp.where(low_q, first_turned / first, second / second_turned).astype(BF16)
    for r in range(ROW_DEVS):
        out_ref[r] = both[r * 16 : (r + 1) * 16]


def output_kernel(x_ref, resid_ref, w_ref, out_ref, wide_ref):
    low = iota((16, LANES), 1) < 64
    for pair in range(HEADS // 2):
        for b in range(QUERY_BLOCKS):
            first = x_ref[2 * pair * QUERY_BLOCKS + b].astype(F32)
            second = x_ref[(2 * pair + 1) * QUERY_BLOCKS + b].astype(F32)
            cols = slice(pair * LANES, (pair + 1) * LANES)
            at = 32 * b
            wide_ref[at : at + 16, cols] = jnp.where(low, first, pltpu.roll(second, 64, 1))
            wide_ref[at + 16 : at + 32, cols] = jnp.where(low, pltpu.roll(first, 64, 1), second)
    mixed = wide_ref[...].astype(BF16)
    product = jnp.dot(mixed, w_ref[...], preferred_element_type=F32)
    out_ref[...] = (resid_ref[...].astype(F32) + product).astype(BF16)


def exchange(values, axes):
    return lax.all_to_all(values, axes, split_axis=0, concat_axis=0, tiled=True)


def per_device(latent, ada_scale, ada_shift, conv_weight, qkv_weight, out_weight, ancestors):
    slab = latent.reshape(TOKENS, CHANS)
    particle = lax.axis_index(PART).astype(jnp.int32)
    place = jnp.stack(
        [particle] + [lax.axis_index(a).astype(jnp.int32) for a in ("core", "x", "z_lo", ROWS)]
    )

    swap = [(0, 1), (1, 0)]
    row = shaped(WIDTH, CHANS)
    copies, first, last = call(
        spread_kernel, [shaped(HALF, TOKENS, CHANS), row, row], [VMEM], 10**5, 10**6
    )(slab)
    here = exchange(copies, CHIPS)
    slabs = [here, lax.ppermute(here, "core", swap)]
    above = lax.ppermute(last, ROWS, [(i, i + 1) for i in range(ROW_DEVS - 1)])
    below = lax.ppermute(first, ROWS, [(i + 1, i) for i in range(ROW_DEVS - 1)])
    mine = jnp.stack([above, below])
    opposite = lax.ppermute(mine, "z_lo", swap)

    columns = call(pick_kernel, shaped(72, LANES, dtype=F32), [SMEM, VMEM], 10**7, 10**6, vmem=8)(
        place, conv_weight
    )
    picked = call(slots_kernel, shaped(ROW_DEVS, 72, LANES), [VMEM, VMEM, ANY], 10**7, 10**6)(
        here, columns, opposite
    )
    pair = call(join_kernel, shaped(2, 2, WIDTH, CHANS), [VMEM, VMEM, ANY], 10**5, 10**6)(
        mine, opposite, picked
    )
    turns = [[((i + d) % 4, i) for i in range(4)] for d in STEPS[1:]]
    edges = jnp.concatenate([pair] + [lax.ppermute(pair, "x", turn) for turn in turns])
    edges = [edges, lax.ppermute(edges, "core", swap)]
    picked = exchange(picked, ROWS)
    totals = call(total_kernel, shaped(HALF, LANES, dtype=F32), [VMEM], 10**5, 10**5)(picked)
    totals = [totals, lax.ppermute(totals, "core", swap)]
    weights = call(
        weights_kernel,
        shaped(3 * LANES, CHANS),
        [VMEM],
        10**6,
        10**6,
        scratch=(
            pltpu.VMEM((SLICE, 9 * CHANS + 2 * LANES), F32),
            pltpu.VMEM((3 * LANES, CHANS), F32),
        ),
    )(picked)
    pieces = call(
        conv_kernel,
        shaped(PARTICLES, 32, LANES),
        [SMEM, SMEM] + [VMEM] * 9,
        2 * 10**9,
        4 * 10**6,
        vmem=20,
        scratch=(pltpu.VMEM((PARTICLES, 32, LANES), BF16),),
    )(place, ancestors, ada_scale[None], ada_shift[None], weights, *totals, *slabs, *edges)
    pieces = exchange(pieces, PART)

    resid, sums = call(
        gather_kernel,
        [shaped(TOKENS, CHANS), shaped(ROW_DEVS, 8, LANES, dtype=F32)],
        [VMEM],
        10**6,
        10**6,
        scratch=(pltpu.VMEM((TOKENS, CHANS), F32),),
    )(pieces)
    sums = exchange(sums, ROWS)
    slots = call(
        project_kernel,
        shaped(ROW_DEVS, SLOT, LANES),
        [VMEM] * 3,
        3 * 10**8,
        4 * 10**6,
        scratch=(pltpu.VMEM((TOKENS, 3 * CHANS), F32),),
    )(sums, resid, qkv_weight)
    slots = exchange(slots, ROWS)
    rows = ROW_DEVS * TOKENS
    mixed = call(
        attend_kernel,
        shaped(ROW_DEVS, 16, LANES),
        [VMEM],
        2 * 10**9,
        2 * 10**6,
        vmem=32,
        scratch=(
            pltpu.VMEM((rows, LANES), BF16),
            pltpu.VMEM((rows, LANES), BF16),
            pltpu.VMEM((ROW_DEVS * 16, LANES), F32),
        ),
    )(slots)
    mixed = exchange(mixed, ROWS)
    block = call(
        output_kernel,
        shaped(TOKENS, CHANS),
        [VMEM] * 3,
        10**8,
        10**6,
        scratch=(pltpu.VMEM((TOKENS, CHANS), F32),),
    )(mixed, resid, out_weight)
    return block.reshape(1, ROWS_HERE, WIDTH, CHANS)


def solution(mesh):
    split = Mesh(mesh.devices.reshape(4, 2, 2, 4, 8), PART + ROWS)
    placed = (P(PART, ROWS, None, None), P(), P(), P(ROWS, None), P(), P(), P())
    return jax.shard_map(
        per_device,
        mesh=split,
        in_specs=placed,
        out_specs=P(PART, ROWS, None, None),
        check_vma=False,
    )
```

```python
import jax
import jax.numpy as jnp
from jax import lax
from jax.experimental import pallas as pl
from jax.experimental.pallas import tpu as pltpu
from jax.sharding import Mesh
from jax.sharding import PartitionSpec as P

HEADS = 10
GROUPS = 32
CHANS = 640
WIDTH = 24
ROWS_HERE = 4
TOKENS = ROWS_HERE * WIDTH
LAST = TOKENS - WIDTH
ALL = TOKENS + 2 * WIDTH
PARTICLES = 16
HALF = PARTICLES // 2
ROW_DEVS = 32
PER_GROUP = CHANS // GROUPS
SLICE = CHANS // PARTICLES
COUNT = ROWS_HERE * ROW_DEVS * WIDTH * PER_GROUP
LANES = 128
KERNEL_ROWS = 9 * CHANS // ROW_DEVS
TAIL = KERNEL_ROWS - LANES
QUERY_BLOCKS = 3
SLOT = TOKENS + 16

PART = ("x", "z_lo", "core")
CHIPS = ("x", "z_lo")
ROWS = ("z_hi", "y")

NT = (((1,), (1,)), ((), ()))
F32 = jnp.float32
BF16 = jnp.bfloat16
SMEM = pl.BlockSpec(memory_space=pltpu.SMEM)
VMEM = pl.BlockSpec(memory_space=pltpu.VMEM)
ANY = pl.BlockSpec(memory_space=pl.ANY)


def call(kernel, out_shape, in_specs, flops, size, vmem=16, scratch=()):
    out_specs = jax.tree.map(lambda _: VMEM, out_shape)
    return pl.pallas_call(
        kernel,
        out_shape=out_shape,
        in_specs=in_specs,
        out_specs=out_specs,
        scratch_shapes=list(scratch),
        compiler_params=pltpu.CompilerParams(vmem_limit_bytes=vmem * 1024 * 1024),
        cost_estimate=pl.CostEstimate(flops=flops, bytes_accessed=size, transcendentals=0),
    )


def shaped(*shape, dtype=BF16):
    return jax.ShapeDtypeStruct(shape, dtype)


def iota(shape, dim):
    return lax.broadcasted_iota(jnp.int32, shape, dim)


def exact_dot(a, b):
    return jnp.dot(a, b, precision=lax.Precision.HIGHEST, preferred_element_type=F32)


def group_rows(values):
    fill = [jnp.zeros((1, CHANS), F32)] * (8 - len(values))
    sums = jnp.concatenate([jnp.sum(v, axis=0, keepdims=True) for v in values] + fill, axis=0)
    squares = [jnp.sum(v * v, axis=0, keepdims=True) for v in values] + fill
    squares = jnp.concatenate(squares, axis=0)
    chan, lane = iota((CHANS, LANES), 0), iota((CHANS, LANES), 1)
    first = ((chan >= lane * PER_GROUP) & (chan < (lane + 1) * PER_GROUP)).astype(F32)
    other = lane - GROUPS
    second = ((chan >= other * PER_GROUP) & (chan < (other + 1) * PER_GROUP)).astype(F32)
    return exact_dot(sums, first) + exact_dot(squares, second)


def mean_and_inverse(totals):
    lane, chan = iota((LANES, CHANS), 0), iota((LANES, CHANS), 1)
    first = ((chan >= lane * PER_GROUP) & (chan < (lane + 1) * PER_GROUP)).astype(F32)
    other = lane - GROUPS
    second = ((chan >= other * PER_GROUP) & (chan < (other + 1) * PER_GROUP)).astype(F32)
    mean = exact_dot(totals, first) * (1.0 / COUNT)
    square = exact_dot(totals, second) * (1.0 / COUNT)
    return mean, lax.rsqrt(square - mean * mean + 1e-05)


def thirds(value):
    parts = []
    for _ in range(3):
        top = value.astype(BF16).astype(F32)
        parts.append(top)
        value = value - top
    return parts


def spread_kernel(x_ref, out_ref, first_ref, last_ref):
    out_ref[...] = jnp.broadcast_to(x_ref[...][None], out_ref.shape)
    wide = x_ref[...].astype(F32)
    first_ref[...] = wide[:WIDTH].astype(BF16)
    last_ref[...] = wide[LAST:].astype(BF16)


def join_kernel(mine_ref, opposite_ref, _, out_ref):
    out_ref[0] = mine_ref[...]
    out_ref[1] = opposite_ref[...]


def pick_kernel(place_ref, w_ref, out_ref):
    row, col = iota((48, CHANS), 0), iota((48, CHANS), 1)
    chosen = ((col == row + place_ref[0] * SLICE) & (row < SLICE)).astype(F32).astype(BF16)
    picked = lax.dot_general(chosen, w_ref[...], NT, preferred_element_type=F32)
    rest = jnp.concatenate([picked[:, LANES:], jnp.zeros((48, LANES - TAIL), F32)], axis=1)
    turned = pltpu.roll(pltpu.roll(rest, 48 - 20, 0), 64, 1)
    row, lane = iota((32, LANES), 0), iota((32, LANES), 1)
    low = jnp.where(lane < 64, rest[:32], turned[:32])
    out_ref[:SLICE] = picked[:SLICE, :LANES]
    out_ref[SLICE:] = jnp.where(row < 20, low, 0.0)


def slots_kernel(x_ref, part_ref, _, out_ref):
    values = [x_ref[j].astype(F32) for j in range(HALF)]
    first, second, third = thirds(group_rows(values))
    row, lane = iota((8, LANES), 0), iota((8, LANES), 1)
    third = jnp.where(lane < 64, third, pltpu.roll(pltpu.roll(third, 4, 0), 64, 1))
    third = jnp.where(row < 4, third, 0.0)
    rest = jnp.zeros((24, LANES), F32)
    sums = pltpu.roll(jnp.concatenate([first + pltpu.roll(second, 64, 1), rest], axis=0), 20, 0)
    sums = sums + pltpu.roll(jnp.concatenate([third, rest], axis=0), 28, 0)
    slot = jnp.concatenate([part_ref[:SLICE], part_ref[SLICE:] + sums], axis=0).astype(BF16)
    out_ref[...] = jnp.broadcast_to(slot[None], out_ref.shape)


def total_kernel(x_ref, out_ref):
    total = jnp.zeros((32, LANES), F32)
    for r in range(ROW_DEVS):
        total = total + x_ref[r].astype(F32)[SLICE:]
    two, third = pltpu.roll(total, 12, 0)[:8], pltpu.roll(total, 4, 0)[:8]
    row, lane = iota((8, LANES), 0), iota((8, LANES), 1)
    third = jnp.where(row < 4, third, pltpu.roll(pltpu.roll(third, 4, 0), 64, 1))
    out_ref[...] = jnp.where(lane < 64, two + pltpu.roll(two, 64, 1) + third, 0.0)


PLACE = {1: 0, 0: 1, 2: 2}


def weights_kernel(x_ref, out_ref, flat_ref, tall_ref):
    flat_ref[...] = jnp.zeros_like(flat_ref)
    row, lane = iota((SLICE, LANES), 0), iota((SLICE, LANES), 1)
    for r in range(ROW_DEVS):
        at = r * KERNEL_ROWS
        block, off = at // LANES, at % LANES
        slot = x_ref[r].astype(F32)
        low = jnp.concatenate([slot[SLICE:], jnp.zeros((8, LANES), F32)], axis=0)
        rest = jnp.where(row < 20, low, pltpu.roll(pltpu.roll(low, 20, 0), 64, 1))
        rest = jnp.where(lane < TAIL, rest, 0.0)
        wide = jnp.concatenate([slot[:SLICE], rest, jnp.zeros((SLICE, LANES), F32)], axis=1)
        if off:
            wide = pltpu.roll(wide, off, 1)
        spot = slice(block * LANES, (block + 3) * LANES)
        flat_ref[:, spot] = flat_ref[:, spot] + wide
    tall_ref[...] = jnp.zeros_like(tall_ref)
    for a in range(3):
        for b in range(3):
            tap = 3 * a + b
            top = a * LANES + PLACE[b] * SLICE
            tall_ref[top : top + SLICE, :] = flat_ref[:, tap * CHANS : (tap + 1) * CHANS]
    out_ref[...] = tall_ref[...].astype(BF16)


def spot(place_ref, q):
    return lax.rem(lax.rem(q, 2) + place_ref[1], 2) * HALF + q // 2


def silu(v):
    half = 0.5 * v
    return half + half * jnp.tanh(half)


def across(full):
    rows = full.shape[0]
    at = lax.rem(iota((rows, LANES), 0), WIDTH)
    left = pltpu.roll(pltpu.roll(full, 1, 0), LANES - SLICE, 1)
    right = pltpu.roll(pltpu.roll(full, rows - 1, 0), LANES - 2 * SLICE, 1)
    total = full + jnp.where(at == 0, 0.0, left) + jnp.where(at == WIDTH - 1, 0.0, right)
    return jnp.where(iota((rows, LANES), 1) < SLICE, total, 0.0)


def packed(value):
    n = value.shape[0] // 3
    out = value[:n]
    for t in (1, 2):
        out = out + pltpu.roll(value[n * t : n * (t + 1)], SLICE * t, 1)
    return out


STEPS = (0, 1, 3, 2)


def beside(place_ref, j):
    dx = lax.rem(j // 2 + 4 - place_ref[2], 4)
    dz = lax.rem(j % 2 + place_ref[3], 2)
    return 2 * jnp.where(dx == 2, 3, jnp.where(dx == 3, 2, dx)) + dz


def merge_kernel(place_ref, x_ref, edge_ref, out_ref):
    for j in range(HALF):
        at = beside(place_ref, j)
        parts = [x_ref[j], edge_ref[at, 0], edge_ref[at, 1]]
        out_ref[j] = jnp.concatenate([v.astype(F32) for v in parts], axis=0).astype(BF16)


def conv_kernel(place_ref, anc_ref, scale_ref, shift_ref, w_ref, *refs):
    totals, slabs, (out_ref, done_ref) = refs[:2], refs[2:4], refs[4:]
    mean, inverse = mean_and_inverse(jnp.concatenate([ref[...] for ref in totals], axis=0))
    gain = inverse * (1.0 + scale_ref[...])
    bias = shift_ref[...] - mean * gain
    row, col = iota((LANES, CHANS), 0), iota((LANES, CHANS), 1)
    chosen = ((col == row + place_ref[0] * SLICE) & (row < SLICE)).astype(F32).astype(BF16)
    weights = w_ref[...]
    top, bottom = place_ref[4] == 0, place_ref[4] == ROW_DEVS - 1
    each = 2
    for step in range(PARTICLES // each):
        active, raw = [], []
        for n in range(step * each, (step + 1) * each):
            x = slabs[n // HALF][n % HALF]
            raw.append(x[:TOKENS])
            active.append(silu(x.astype(F32) * gain[n : n + 1] + bias[n : n + 1]).astype(BF16))
        active = jnp.concatenate(active, axis=0)
        raw = jnp.concatenate(raw, axis=0)
        taps = lax.dot_general(active, weights, NT, preferred_element_type=F32)
        field = lax.dot_general(raw, chosen, NT, preferred_element_type=F32)
        for k in range(each):
            here = taps[k * ALL : (k + 1) * ALL]
            t0, t1, t2 = (here[:, a * LANES : (a + 1) * LANES] for a in range(3))
            above = jnp.where(top, 0.0, t0[TOKENS : TOKENS + WIDTH])
            below = jnp.where(bottom, 0.0, t2[TOKENS + WIDTH :])
            full = field[k * TOKENS : (k + 1) * TOKENS] + t1[:TOKENS]
            full = full + jnp.concatenate([above, t0[:LAST]], axis=0)
            full = full + jnp.concatenate([t2[WIDTH:TOKENS], below], axis=0)
            done_ref[step * each + k] = packed(across(full)).astype(BF16)
    for p in range(PARTICLES):
        out_ref[p] = done_ref[spot(place_ref, anc_ref[p])]


def gather_kernel(x_ref, resid_ref, out_ref, wide_ref):
    lane = iota((32, LANES), 1)
    for t in range(3):
        blocks = [jnp.zeros((32, LANES), F32) for _ in range(CHANS // LANES)]
        for p in range(PARTICLES):
            block, off = (p * SLICE) // LANES, (p * SLICE) % LANES
            turn = (off - t * SLICE) % LANES
            piece = x_ref[p].astype(F32)
            if turn:
                piece = pltpu.roll(piece, turn, 1)
            end = off + SLICE
            blocks[block] = jnp.where((lane >= off) & (lane < end), piece, blocks[block])
            if end > LANES:
                blocks[block + 1] = jnp.where(lane < end - LANES, piece, blocks[block + 1])
        for n, value in enumerate(blocks):
            wide_ref[32 * t : 32 * (t + 1), n * LANES : (n + 1) * LANES] = value
    wide = wide_ref[...]
    resid_ref[...] = wide.astype(BF16)
    out_ref[...] = jnp.broadcast_to(group_rows([wide])[None], out_ref.shape)


def project_kernel(totals_ref, resid_ref, w_ref, out_ref, both_ref):
    mean, inverse = mean_and_inverse(jnp.sum(totals_ref[...], axis=0))
    normed = ((resid_ref[...].astype(F32) - mean[:1]) * inverse[:1]).astype(BF16)
    both_ref[...] = jnp.dot(normed, w_ref[...], preferred_element_type=F32)
    low = iota((TOKENS, LANES), 1) < 64
    low_s = iota((16, LANES), 1) < 64
    for pair in range(HEADS // 2):
        q, k, v = (
            both_ref[:, n * CHANS + pair * LANES : n * CHANS + (pair + 1) * LANES] for n in range(3)
        )
        q_turn, k_turn, v_turn = (pltpu.roll(x, 64, 1) for x in (q, k, v))
        mixed = (jnp.where(low, k, v_turn), jnp.where(low, k_turn, v))
        lows, highs = (q, q_turn), (q_turn, q)
        for side in range(2):
            keys_values = mixed[side].astype(BF16)
            for b in range(QUERY_BLOCKS):
                slot = (2 * pair + side) * QUERY_BLOCKS + b
                at = 32 * b
                two = jnp.where(low_s, lows[side][at : at + 16], highs[side][at + 16 : at + 32])
                out_ref[slot, :TOKENS] = keys_values
                out_ref[slot, TOKENS:] = two.astype(BF16)
    for slot in range(HEADS * QUERY_BLOCKS, ROW_DEVS):
        out_ref[slot] = jnp.zeros((SLOT, LANES), BF16)


def attend_kernel(x_ref, out_ref, keys_ref, ones_ref, query_ref):
    low = iota((TOKENS, LANES), 1) < 64
    for r in range(ROW_DEVS):
        block = x_ref[r, :TOKENS]
        keys_ref[r * TOKENS : (r + 1) * TOKENS] = block
        ones_ref[r * TOKENS : (r + 1) * TOKENS] = jnp.where(low, jnp.ones_like(block), block)
        query_ref[r * 16 : (r + 1) * 16] = x_ref[r, TOKENS:].astype(F32)
    size, chunk = 512, 1024
    low_q = iota((size, LANES), 1) < 64
    factor = 0.125 * 1.4426950408889634
    done = []
    for side in range(2):
        here = query_ref[...]
        turned = here if side == 0 else pltpu.roll(here, 64, 1)
        query = jnp.where(low_q, turned, 0.0).astype(BF16)
        top = result = None
        for c in range(0, ROW_DEVS * TOKENS, chunk):
            span = slice(c, c + chunk)
            scores = lax.dot_general(query, keys_ref[span], NT, preferred_element_type=F32)
            higher = jnp.max(scores, axis=1, keepdims=True)
            if c:
                higher = jnp.maximum(higher, top)
            weights = jnp.exp2((scores - higher) * factor).astype(BF16)
            new = jnp.dot(weights, ones_ref[span], preferred_element_type=F32)
            result = result * jnp.exp2((top - higher) * factor) + new if c else new
            top = higher
        done.append((result, pltpu.roll(result, 64, 1)))
    (first, first_turned), (second, second_turned) = done
    both = jnp.where(low_q, first_turned / first, second / second_turned).astype(BF16)
    for r in range(ROW_DEVS):
        out_ref[r] = both[r * 16 : (r + 1) * 16]


def output_kernel(x_ref, resid_ref, w_ref, out_ref, wide_ref):
    low = iota((16, LANES), 1) < 64
    for pair in range(HEADS // 2):
        for b in range(QUERY_BLOCKS):
            first = x_ref[2 * pair * QUERY_BLOCKS + b].astype(F32)
            second = x_ref[(2 * pair + 1) * QUERY_BLOCKS + b].astype(F32)
            cols = slice(pair * LANES, (pair + 1) * LANES)
            at = 32 * b
            wide_ref[at : at + 16, cols] = jnp.where(low, first, pltpu.roll(second, 64, 1))
            wide_ref[at + 16 : at + 32, cols] = jnp.where(low, pltpu.roll(first, 64, 1), second)
    mixed = wide_ref[...].astype(BF16)
    product = jnp.dot(mixed, w_ref[...], preferred_element_type=F32)
    out_ref[...] = (resid_ref[...].astype(F32) + product).astype(BF16)


def exchange(values, axes):
    return lax.all_to_all(values, axes, split_axis=0, concat_axis=0, tiled=True)


def per_device(latent, ada_scale, ada_shift, conv_weight, qkv_weight, out_weight, ancestors):
    slab = latent.reshape(TOKENS, CHANS)
    particle = lax.axis_index(PART).astype(jnp.int32)
    place = jnp.stack(
        [particle] + [lax.axis_index(a).astype(jnp.int32) for a in ("core", "x", "z_lo", ROWS)]
    )

    swap = [(0, 1), (1, 0)]
    row = shaped(WIDTH, CHANS)
    copies, first, last = call(
        spread_kernel, [shaped(HALF, TOKENS, CHANS), row, row], [VMEM], 10**5, 10**6
    )(slab)
    here = exchange(copies, CHIPS)
    above = lax.ppermute(last, ROWS, [(i, i + 1) for i in range(ROW_DEVS - 1)])
    below = lax.ppermute(first, ROWS, [(i + 1, i) for i in range(ROW_DEVS - 1)])
    mine = jnp.stack([above, below])
    opposite = lax.ppermute(mine, "z_lo", swap)

    columns = call(pick_kernel, shaped(72, LANES, dtype=F32), [SMEM, VMEM], 10**7, 10**6, vmem=8)(
        place, conv_weight
    )
    picked = call(slots_kernel, shaped(ROW_DEVS, 72, LANES), [VMEM, VMEM, ANY], 10**7, 10**6)(
        here, columns, opposite
    )
    pair = call(join_kernel, shaped(2, 2, WIDTH, CHANS), [VMEM, VMEM, ANY], 10**5, 10**6)(
        mine, opposite, picked
    )
    turns = [[((i + d) % 4, i) for i in range(4)] for d in STEPS[1:]]
    edges = jnp.concatenate([pair] + [lax.ppermute(pair, "x", turn) for turn in turns])
    merged = call(merge_kernel, shaped(HALF, ALL, CHANS), [SMEM, VMEM, VMEM], 10**6, 10**6)(
        place, here, edges
    )
    slabs = [merged, lax.ppermute(merged, "core", swap)]
    picked = exchange(picked, ROWS)
    totals = call(total_kernel, shaped(HALF, LANES, dtype=F32), [VMEM], 10**5, 10**5)(picked)
    totals = [totals, lax.ppermute(totals, "core", swap)]
    weights = call(
        weights_kernel,
        shaped(3 * LANES, CHANS),
        [VMEM],
        3 * 10**10,
        10**6,
        scratch=(
            pltpu.VMEM((SLICE, 9 * CHANS + 2 * LANES), F32),
            pltpu.VMEM((3 * LANES, CHANS), F32),
        ),
    )(picked)
    pieces = call(
        conv_kernel,
        shaped(PARTICLES, 32, LANES),
        [SMEM, SMEM] + [VMEM] * 7,
        2 * 10**9,
        4 * 10**6,
        vmem=20,
        scratch=(pltpu.VMEM((PARTICLES, 32, LANES), BF16),),
    )(place, ancestors, ada_scale[None], ada_shift[None], weights, *totals, *slabs)
    pieces = exchange(pieces, PART)

    resid, sums = call(
        gather_kernel,
        [shaped(TOKENS, CHANS), shaped(ROW_DEVS, 8, LANES, dtype=F32)],
        [VMEM],
        10**6,
        10**6,
        scratch=(pltpu.VMEM((TOKENS, CHANS), F32),),
    )(pieces)
    sums = exchange(sums, ROWS)
    slots = call(
        project_kernel,
        shaped(ROW_DEVS, SLOT, LANES),
        [VMEM] * 3,
        3 * 10**8,
        4 * 10**6,
        scratch=(pltpu.VMEM((TOKENS, 3 * CHANS), F32),),
    )(sums, resid, qkv_weight)
    slots = exchange(slots, ROWS)
    rows = ROW_DEVS * TOKENS
    mixed = call(
        attend_kernel,
        shaped(ROW_DEVS, 16, LANES),
        [VMEM],
        2 * 10**9,
        2 * 10**6,
        vmem=32,
        scratch=(
            pltpu.VMEM((rows, LANES), BF16),
            pltpu.VMEM((rows, LANES), BF16),
            pltpu.VMEM((ROW_DEVS * 16, LANES), F32),
        ),
    )(slots)
    mixed = exchange(mixed, ROWS)
    block = call(
        output_kernel,
        shaped(TOKENS, CHANS),
        [VMEM] * 3,
        10**8,
        10**6,
        scratch=(pltpu.VMEM((TOKENS, CHANS), F32),),
    )(mixed, resid, out_weight)
    return block.reshape(1, ROWS_HERE, WIDTH, CHANS)


def solution(mesh):
    split = Mesh(mesh.devices.reshape(4, 2, 2, 4, 8), PART + ROWS)
    placed = (P(PART, ROWS, None, None), P(), P(), P(ROWS, None), P(), P(), P())
    return jax.shard_map(
        per_device,
        mesh=split,
        in_specs=placed,
        out_specs=P(PART, ROWS, None, None),
        check_vma=False,
    )
```

```python
import jax
import jax.numpy as jnp
from jax import lax
from jax.experimental import pallas as pl
from jax.experimental.pallas import tpu as pltpu
from jax.sharding import Mesh
from jax.sharding import PartitionSpec as P

HEADS = 10
GROUPS = 32
CHANS = 640
WIDTH = 24
ROWS_HERE = 4
TOKENS = ROWS_HERE * WIDTH
LAST = TOKENS - WIDTH
ALL = TOKENS + 2 * WIDTH
PARTICLES = 16
HALF = PARTICLES // 2
ROW_DEVS = 32
PER_GROUP = CHANS // GROUPS
SLICE = CHANS // PARTICLES
COUNT = ROWS_HERE * ROW_DEVS * WIDTH * PER_GROUP
LANES = 128
KERNEL_ROWS = 9 * CHANS // ROW_DEVS
TAIL = KERNEL_ROWS - LANES
QUERY_BLOCKS = 3
SLOT = TOKENS + 16

PART = ("x", "z_lo", "core")
CHIPS = ("x", "z_lo")
ROWS = ("z_hi", "y")

NT = (((1,), (1,)), ((), ()))
F32 = jnp.float32
BF16 = jnp.bfloat16
SMEM = pl.BlockSpec(memory_space=pltpu.SMEM)
VMEM = pl.BlockSpec(memory_space=pltpu.VMEM)
ANY = pl.BlockSpec(memory_space=pl.ANY)


def call(kernel, out_shape, in_specs, flops, size, vmem=16, scratch=()):
    out_specs = jax.tree.map(lambda _: VMEM, out_shape)
    return pl.pallas_call(
        kernel,
        out_shape=out_shape,
        in_specs=in_specs,
        out_specs=out_specs,
        scratch_shapes=list(scratch),
        compiler_params=pltpu.CompilerParams(vmem_limit_bytes=vmem * 1024 * 1024),
        cost_estimate=pl.CostEstimate(flops=flops, bytes_accessed=size, transcendentals=0),
    )


def shaped(*shape, dtype=BF16):
    return jax.ShapeDtypeStruct(shape, dtype)


def iota(shape, dim):
    return lax.broadcasted_iota(jnp.int32, shape, dim)


def exact_dot(a, b):
    return jnp.dot(a, b, precision=lax.Precision.HIGHEST, preferred_element_type=F32)


def group_rows(values):
    fill = [jnp.zeros((1, CHANS), F32)] * (8 - len(values))
    sums = jnp.concatenate([jnp.sum(v, axis=0, keepdims=True) for v in values] + fill, axis=0)
    squares = [jnp.sum(v * v, axis=0, keepdims=True) for v in values] + fill
    squares = jnp.concatenate(squares, axis=0)
    chan, lane = iota((CHANS, LANES), 0), iota((CHANS, LANES), 1)
    first = ((chan >= lane * PER_GROUP) & (chan < (lane + 1) * PER_GROUP)).astype(F32)
    other = lane - GROUPS
    second = ((chan >= other * PER_GROUP) & (chan < (other + 1) * PER_GROUP)).astype(F32)
    return exact_dot(sums, first) + exact_dot(squares, second)


def mean_and_inverse(totals):
    lane, chan = iota((LANES, CHANS), 0), iota((LANES, CHANS), 1)
    first = ((chan >= lane * PER_GROUP) & (chan < (lane + 1) * PER_GROUP)).astype(F32)
    other = lane - GROUPS
    second = ((chan >= other * PER_GROUP) & (chan < (other + 1) * PER_GROUP)).astype(F32)
    mean = exact_dot(totals, first) * (1.0 / COUNT)
    square = exact_dot(totals, second) * (1.0 / COUNT)
    return mean, lax.rsqrt(square - mean * mean + 1e-05)


def thirds(value):
    parts = []
    for _ in range(3):
        top = value.astype(BF16).astype(F32)
        parts.append(top)
        value = value - top
    return parts


def spread_kernel(x_ref, out_ref, first_ref, last_ref):
    out_ref[...] = jnp.broadcast_to(x_ref[...][None], out_ref.shape)
    wide = x_ref[...].astype(F32)
    first_ref[...] = wide[:WIDTH].astype(BF16)
    last_ref[...] = wide[LAST:].astype(BF16)


def join_kernel(mine_ref, opposite_ref, _, out_ref):
    out_ref[0] = mine_ref[...]
    out_ref[1] = opposite_ref[...]


def pick_kernel(place_ref, w_ref, out_ref):
    row, col = iota((48, CHANS), 0), iota((48, CHANS), 1)
    chosen = ((col == row + place_ref[0] * SLICE) & (row < SLICE)).astype(F32).astype(BF16)
    picked = lax.dot_general(chosen, w_ref[...], NT, preferred_element_type=F32)
    rest = jnp.concatenate([picked[:, LANES:], jnp.zeros((48, LANES - TAIL), F32)], axis=1)
    turned = pltpu.roll(pltpu.roll(rest, 48 - 20, 0), 64, 1)
    row, lane = iota((32, LANES), 0), iota((32, LANES), 1)
    low = jnp.where(lane < 64, rest[:32], turned[:32])
    out_ref[:SLICE] = picked[:SLICE, :LANES]
    out_ref[SLICE:] = jnp.where(row < 20, low, 0.0)


def slots_kernel(x_ref, part_ref, _, out_ref):
    values = [x_ref[j].astype(F32) for j in range(HALF)]
    first, second, third = thirds(group_rows(values))
    row, lane = iota((8, LANES), 0), iota((8, LANES), 1)
    third = jnp.where(lane < 64, third, pltpu.roll(pltpu.roll(third, 4, 0), 64, 1))
    third = jnp.where(row < 4, third, 0.0)
    rest = jnp.zeros((24, LANES), F32)
    sums = pltpu.roll(jnp.concatenate([first + pltpu.roll(second, 64, 1), rest], axis=0), 20, 0)
    sums = sums + pltpu.roll(jnp.concatenate([third, rest], axis=0), 28, 0)
    slot = jnp.concatenate([part_ref[:SLICE], part_ref[SLICE:] + sums], axis=0).astype(BF16)
    out_ref[...] = jnp.broadcast_to(slot[None], out_ref.shape)


def total_kernel(x_ref, out_ref):
    total = jnp.zeros((32, LANES), F32)
    for r in range(ROW_DEVS):
        total = total + x_ref[r].astype(F32)[SLICE:]
    two, third = pltpu.roll(total, 12, 0)[:8], pltpu.roll(total, 4, 0)[:8]
    row, lane = iota((8, LANES), 0), iota((8, LANES), 1)
    third = jnp.where(row < 4, third, pltpu.roll(pltpu.roll(third, 4, 0), 64, 1))
    out_ref[...] = jnp.where(lane < 64, two + pltpu.roll(two, 64, 1) + third, 0.0)


PLACE = {1: 0, 0: 1, 2: 2}


def weights_kernel(x_ref, out_ref, flat_ref, tall_ref):
    flat_ref[...] = jnp.zeros_like(flat_ref)
    row, lane = iota((SLICE, LANES), 0), iota((SLICE, LANES), 1)
    for r in range(ROW_DEVS):
        at = r * KERNEL_ROWS
        block, off = at // LANES, at % LANES
        slot = x_ref[r].astype(F32)
        low = jnp.concatenate([slot[SLICE:], jnp.zeros((8, LANES), F32)], axis=0)
        rest = jnp.where(row < 20, low, pltpu.roll(pltpu.roll(low, 20, 0), 64, 1))
        rest = jnp.where(lane < TAIL, rest, 0.0)
        wide = jnp.concatenate([slot[:SLICE], rest, jnp.zeros((SLICE, LANES), F32)], axis=1)
        if off:
            wide = pltpu.roll(wide, off, 1)
        spot = slice(block * LANES, (block + 3) * LANES)
        flat_ref[:, spot] = flat_ref[:, spot] + wide
    tall_ref[...] = jnp.zeros_like(tall_ref)
    for a in range(3):
        for b in range(3):
            tap = 3 * a + b
            top = a * LANES + PLACE[b] * SLICE
            tall_ref[top : top + SLICE, :] = flat_ref[:, tap * CHANS : (tap + 1) * CHANS]
    out_ref[...] = tall_ref[...].astype(BF16)


def spot(place_ref, q):
    return lax.rem(lax.rem(q, 2) + place_ref[1], 2) * HALF + q // 2


def silu(v):
    half = 0.5 * v
    return half + half * jnp.tanh(half)


def across(full):
    rows = full.shape[0]
    at = lax.rem(iota((rows, LANES), 0), WIDTH)
    left = pltpu.roll(pltpu.roll(full, 1, 0), LANES - SLICE, 1)
    right = pltpu.roll(pltpu.roll(full, rows - 1, 0), LANES - 2 * SLICE, 1)
    total = full + jnp.where(at == 0, 0.0, left) + jnp.where(at == WIDTH - 1, 0.0, right)
    return jnp.where(iota((rows, LANES), 1) < SLICE, total, 0.0)


def packed(value):
    n = value.shape[0] // 3
    out = value[:n]
    for t in (1, 2):
        out = out + pltpu.roll(value[n * t : n * (t + 1)], SLICE * t, 1)
    return out


STEPS = (0, 1, 3, 2)


def beside(place_ref, j):
    dx = lax.rem(j // 2 + 4 - place_ref[2], 4)
    dz = lax.rem(j % 2 + place_ref[3], 2)
    return 2 * jnp.where(dx == 2, 3, jnp.where(dx == 3, 2, dx)) + dz


def merge_kernel(place_ref, x_ref, edge_ref, out_ref):
    for j in range(HALF):
        at = beside(place_ref, j)
        parts = [x_ref[j], edge_ref[at, 0], edge_ref[at, 1]]
        out_ref[j] = jnp.concatenate([v.astype(F32) for v in parts], axis=0).astype(BF16)


def conv_kernel(place_ref, anc_ref, scale_ref, shift_ref, w_ref, *refs):
    totals, own_ref, far_ref, (out_ref, done_ref, other_ref, sem) = refs[:2], *refs[2:4], refs[4:]
    copy = pltpu.make_async_copy(far_ref, other_ref, sem)
    copy.start()
    slabs = (own_ref, other_ref)
    mean, inverse = mean_and_inverse(jnp.concatenate([ref[...] for ref in totals], axis=0))
    gain = inverse * (1.0 + scale_ref[...])
    bias = shift_ref[...] - mean * gain
    row, col = iota((LANES, CHANS), 0), iota((LANES, CHANS), 1)
    chosen = ((col == row + place_ref[0] * SLICE) & (row < SLICE)).astype(F32).astype(BF16)
    weights = w_ref[...]
    top, bottom = place_ref[4] == 0, place_ref[4] == ROW_DEVS - 1
    each = 2
    for step in range(PARTICLES // each):
        if step * each == HALF:
            copy.wait()
        active, raw = [], []
        for n in range(step * each, (step + 1) * each):
            x = slabs[n // HALF][n % HALF]
            raw.append(x[:TOKENS])
            active.append(silu(x.astype(F32) * gain[n : n + 1] + bias[n : n + 1]).astype(BF16))
        active = jnp.concatenate(active, axis=0)
        raw = jnp.concatenate(raw, axis=0)
        taps = lax.dot_general(active, weights, NT, preferred_element_type=F32)
        field = lax.dot_general(raw, chosen, NT, preferred_element_type=F32)
        for k in range(each):
            here = taps[k * ALL : (k + 1) * ALL]
            t0, t1, t2 = (here[:, a * LANES : (a + 1) * LANES] for a in range(3))
            above = jnp.where(top, 0.0, t0[TOKENS : TOKENS + WIDTH])
            below = jnp.where(bottom, 0.0, t2[TOKENS + WIDTH :])
            full = field[k * TOKENS : (k + 1) * TOKENS] + t1[:TOKENS]
            full = full + jnp.concatenate([above, t0[:LAST]], axis=0)
            full = full + jnp.concatenate([t2[WIDTH:TOKENS], below], axis=0)
            done_ref[step * each + k] = packed(across(full)).astype(BF16)
    for p in range(PARTICLES):
        out_ref[p] = done_ref[spot(place_ref, anc_ref[p])]


def gather_kernel(x_ref, resid_ref, out_ref, wide_ref):
    lane = iota((32, LANES), 1)
    for t in range(3):
        blocks = [jnp.zeros((32, LANES), F32) for _ in range(CHANS // LANES)]
        for p in range(PARTICLES):
            block, off = (p * SLICE) // LANES, (p * SLICE) % LANES
            turn = (off - t * SLICE) % LANES
            piece = x_ref[p].astype(F32)
            if turn:
                piece = pltpu.roll(piece, turn, 1)
            end = off + SLICE
            blocks[block] = jnp.where((lane >= off) & (lane < end), piece, blocks[block])
            if end > LANES:
                blocks[block + 1] = jnp.where(lane < end - LANES, piece, blocks[block + 1])
        for n, value in enumerate(blocks):
            wide_ref[32 * t : 32 * (t + 1), n * LANES : (n + 1) * LANES] = value
    wide = wide_ref[...]
    resid_ref[...] = wide.astype(BF16)
    out_ref[...] = jnp.broadcast_to(group_rows([wide])[None, :1], out_ref.shape)


def project_kernel(totals_ref, resid_ref, w_ref, out_ref, both_ref):
    totals = jnp.broadcast_to(jnp.sum(totals_ref[...], axis=0), (8, LANES))
    mean, inverse = mean_and_inverse(totals)
    normed = ((resid_ref[...].astype(F32) - mean[:1]) * inverse[:1]).astype(BF16)
    both_ref[...] = jnp.dot(normed, w_ref[...], preferred_element_type=F32)
    low = iota((TOKENS, LANES), 1) < 64
    low_s = iota((16, LANES), 1) < 64
    for pair in range(HEADS // 2):
        q, k, v = (
            both_ref[:, n * CHANS + pair * LANES : n * CHANS + (pair + 1) * LANES] for n in range(3)
        )
        q_turn, k_turn, v_turn = (pltpu.roll(x, 64, 1) for x in (q, k, v))
        mixed = (jnp.where(low, k, v_turn), jnp.where(low, k_turn, v))
        lows, highs = (q, q_turn), (q_turn, q)
        for side in range(2):
            keys_values = mixed[side].astype(BF16)
            for b in range(QUERY_BLOCKS):
                slot = (2 * pair + side) * QUERY_BLOCKS + b
                at = 32 * b
                two = jnp.where(low_s, lows[side][at : at + 16], highs[side][at + 16 : at + 32])
                out_ref[slot, :TOKENS] = keys_values
                out_ref[slot, TOKENS:] = two.astype(BF16)
    for slot in range(HEADS * QUERY_BLOCKS, ROW_DEVS):
        out_ref[slot] = jnp.zeros((SLOT, LANES), BF16)


def attend_kernel(x_ref, out_ref, keys_ref, ones_ref, query_ref):
    low = iota((TOKENS, LANES), 1) < 64
    for r in range(ROW_DEVS):
        block = x_ref[r, :TOKENS]
        keys_ref[r * TOKENS : (r + 1) * TOKENS] = block
        ones_ref[r * TOKENS : (r + 1) * TOKENS] = jnp.where(low, jnp.ones_like(block), block)
        query_ref[r * 16 : (r + 1) * 16] = x_ref[r, TOKENS:].astype(F32)
    size, chunk = 512, 1024
    low_q = iota((size, LANES), 1) < 64
    factor = 0.125 * 1.4426950408889634
    done = []
    for side in range(2):
        here = query_ref[...]
        turned = here if side == 0 else pltpu.roll(here, 64, 1)
        query = jnp.where(low_q, turned, 0.0).astype(BF16)
        top = result = None
        for c in range(0, ROW_DEVS * TOKENS, chunk):
            span = slice(c, c + chunk)
            scores = lax.dot_general(query, keys_ref[span], NT, preferred_element_type=F32)
            higher = jnp.max(scores, axis=1, keepdims=True)
            if c:
                higher = jnp.maximum(higher, top)
            weights = jnp.exp2((scores - higher) * factor).astype(BF16)
            new = jnp.dot(weights, ones_ref[span], preferred_element_type=F32)
            result = result * jnp.exp2((top - higher) * factor) + new if c else new
            top = higher
        done.append((result, pltpu.roll(result, 64, 1)))
    (first, first_turned), (second, second_turned) = done
    both = jnp.where(low_q, first_turned / first, second / second_turned).astype(BF16)
    for r in range(ROW_DEVS):
        out_ref[r] = both[r * 16 : (r + 1) * 16]


def output_kernel(x_ref, resid_ref, w_ref, out_ref, wide_ref):
    low = iota((16, LANES), 1) < 64
    for pair in range(HEADS // 2):
        for b in range(QUERY_BLOCKS):
            first = x_ref[2 * pair * QUERY_BLOCKS + b].astype(F32)
            second = x_ref[(2 * pair + 1) * QUERY_BLOCKS + b].astype(F32)
            cols = slice(pair * LANES, (pair + 1) * LANES)
            at = 32 * b
            wide_ref[at : at + 16, cols] = jnp.where(low, first, pltpu.roll(second, 64, 1))
            wide_ref[at + 16 : at + 32, cols] = jnp.where(low, pltpu.roll(first, 64, 1), second)
    mixed = wide_ref[...].astype(BF16)
    product = jnp.dot(mixed, w_ref[...], preferred_element_type=F32)
    out_ref[...] = (resid_ref[...].astype(F32) + product).astype(BF16)


def exchange(values, axes):
    return lax.all_to_all(values, axes, split_axis=0, concat_axis=0, tiled=True)


def per_device(latent, ada_scale, ada_shift, conv_weight, qkv_weight, out_weight, ancestors):
    slab = latent.reshape(TOKENS, CHANS)
    particle = lax.axis_index(PART).astype(jnp.int32)
    place = jnp.stack(
        [particle] + [lax.axis_index(a).astype(jnp.int32) for a in ("core", "x", "z_lo", ROWS)]
    )

    swap = [(0, 1), (1, 0)]
    row = shaped(WIDTH, CHANS)
    copies, first, last = call(
        spread_kernel, [shaped(HALF, TOKENS, CHANS), row, row], [VMEM], 10**5, 10**6
    )(slab)
    here = exchange(copies, CHIPS)
    above = lax.ppermute(last, ROWS, [(i, i + 1) for i in range(ROW_DEVS - 1)])
    below = lax.ppermute(first, ROWS, [(i + 1, i) for i in range(ROW_DEVS - 1)])
    mine = jnp.stack([above, below])
    opposite = lax.ppermute(mine, "z_lo", swap)

    columns = call(pick_kernel, shaped(72, LANES, dtype=F32), [SMEM, VMEM], 10**7, 10**6, vmem=8)(
        place, conv_weight
    )
    picked = call(slots_kernel, shaped(ROW_DEVS, 72, LANES), [VMEM, VMEM, ANY], 10**7, 10**6)(
        here, columns, opposite
    )
    pair = call(join_kernel, shaped(2, 2, WIDTH, CHANS), [VMEM, VMEM, ANY], 10**5, 10**6)(
        mine, opposite, picked
    )
    turns = [[((i + d) % 4, i) for i in range(4)] for d in STEPS[1:]]
    edges = jnp.concatenate([pair] + [lax.ppermute(pair, "x", turn) for turn in turns])
    merged = call(merge_kernel, shaped(HALF, ALL, CHANS), [SMEM, VMEM, VMEM], 10**6, 10**6)(
        place, here, edges
    )
    slabs = [merged, lax.ppermute(merged, "core", swap)]
    picked = exchange(picked, ROWS)
    totals = call(total_kernel, shaped(HALF, LANES, dtype=F32), [VMEM], 10**5, 10**5)(picked)
    totals = [totals, lax.ppermute(totals, "core", swap)]
    weights = call(
        weights_kernel,
        shaped(3 * LANES, CHANS),
        [VMEM],
        3 * 10**10,
        10**6,
        scratch=(
            pltpu.VMEM((SLICE, 9 * CHANS + 2 * LANES), F32),
            pltpu.VMEM((3 * LANES, CHANS), F32),
        ),
    )(picked)
    pieces = call(
        conv_kernel,
        shaped(PARTICLES, 32, LANES),
        [SMEM, SMEM] + [VMEM] * 6 + [ANY],
        2 * 10**9,
        4 * 10**6,
        vmem=20,
        scratch=(
            pltpu.VMEM((PARTICLES, 32, LANES), BF16),
            pltpu.VMEM((HALF, ALL, CHANS), BF16),
            pltpu.SemaphoreType.DMA,
        ),
    )(place, ancestors, ada_scale[None], ada_shift[None], weights, *totals, *slabs)
    pieces = exchange(pieces, PART)

    resid, sums = call(
        gather_kernel,
        [shaped(TOKENS, CHANS), shaped(ROW_DEVS, 1, LANES, dtype=F32)],
        [VMEM],
        10**6,
        10**6,
        scratch=(pltpu.VMEM((TOKENS, CHANS), F32),),
    )(pieces)
    sums = exchange(sums, ROWS)
    slots = call(
        project_kernel,
        shaped(ROW_DEVS, SLOT, LANES),
        [VMEM] * 3,
        3 * 10**8,
        4 * 10**6,
        scratch=(pltpu.VMEM((TOKENS, 3 * CHANS), F32),),
    )(sums, resid, qkv_weight)
    slots = exchange(slots, ROWS)
    rows = ROW_DEVS * TOKENS
    mixed = call(
        attend_kernel,
        shaped(ROW_DEVS, 16, LANES),
        [VMEM],
        2 * 10**9,
        2 * 10**6,
        vmem=32,
        scratch=(
            pltpu.VMEM((rows, LANES), BF16),
            pltpu.VMEM((rows, LANES), BF16),
            pltpu.VMEM((ROW_DEVS * 16, LANES), F32),
        ),
    )(slots)
    mixed = exchange(mixed, ROWS)
    block = call(
        output_kernel,
        shaped(TOKENS, CHANS),
        [VMEM] * 3,
        10**8,
        10**6,
        scratch=(pltpu.VMEM((TOKENS, CHANS), F32),),
    )(mixed, resid, out_weight)
    return block.reshape(1, ROWS_HERE, WIDTH, CHANS)


def solution(mesh):
    split = Mesh(mesh.devices.reshape(4, 2, 2, 4, 8), PART + ROWS)
    placed = (P(PART, ROWS, None, None), P(), P(), P(ROWS, None), P(), P(), P())
    return jax.shard_map(
        per_device,
        mesh=split,
        in_specs=placed,
        out_specs=P(PART, ROWS, None, None),
        check_vma=False,
    )
```

```python
import jax
import jax.numpy as jnp
from jax import lax
from jax.experimental import pallas as pl
from jax.experimental.pallas import tpu as pltpu
from jax.sharding import Mesh
from jax.sharding import PartitionSpec as P

HEADS = 10
GROUPS = 32
CHANS = 640
WIDTH = 24
ROWS_HERE = 4
TOKENS = ROWS_HERE * WIDTH
LAST = TOKENS - WIDTH
ALL = TOKENS + 2 * WIDTH
PARTICLES = 16
HALF = PARTICLES // 2
ROW_DEVS = 32
PER_GROUP = CHANS // GROUPS
SLICE = CHANS // PARTICLES
COUNT = ROWS_HERE * ROW_DEVS * WIDTH * PER_GROUP
LANES = 128
KERNEL_ROWS = 9 * CHANS // ROW_DEVS
TAIL = KERNEL_ROWS - LANES
QUERY_BLOCKS = 3
SLOT = TOKENS + 16

PART = ("x", "z_lo", "core")
CHIPS = ("x", "z_lo")
ROWS = ("z_hi", "y")

NT = (((1,), (1,)), ((), ()))
F32 = jnp.float32
BF16 = jnp.bfloat16
SMEM = pl.BlockSpec(memory_space=pltpu.SMEM)
VMEM = pl.BlockSpec(memory_space=pltpu.VMEM)
ANY = pl.BlockSpec(memory_space=pl.ANY)


def call(kernel, out_shape, in_specs, flops, size, vmem=16, scratch=()):
    out_specs = jax.tree.map(lambda _: VMEM, out_shape)
    return pl.pallas_call(
        kernel,
        out_shape=out_shape,
        in_specs=in_specs,
        out_specs=out_specs,
        scratch_shapes=list(scratch),
        compiler_params=pltpu.CompilerParams(vmem_limit_bytes=vmem * 1024 * 1024),
        cost_estimate=pl.CostEstimate(flops=flops, bytes_accessed=size, transcendentals=0),
    )


def shaped(*shape, dtype=BF16):
    return jax.ShapeDtypeStruct(shape, dtype)


def iota(shape, dim):
    return lax.broadcasted_iota(jnp.int32, shape, dim)


def exact_dot(a, b):
    return jnp.dot(a, b, precision=lax.Precision.HIGHEST, preferred_element_type=F32)


def group_rows(values):
    fill = [jnp.zeros((1, CHANS), F32)] * (8 - len(values))
    sums = jnp.concatenate([jnp.sum(v, axis=0, keepdims=True) for v in values] + fill, axis=0)
    squares = [jnp.sum(v * v, axis=0, keepdims=True) for v in values] + fill
    squares = jnp.concatenate(squares, axis=0)
    chan, lane = iota((CHANS, LANES), 0), iota((CHANS, LANES), 1)
    first = ((chan >= lane * PER_GROUP) & (chan < (lane + 1) * PER_GROUP)).astype(F32)
    other = lane - GROUPS
    second = ((chan >= other * PER_GROUP) & (chan < (other + 1) * PER_GROUP)).astype(F32)
    return exact_dot(sums, first) + exact_dot(squares, second)


def mean_and_inverse(totals):
    lane, chan = iota((LANES, CHANS), 0), iota((LANES, CHANS), 1)
    first = ((chan >= lane * PER_GROUP) & (chan < (lane + 1) * PER_GROUP)).astype(F32)
    other = lane - GROUPS
    second = ((chan >= other * PER_GROUP) & (chan < (other + 1) * PER_GROUP)).astype(F32)
    mean = exact_dot(totals, first) * (1.0 / COUNT)
    square = exact_dot(totals, second) * (1.0 / COUNT)
    return mean, lax.rsqrt(square - mean * mean + 1e-05)


def thirds(value):
    parts = []
    for _ in range(3):
        top = value.astype(BF16).astype(F32)
        parts.append(top)
        value = value - top
    return parts


def spread_kernel(x_ref, out_ref, first_ref, last_ref):
    out_ref[...] = jnp.broadcast_to(x_ref[...][None], out_ref.shape)
    wide = x_ref[...].astype(F32)
    first_ref[...] = wide[:WIDTH].astype(BF16)
    last_ref[...] = wide[LAST:].astype(BF16)


def join_kernel(mine_ref, opposite_ref, _, out_ref):
    out_ref[0] = mine_ref[...]
    out_ref[1] = opposite_ref[...]


def pick_kernel(place_ref, w_ref, out_ref):
    row, col = iota((48, CHANS), 0), iota((48, CHANS), 1)
    chosen = ((col == row + place_ref[0] * SLICE) & (row < SLICE)).astype(F32).astype(BF16)
    picked = lax.dot_general(chosen, w_ref[...], NT, preferred_element_type=F32)
    rest = jnp.concatenate([picked[:, LANES:], jnp.zeros((48, LANES - TAIL), F32)], axis=1)
    turned = pltpu.roll(pltpu.roll(rest, 48 - 20, 0), 64, 1)
    row, lane = iota((32, LANES), 0), iota((32, LANES), 1)
    low = jnp.where(lane < 64, rest[:32], turned[:32])
    out_ref[:SLICE] = picked[:SLICE, :LANES]
    out_ref[SLICE:] = jnp.where(row < 20, low, 0.0)


def slots_kernel(x_ref, part_ref, _, out_ref):
    values = [x_ref[j].astype(F32) for j in range(HALF)]
    first, second, third = thirds(group_rows(values))
    row, lane = iota((8, LANES), 0), iota((8, LANES), 1)
    third = jnp.where(lane < 64, third, pltpu.roll(pltpu.roll(third, 4, 0), 64, 1))
    third = jnp.where(row < 4, third, 0.0)
    rest = jnp.zeros((24, LANES), F32)
    sums = pltpu.roll(jnp.concatenate([first + pltpu.roll(second, 64, 1), rest], axis=0), 20, 0)
    sums = sums + pltpu.roll(jnp.concatenate([third, rest], axis=0), 28, 0)
    slot = jnp.concatenate([part_ref[:SLICE], part_ref[SLICE:] + sums], axis=0).astype(BF16)
    out_ref[...] = jnp.broadcast_to(slot[None], out_ref.shape)


def total_kernel(x_ref, out_ref):
    total = jnp.zeros((32, LANES), F32)
    for r in range(ROW_DEVS):
        total = total + x_ref[r].astype(F32)[SLICE:]
    two, third = pltpu.roll(total, 12, 0)[:8], pltpu.roll(total, 4, 0)[:8]
    row, lane = iota((8, LANES), 0), iota((8, LANES), 1)
    third = jnp.where(row < 4, third, pltpu.roll(pltpu.roll(third, 4, 0), 64, 1))
    out_ref[...] = jnp.where(lane < 64, two + pltpu.roll(two, 64, 1) + third, 0.0)


PLACE = {1: 0, 0: 1, 2: 2}


def weights_kernel(x_ref, out_ref, flat_ref, tall_ref):
    flat_ref[...] = jnp.zeros_like(flat_ref)
    row, lane = iota((SLICE, LANES), 0), iota((SLICE, LANES), 1)
    for r in range(ROW_DEVS):
        at = r * KERNEL_ROWS
        block, off = at // LANES, at % LANES
        slot = x_ref[r].astype(F32)
        low = jnp.concatenate([slot[SLICE:], jnp.zeros((8, LANES), F32)], axis=0)
        rest = jnp.where(row < 20, low, pltpu.roll(pltpu.roll(low, 20, 0), 64, 1))
        rest = jnp.where(lane < TAIL, rest, 0.0)
        wide = jnp.concatenate([slot[:SLICE], rest, jnp.zeros((SLICE, LANES), F32)], axis=1)
        if off:
            wide = pltpu.roll(wide, off, 1)
        spot = slice(block * LANES, (block + 3) * LANES)
        flat_ref[:, spot] = flat_ref[:, spot] + wide
    tall_ref[...] = jnp.zeros_like(tall_ref)
    for a in range(3):
        for b in range(3):
            tap = 3 * a + b
            top = a * LANES + PLACE[b] * SLICE
            tall_ref[top : top + SLICE, :] = flat_ref[:, tap * CHANS : (tap + 1) * CHANS]
    out_ref[...] = tall_ref[...].astype(BF16)


def spot(place_ref, q):
    return lax.rem(lax.rem(q, 2) + place_ref[1], 2) * HALF + q // 2


def silu(v):
    half = 0.5 * v
    return half + half * jnp.tanh(half)


def across(full):
    rows = full.shape[0]
    at = lax.rem(iota((rows, LANES), 0), WIDTH)
    left = pltpu.roll(pltpu.roll(full, 1, 0), LANES - SLICE, 1)
    right = pltpu.roll(pltpu.roll(full, rows - 1, 0), LANES - 2 * SLICE, 1)
    total = full + jnp.where(at == 0, 0.0, left) + jnp.where(at == WIDTH - 1, 0.0, right)
    return jnp.where(iota((rows, LANES), 1) < SLICE, total, 0.0)


def packed(value):
    n = value.shape[0] // 3
    out = value[:n]
    for t in (1, 2):
        out = out + pltpu.roll(value[n * t : n * (t + 1)], SLICE * t, 1)
    return out


STEPS = (0, 1, 3, 2)


def beside(place_ref, j):
    dx = lax.rem(j // 2 + 4 - place_ref[2], 4)
    dz = lax.rem(j % 2 + place_ref[3], 2)
    return 2 * jnp.where(dx == 2, 3, jnp.where(dx == 3, 2, dx)) + dz


def merge_kernel(place_ref, x_ref, edge_ref, out_ref):
    for j in range(HALF):
        at = beside(place_ref, j)
        parts = [x_ref[j], edge_ref[at, 0], edge_ref[at, 1]]
        out_ref[j] = jnp.concatenate([v.astype(F32) for v in parts], axis=0).astype(BF16)


def conv_kernel(place_ref, anc_ref, scale_ref, shift_ref, w_ref, *refs):
    totals, slabs, (out_ref, done_ref) = refs[:2], refs[2:4], refs[4:]
    mean, inverse = mean_and_inverse(jnp.concatenate([ref[...] for ref in totals], axis=0))
    gain = inverse * (1.0 + scale_ref[...])
    bias = shift_ref[...] - mean * gain
    row, col = iota((LANES, CHANS), 0), iota((LANES, CHANS), 1)
    chosen = ((col == row + place_ref[0] * SLICE) & (row < SLICE)).astype(F32).astype(BF16)
    weights = w_ref[...]
    top, bottom = place_ref[4] == 0, place_ref[4] == ROW_DEVS - 1
    each = 2
    for step in range(PARTICLES // each):
        active, raw = [], []
        for n in range(step * each, (step + 1) * each):
            x = slabs[n // HALF][n % HALF]
            raw.append(x[:TOKENS])
            active.append(silu(x.astype(F32) * gain[n : n + 1] + bias[n : n + 1]).astype(BF16))
        active = jnp.concatenate(active, axis=0)
        raw = jnp.concatenate(raw, axis=0)
        taps = lax.dot_general(active, weights, NT, preferred_element_type=F32)
        field = lax.dot_general(raw, chosen, NT, preferred_element_type=F32)
        for k in range(each):
            here = taps[k * ALL : (k + 1) * ALL]
            t0, t1, t2 = (here[:, a * LANES : (a + 1) * LANES] for a in range(3))
            above = jnp.where(top, 0.0, t0[TOKENS : TOKENS + WIDTH])
            below = jnp.where(bottom, 0.0, t2[TOKENS + WIDTH :])
            full = field[k * TOKENS : (k + 1) * TOKENS] + t1[:TOKENS]
            full = full + jnp.concatenate([above, t0[:LAST]], axis=0)
            full = full + jnp.concatenate([t2[WIDTH:TOKENS], below], axis=0)
            done_ref[step * each + k] = packed(across(full)).astype(BF16)
    for p in range(PARTICLES):
        out_ref[p] = done_ref[spot(place_ref, anc_ref[p])]


def gather_kernel(x_ref, resid_ref, out_ref, wide_ref):
    lane = iota((32, LANES), 1)
    for t in range(3):
        blocks = [jnp.zeros((32, LANES), F32) for _ in range(CHANS // LANES)]
        for p in range(PARTICLES):
            block, off = (p * SLICE) // LANES, (p * SLICE) % LANES
            turn = (off - t * SLICE) % LANES
            piece = x_ref[p].astype(F32)
            if turn:
                piece = pltpu.roll(piece, turn, 1)
            end = off + SLICE
            blocks[block] = jnp.where((lane >= off) & (lane < end), piece, blocks[block])
            if end > LANES:
                blocks[block + 1] = jnp.where(lane < end - LANES, piece, blocks[block + 1])
        for n, value in enumerate(blocks):
            wide_ref[32 * t : 32 * (t + 1), n * LANES : (n + 1) * LANES] = value
    wide = wide_ref[...]
    resid_ref[...] = wide.astype(BF16)
    out_ref[...] = jnp.broadcast_to(group_rows([wide])[None, :1], out_ref.shape)


def project_kernel(totals_ref, resid_ref, w_ref, out_ref, both_ref):
    totals = jnp.broadcast_to(jnp.sum(totals_ref[...], axis=0), (8, LANES))
    mean, inverse = mean_and_inverse(totals)
    normed = ((resid_ref[...].astype(F32) - mean[:1]) * inverse[:1]).astype(BF16)
    both_ref[...] = jnp.dot(normed, w_ref[...], preferred_element_type=F32)
    low = iota((TOKENS, LANES), 1) < 64
    low_s = iota((16, LANES), 1) < 64
    for pair in range(HEADS // 2):
        q, k, v = (
            both_ref[:, n * CHANS + pair * LANES : n * CHANS + (pair + 1) * LANES] for n in range(3)
        )
        q_turn, k_turn, v_turn = (pltpu.roll(x, 64, 1) for x in (q, k, v))
        mixed = (jnp.where(low, k, v_turn), jnp.where(low, k_turn, v))
        lows, highs = (q, q_turn), (q_turn, q)
        for side in range(2):
            keys_values = mixed[side].astype(BF16)
            for b in range(QUERY_BLOCKS):
                slot = (2 * pair + side) * QUERY_BLOCKS + b
                at = 32 * b
                two = jnp.where(low_s, lows[side][at : at + 16], highs[side][at + 16 : at + 32])
                out_ref[slot, :TOKENS] = keys_values
                out_ref[slot, TOKENS:] = two.astype(BF16)
    for slot in range(HEADS * QUERY_BLOCKS, ROW_DEVS):
        out_ref[slot] = jnp.zeros((SLOT, LANES), BF16)


def attend_kernel(x_ref, out_ref, keys_ref, ones_ref, query_ref):
    low = iota((TOKENS, LANES), 1) < 64
    for r in range(ROW_DEVS):
        block = x_ref[r, :TOKENS]
        keys_ref[r * TOKENS : (r + 1) * TOKENS] = block
        ones_ref[r * TOKENS : (r + 1) * TOKENS] = jnp.where(low, jnp.ones_like(block), block)
        query_ref[r * 16 : (r + 1) * 16] = x_ref[r, TOKENS:].astype(F32)
    size, chunk = 512, 1024
    low_q = iota((size, LANES), 1) < 64
    factor = 0.125 * 1.4426950408889634
    done = []
    for side in range(2):
        here = query_ref[...]
        turned = here if side == 0 else pltpu.roll(here, 64, 1)
        query = jnp.where(low_q, turned, 0.0).astype(BF16)
        top = result = None
        for c in range(0, ROW_DEVS * TOKENS, chunk):
            span = slice(c, c + chunk)
            scores = lax.dot_general(query, keys_ref[span], NT, preferred_element_type=F32)
            higher = jnp.max(scores, axis=1, keepdims=True)
            if c:
                higher = jnp.maximum(higher, top)
            weights = jnp.exp2((scores - higher) * factor).astype(BF16)
            new = jnp.dot(weights, ones_ref[span], preferred_element_type=F32)
            result = result * jnp.exp2((top - higher) * factor) + new if c else new
            top = higher
        done.append((result, pltpu.roll(result, 64, 1)))
    (first, first_turned), (second, second_turned) = done
    both = jnp.where(low_q, first_turned / first, second / second_turned).astype(BF16)
    for r in range(ROW_DEVS):
        out_ref[r] = both[r * 16 : (r + 1) * 16]


def output_kernel(x_ref, resid_ref, w_ref, out_ref, wide_ref):
    low = iota((16, LANES), 1) < 64
    for pair in range(HEADS // 2):
        for b in range(QUERY_BLOCKS):
            first = x_ref[2 * pair * QUERY_BLOCKS + b].astype(F32)
            second = x_ref[(2 * pair + 1) * QUERY_BLOCKS + b].astype(F32)
            cols = slice(pair * LANES, (pair + 1) * LANES)
            at = 32 * b
            wide_ref[at : at + 16, cols] = jnp.where(low, first, pltpu.roll(second, 64, 1))
            wide_ref[at + 16 : at + 32, cols] = jnp.where(low, pltpu.roll(first, 64, 1), second)
    mixed = wide_ref[...].astype(BF16)
    product = jnp.dot(mixed, w_ref[...], preferred_element_type=F32)
    out_ref[...] = (resid_ref[...].astype(F32) + product).astype(BF16)


def exchange(values, axes):
    return lax.all_to_all(values, axes, split_axis=0, concat_axis=0, tiled=True)


def per_device(latent, ada_scale, ada_shift, conv_weight, qkv_weight, out_weight, ancestors):
    slab = latent.reshape(TOKENS, CHANS)
    particle = lax.axis_index(PART).astype(jnp.int32)
    place = jnp.stack(
        [particle] + [lax.axis_index(a).astype(jnp.int32) for a in ("core", "x", "z_lo", ROWS)]
    )

    swap = [(0, 1), (1, 0)]
    row = shaped(WIDTH, CHANS)
    copies, first, last = call(
        spread_kernel, [shaped(HALF, TOKENS, CHANS), row, row], [VMEM], 10**5, 10**6
    )(slab)
    here = exchange(copies, CHIPS)
    above = lax.ppermute(last, ROWS, [(i, i + 1) for i in range(ROW_DEVS - 1)])
    below = lax.ppermute(first, ROWS, [(i + 1, i) for i in range(ROW_DEVS - 1)])
    mine = jnp.stack([above, below])
    opposite = lax.ppermute(mine, "z_lo", swap)

    columns = call(pick_kernel, shaped(72, LANES, dtype=F32), [SMEM, VMEM], 10**7, 10**6, vmem=8)(
        place, conv_weight
    )
    picked = call(slots_kernel, shaped(ROW_DEVS, 72, LANES), [VMEM, VMEM, ANY], 10**7, 10**6)(
        here, columns, opposite
    )
    pair = call(join_kernel, shaped(2, 2, WIDTH, CHANS), [VMEM, VMEM, ANY], 10**5, 10**6)(
        mine, opposite, picked
    )
    turns = [[((i + d) % 4, i) for i in range(4)] for d in STEPS[1:]]
    edges = jnp.concatenate([pair] + [lax.ppermute(pair, "x", turn) for turn in turns])
    merged = call(merge_kernel, shaped(HALF, ALL, CHANS), [SMEM, VMEM, VMEM], 10**6, 10**6)(
        place, here, edges
    )
    slabs = [merged, lax.ppermute(merged, "core", swap)]
    picked = exchange(picked, ROWS)
    totals = call(total_kernel, shaped(HALF, LANES, dtype=F32), [VMEM], 10**5, 10**5)(picked)
    totals = [totals, lax.ppermute(totals, "core", swap)]
    weights = call(
        weights_kernel,
        shaped(3 * LANES, CHANS),
        [VMEM],
        3 * 10**10,
        10**6,
        scratch=(
            pltpu.VMEM((SLICE, 9 * CHANS + 2 * LANES), F32),
            pltpu.VMEM((3 * LANES, CHANS), F32),
        ),
    )(picked)
    pieces = call(
        conv_kernel,
        shaped(PARTICLES, 32, LANES),
        [SMEM, SMEM] + [VMEM] * 7,
        2 * 10**9,
        4 * 10**6,
        vmem=20,
        scratch=(pltpu.VMEM((PARTICLES, 32, LANES), BF16),),
    )(place, ancestors, ada_scale[None], ada_shift[None], weights, *totals, *slabs)
    pieces = exchange(pieces, PART)

    resid, sums = call(
        gather_kernel,
        [shaped(TOKENS, CHANS), shaped(ROW_DEVS, 1, LANES, dtype=F32)],
        [VMEM],
        10**6,
        10**6,
        scratch=(pltpu.VMEM((TOKENS, CHANS), F32),),
    )(pieces)
    sums = exchange(sums, ROWS)
    slots = call(
        project_kernel,
        shaped(ROW_DEVS, SLOT, LANES),
        [VMEM] * 3,
        3 * 10**8,
        4 * 10**6,
        scratch=(pltpu.VMEM((TOKENS, 3 * CHANS), F32),),
    )(sums, resid, qkv_weight)
    slots = exchange(slots, ROWS)
    rows = ROW_DEVS * TOKENS
    mixed = call(
        attend_kernel,
        shaped(ROW_DEVS, 16, LANES),
        [VMEM],
        2 * 10**9,
        2 * 10**6,
        vmem=32,
        scratch=(
            pltpu.VMEM((rows, LANES), BF16),
            pltpu.VMEM((rows, LANES), BF16),
            pltpu.VMEM((ROW_DEVS * 16, LANES), F32),
        ),
    )(slots)
    mixed = exchange(mixed, ROWS)
    block = call(
        output_kernel,
        shaped(TOKENS, CHANS),
        [VMEM] * 3,
        10**8,
        10**6,
        scratch=(pltpu.VMEM((TOKENS, CHANS), F32),),
    )(mixed, resid, out_weight)
    return block.reshape(1, ROWS_HERE, WIDTH, CHANS)


def solution(mesh):
    split = Mesh(mesh.devices.reshape(4, 2, 2, 4, 8), PART + ROWS)
    placed = (P(PART, ROWS, None, None), P(), P(), P(ROWS, None), P(), P(), P())
    return jax.shard_map(
        per_device,
        mesh=split,
        in_specs=placed,
        out_specs=P(PART, ROWS, None, None),
        check_vma=False,
    )
```
